512 devices in a mesh: gx: 8 (over z), gy: 8 (over y), gz: 8 (over x, core).
Axes of the slice: x: 4, y: 8, z: 8, core: 2. Of those that a mesh axis runs over, the one named last changes fastest.
Arguments:
- hidden_panel: float32 [32, 4194304], P(None, ('gx', 'gy', 'gz')), may hold values from -6 to 6
- sign_bits: int32 [4194304], P(('gx', 'gy', 'gz')), may hold values 0 or 1
- pick_rows: int32 [32768], P(('gx', 'gy', 'gz')), may hold values from 0 to 8191
- pick_owner: int32 [32768], P(('gx', 'gy', 'gz')), may hold values from -1 to 16383, as said below
Outputs:
- sketch: float32 [32, 16384], P(None, ('gx', 'gy', 'gz'))
The draws below stay inside these ranges and needn't reach their ends.
Inputs may be any that keep to these rules, and one draw needn't show every extreme that they name: `pick_owner`: each sketch row 0 to 16383 stands in exactly one slot and every other slot holds -1. On each device the slots that are not -1 come first. On some device all 64 slots are filled and on some device none is.
All inputs are finite; a program needn't handle non-finite values. No bound on the sum of `sign_bits` on one device may be relied on, other than what follows from the above.
Results may differ from the reference program's by a relative error of at most 0.000086.
Values sent between devices are 32-bit elements; how exact they have to be, the bound alone decides.
No kernel may reach another device: no remote copies, remote signals or barrier semaphores. Data moves between devices by JAX's collectives and lax.ppermute only.
A program may use at most 128 MiB of HBM per device.

```python
import math
import jax
import jax.numpy as jnp
from jax import lax

PANEL = 32
ROWS_DEV = 8192
S_DEV = 32
CAP = 64
ROWS = 4194304
SAMPLES = 16384
N_GX = 8
N_GY = 8
N_GZ = 8


def draw_pick_owner(key, part):
    key = jax.random.fold_in(key, 11)
    dev_count = N_GX * N_GY * N_GZ
    half_count = dev_count // 2
    key_order, key_offsets, key_perm = jax.random.split(key, 3)
    device_order = jax.random.permutation(key_order, dev_count).astype(jnp.int32)
    offsets = jax.random.randint(key_offsets, (half_count,), 0, S_DEV + 1).astype(jnp.int32)
    offsets = offsets.at[0].set(S_DEV)
    counts = jnp.zeros((dev_count,), jnp.int32)
    counts = counts.at[device_order[:half_count]].set(S_DEV + offsets)
    counts = counts.at[device_order[half_count:]].set(S_DEV - offsets)
    slot_index = jnp.arange(CAP, dtype=jnp.int32)[None, :]
    is_live = slot_index < counts[:, None]
    first_pos = jnp.cumsum(counts) - counts
    position = jnp.clip(first_pos[:, None] + slot_index, 0, SAMPLES - 1)
    shuffled = jax.random.permutation(key_perm, SAMPLES).astype(jnp.int32)
    owners = jnp.where(is_live, shuffled[position], -1)
    return owners.reshape(-1).astype(jnp.int32)


def set_ends(entries, own_key, low, high):
    place = [jax.random.randint(jax.random.fold_in(own_key, axis), (), 0, length) for axis, length in enumerate(entries.shape)]
    widest = entries.shape.index(max(entries.shape))
    next_to = place[:widest] + [(place[widest] + 1) % entries.shape[widest]] + place[widest + 1:]
    return entries.at[tuple(place)].set(low).at[tuple(next_to)].set(high)


def steps_of(own_key, shape, cuts, smallest, largest):
    def one(dim, parts):
        steps = jax.random.uniform(jax.random.fold_in(jax.random.fold_in(own_key, 6), dim), (parts,), jnp.float32, smallest / len(cuts), largest / len(cuts))
        return jnp.repeat(jnp.exp(steps), shape[dim] // parts).reshape((-1,) + (1,) * (len(shape) - dim - 1))

    level = one(*cuts[0])
    for cut in cuts[1:]:
        level = level * one(*cut)
    return level


def noise(key, dims, spread, limit, pieces=(), kind=jnp.bfloat16):
    entries = spread * jax.random.normal(key, dims, jnp.float32)
    if pieces:
        entries = entries * steps_of(key, dims, pieces, -0.22, 0.18)
    return jnp.clip(entries, -limit, limit).astype(kind)


def setup_inputs(seed: int = 0) -> dict:
    arg_keys = jax.random.split(jax.random.key(seed), 5)
    return {
        "hidden_panel": noise(arg_keys[0], (PANEL, ROWS), 1.0, 6.0, ((1, 512),), jnp.float32),
        "sign_bits": set_ends((jax.random.randint(arg_keys[1], (ROWS,), 0, 2) < 1).astype(jnp.int32), jax.random.fold_in(arg_keys[1], 1), 0, 1),
        "pick_rows": set_ends(jax.random.randint(arg_keys[2], (N_GX * N_GY * N_GZ * CAP,), 0, ROWS_DEV), jax.random.fold_in(arg_keys[2], 1), 0, ROWS_DEV - 1).astype(jnp.int32),
        "pick_owner": draw_pick_owner(jax.random.fold_in(arg_keys[4], 71), 0),
    }


def bit_parity(values, bit_count):
    parity = jnp.zeros_like(values)
    for bit_pos in range(bit_count):
        parity = parity ^ values >> bit_pos & 1
    return parity

def hadamard(matrix_order):
    positions = jnp.arange(matrix_order, dtype=jnp.int32)
    parity = bit_parity(positions[:, None] & positions[None, :], max(matrix_order.bit_length(), 1))
    return (1 - 2 * parity).astype(jnp.float32)

def reference(hidden_panel, sign_bits, pick_rows, pick_owner):
    dev_count = N_GX * N_GY * N_GZ
    blocks = ROWS_DEV // 256
    signed = hidden_panel * (1 - 2 * sign_bits).astype(jnp.float32)[None, :]
    folded = signed.reshape(PANEL, dev_count, blocks, 256)
    folded = jnp.einsum('pdab,bc->pdac', folded, hadamard(256), precision=lax.Precision.HIGHEST)
    folded = jnp.einsum('pdab,ca->pdcb', folded, hadamard(blocks), precision=lax.Precision.HIGHEST)
    folded = jnp.einsum('pdab,ed->peab', folded, hadamard(dev_count), precision=lax.Precision.HIGHEST)
    mixed = folded.reshape(PANEL, ROWS) * (1.0 / math.sqrt(ROWS))
    slot_dev = jnp.arange(dev_count * CAP, dtype=jnp.int32) // CAP
    global_row = (slot_dev * ROWS_DEV + pick_rows).astype(jnp.int32)
    target = jnp.where(pick_owner >= 0, pick_owner, SAMPLES).astype(jnp.int32)
    source = jnp.zeros((SAMPLES,), jnp.int32).at[target].set(global_row, mode='drop')
    return jnp.take(mixed, source, axis=1)
```

```python
import functools

import jax
import jax.numpy as jnp
import numpy as np
from jax import lax
from jax.experimental import pallas as pl
from jax.experimental.pallas import tpu as pltpu
from jax.sharding import Mesh, PartitionSpec as P

PANEL = 32
ROWS_DEV = 8192
CAP = 64
DEVS = 512
BASE = 256
FOLDS = ROWS_DEV // BASE
PAD = 8
TABLE = 2 * ROWS_DEV + 2 * PAD
LANES = 128
CHUNKS = 256
SCALE = 2.0**-11
NT = (((1,), (1,)), ((), ()))


def hadamard_np(order):
    matrix = np.ones((1, 1), np.float32)
    while matrix.shape[0] < order:
        matrix = np.block([[matrix, matrix], [matrix, -matrix]])
    return matrix


def butterflies(parts):
    half = 1
    while half < len(parts):
        for start in range(0, len(parts), 2 * half):
            for i in range(start, start + half):
                low, high = parts[i], parts[i + half]
                parts[i], parts[i + half] = low + high, low - high
        half *= 2
    return parts


def table_kernel(own_ref, other_ref, had_ref, table_ref, mixed):
    for half in range(BASE // LANES):
        def fold_rows(group, _, half=half):
            rows = pl.ds(pl.multiple_of(group * 8, 8), 8)
            for combine, at in ((lambda a, b: a + b, 0), (lambda a, b: a - b, PANEL)):
                parts = []
                for fold in range(FOLDS):
                    lanes = pl.ds(fold * BASE + half * LANES, LANES)
                    parts.append(combine(own_ref[rows, lanes], other_ref[rows, lanes]))
                out_rows = pl.ds(pl.multiple_of(group * 8 + at, 8), 8)
                for fold, part in enumerate(butterflies(parts)):
                    mixed[fold, out_rows, pl.ds(half * LANES, LANES)] = part
            return 0

        lax.fori_loop(0, PANEL // 8, fold_rows, 0)

    def transform(fold, _):
        block = mixed[fold]
        high = block.astype(jnp.bfloat16)
        low = (block - high.astype(jnp.float32)).astype(jnp.bfloat16)
        out = jnp.zeros((BASE, 2 * LANES), jnp.float32)
        for piece in (high, low):
            rhs = jnp.concatenate([piece[:PANEL]] * 4 + [piece[PANEL:]] * 4, axis=0)
            out += lax.dot_general(had_ref[...], rhs, NT, preferred_element_type=jnp.float32)
        at = pl.multiple_of(fold * BASE + PAD, 8)
        table_ref[pl.ds(at, BASE), :] = out[:, :LANES]
        table_ref[pl.ds(pl.multiple_of(at + ROWS_DEV, 8), BASE), :] = out[:, LANES:]
        return 0

    lax.fori_loop(0, FOLDS, transform, 0)
    edge = jnp.zeros((PAD, LANES), jnp.float32)
    table_ref[pl.ds(0, PAD), :] = edge
    table_ref[pl.ds(TABLE - PAD, PAD), :] = edge


def make_table(own, other):
    had = jnp.asarray(hadamard_np(BASE), jnp.bfloat16)
    return pl.pallas_call(
        table_kernel,
        out_shape=jax.ShapeDtypeStruct((TABLE, LANES), jnp.float32),
        in_specs=[pl.BlockSpec(memory_space=pltpu.VMEM)] * 3,
        out_specs=pl.BlockSpec(memory_space=pltpu.VMEM),
        scratch_shapes=[pltpu.VMEM((FOLDS, 2 * PANEL, BASE), jnp.float32)],
        compiler_params=pltpu.CompilerParams(vmem_limit_bytes=40 * 2**20),
        cost_estimate=pl.CostEstimate(flops=2 * 10**9, bytes_accessed=10 * 2**20, transcendentals=0),
        name="local_transform",
    )(own, other, had)


def pick_kernel(me_ref, slots_ref, spread_ref, table_hbm, out_ref, table, where_vmem, where_smem, signs, pairs, sems):
    table_copy = pltpu.make_async_copy(table_hbm, table, sems.at[0])
    table_copy.start()
    me = me_ref[0]
    core = me & 1
    lane = lax.broadcasted_iota(jnp.int32, (CHUNKS, LANES), 1)
    even, odd = slots_ref[pl.ds(0, CHUNKS, stride=2), :], slots_ref[pl.ds(1, CHUNKS, stride=2), :]
    first = lane < CAP
    picks = jnp.where(first, even, pltpu.roll(odd, CAP, 1))
    owner = jnp.where(first, pltpu.roll(even, CAP, 1), odd)
    device = 2 * lax.broadcasted_iota(jnp.int32, (CHUNKS, LANES), 0) + jnp.where(first, 0, 1)
    odd_bits = device & me
    for shift in (8, 4, 2, 1):
        odd_bits = odd_bits ^ (odd_bits >> shift)
    chip = owner >> 6
    chunk = (chip & 3) * 64 + (chip >> 2)
    mine = (owner >= 0) & (((owner >> 5) & 1) == core)
    pairs[0] = jnp.where(mine, chunk >> 1, -1)
    pairs[1] = (chunk & 1) * 32 + (owner & 31)
    pairs[2] = picks & (BASE - 1)
    pairs[3] = (device & 1) * FOLDS + (picks >> 8)
    pairs[4] = 1 - 2 * (odd_bits & 1)
    high_at = lax.broadcasted_iota(jnp.int32, (128, LANES), 0)
    low_at = lax.broadcasted_iota(jnp.int32, (64, LANES), 0)
    step = 8

    def invert(block, total):
        rows = pl.ds(pl.multiple_of(block * step, step), step)
        high, low, base, fold, sign = (pairs[i, rows, :] for i in range(5))
        base, fold, sign = (v.astype(jnp.float32) for v in (base, fold, sign))
        lhs, rhs = [], []
        for i in range(step):
            at = lambda v: v[i : i + 1, :]
            lhs.append(jnp.where(at(high) == high_at, 1.0, 0.0).astype(jnp.bfloat16))
            hit = at(low) == low_at
            rhs.append(
                jnp.concatenate(
                    [jnp.where(hit, at(v), 0.0) for v in (base, fold, sign)], axis=0
                ).astype(jnp.bfloat16)
            )
        return total + lax.dot_general(
            jnp.concatenate(lhs, axis=1),
            jnp.concatenate(rhs, axis=1),
            NT,
            preferred_element_type=jnp.float32,
        )

    total = lax.fori_loop(0, CHUNKS // step, invert, jnp.zeros((128, 192), jnp.float32))
    where_vmem[...] = (total[:, 64:128] * float(BASE) + total[:, :64]).astype(jnp.int32) + PAD
    where_copy = pltpu.make_async_copy(where_vmem, where_smem, sems.at[1])
    where_copy.start()
    sign = (total[:, 128:192] * SCALE).astype(jnp.bfloat16)
    for i in range(16):
        signs[pl.ds(i, 128, stride=16), :] = jnp.dot(
            sign, spread_ref[:, i * LANES : (i + 1) * LANES], preferred_element_type=jnp.float32
        )
    table_copy.wait()
    where_copy.wait()
    quarter = lax.broadcasted_iota(jnp.int32, (8, LANES), 1) // PANEL
    sub = lax.broadcasted_iota(jnp.int32, (8, LANES), 0)
    slot_of = sub * 4 + quarter

    def gather(pair, _):
        for side in range(2):
            parts = []
            for k in range(32):
                row = where_smem[pair, side * 32 + k]
                parts.append(table[pl.ds(row - k // 4, 8), :])
            value = parts[0]
            for k in range(1, 32):
                value = jnp.where(slot_of == k, parts[k], value)
            at = 2 * pair + side
            out_ref[at] = value * signs[pl.ds(pl.multiple_of(at * 8, 8), 8), :]
        return 0

    lax.fori_loop(0, CHUNKS // 2, gather, 0)


def spread_np():
    column = np.arange(16 * LANES)
    return (np.arange(64)[:, None] == (column // LANES * 4 + column % LANES // PANEL)[None, :]).astype(np.float32)


def pick_columns(me, slots, table):
    spread = jnp.asarray(spread_np(), jnp.bfloat16)
    return pl.pallas_call(
        pick_kernel,
        out_shape=jax.ShapeDtypeStruct((CHUNKS, 8, LANES), jnp.float32),
        in_specs=[
            pl.BlockSpec(memory_space=pltpu.SMEM),
            pl.BlockSpec(memory_space=pltpu.VMEM),
            pl.BlockSpec(memory_space=pltpu.VMEM),
            pl.BlockSpec(memory_space=pl.ANY),
        ],
        out_specs=pl.BlockSpec(memory_space=pltpu.VMEM),
        scratch_shapes=[
            pltpu.VMEM((TABLE, LANES), jnp.float32),
            pltpu.VMEM((128, 64), jnp.int32),
            pltpu.SMEM((128, 64), jnp.int32),
            pltpu.VMEM((CHUNKS * 8, LANES), jnp.float32),
            pltpu.VMEM((5, CHUNKS, LANES), jnp.int32),
            pltpu.SemaphoreType.DMA((2,)),
        ],
        compiler_params=pltpu.CompilerParams(vmem_limit_bytes=40 * 2**20),
        cost_estimate=pl.CostEstimate(flops=2 * 10**9, bytes_accessed=10 * 2**20, transcendentals=0),
        name="pick_columns",
    )(me, slots, spread, table)


def local(hidden_panel, sign_bits, pick_rows, pick_owner):
    me = ((lax.axis_index("gx") * 8 + lax.axis_index("gy")) * 4 + lax.axis_index("x")) * 2 + lax.axis_index("core")
    slots = jnp.concatenate([pick_rows, pick_owner]).reshape(1, 1, 2 * CAP)
    slots = lax.all_to_all(
        jnp.broadcast_to(slots, (DEVS, 1, 2 * CAP)),
        ("gx", "gy", "x", "core"),
        split_axis=0,
        concat_axis=0,
        tiled=True,
    ).reshape(DEVS, 2 * CAP)
    own = hidden_panel * (1 - 2 * sign_bits).astype(jnp.float32)[None, :]
    other = lax.ppermute(own, "core", [(0, 1), (1, 0)])
    table = make_table(own, other)
    columns = pick_columns(me.reshape(1).astype(jnp.int32), slots, table)
    columns = lax.all_to_all(columns, "x", split_axis=0, concat_axis=0, tiled=True)
    columns = columns.reshape(4, 64, 8, LANES).sum(axis=0)
    columns = lax.all_to_all(columns, ("gx", "gy"), split_axis=0, concat_axis=0, tiled=True)
    return columns.sum(axis=0).reshape(PANEL, PANEL).T


def solution(mesh):
    inner = Mesh(mesh.devices.reshape(8, 8, 4, 2), ("gx", "gy", "x", "core"))
    rows = ("gx", "gy", "x", "core")
    return jax.shard_map(
        local,
        mesh=inner,
        in_specs=(P(None, rows), P(rows), P(rows), P(rows)),
        out_specs=P(None, rows),
        check_vma=False,
    )
```

```python
import functools

import jax
import jax.numpy as jnp
import numpy as np
from jax import lax
from jax.experimental import pallas as pl
from jax.experimental.pallas import tpu as pltpu
from jax.sharding import Mesh, PartitionSpec as P

PANEL = 32
ROWS_DEV = 8192
CAP = 64
DEVS = 512
BASE = 256
FOLDS = ROWS_DEV // BASE
PAD = 8
TABLE = 2 * ROWS_DEV + 2 * PAD
LANES = 128
CHUNKS = 256
QUARTER = CHUNKS // 4
SCALE = 2.0**-11
NT = (((1,), (1,)), ((), ()))


def hadamard_np(order):
    matrix = np.ones((1, 1), np.float32)
    while matrix.shape[0] < order:
        matrix = np.block([[matrix, matrix], [matrix, -matrix]])
    return matrix


def butterflies(parts):
    half = 1
    while half < len(parts):
        for start in range(0, len(parts), 2 * half):
            for i in range(start, start + half):
                low, high = parts[i], parts[i + half]
                parts[i], parts[i + half] = low + high, low - high
        half *= 2
    return parts


def table_kernel(own_ref, other_ref, had_ref, table_ref, mixed):
    for half in range(BASE // LANES):
        def fold_rows(group, _, half=half):
            rows = pl.ds(pl.multiple_of(group * 8, 8), 8)
            for combine, at in ((lambda a, b: a + b, 0), (lambda a, b: a - b, PANEL)):
                parts = []
                for fold in range(FOLDS):
                    lanes = pl.ds(fold * BASE + half * LANES, LANES)
                    parts.append(combine(own_ref[rows, lanes], other_ref[rows, lanes]))
                out_rows = pl.ds(pl.multiple_of(group * 8 + at, 8), 8)
                for fold, part in enumerate(butterflies(parts)):
                    mixed[fold, out_rows, pl.ds(half * LANES, LANES)] = part
            return 0

        lax.fori_loop(0, PANEL // 8, fold_rows, 0)

    def transform(fold, _):
        block = mixed[fold]
        high = block.astype(jnp.bfloat16)
        low = (block - high.astype(jnp.float32)).astype(jnp.bfloat16)
        out = jnp.zeros((BASE, 2 * LANES), jnp.float32)
        for piece in (high, low):
            rhs = jnp.concatenate([piece[:PANEL]] * 4 + [piece[PANEL:]] * 4, axis=0)
            out += lax.dot_general(had_ref[...], rhs, NT, preferred_element_type=jnp.float32)
        at = pl.multiple_of(fold * BASE + PAD, 8)
        table_ref[pl.ds(at, BASE), :] = out[:, :LANES]
        table_ref[pl.ds(pl.multiple_of(at + ROWS_DEV, 8), BASE), :] = out[:, LANES:]
        return 0

    lax.fori_loop(0, FOLDS, transform, 0)
    edge = jnp.zeros((PAD, LANES), jnp.float32)
    table_ref[pl.ds(0, PAD), :] = edge
    table_ref[pl.ds(TABLE - PAD, PAD), :] = edge


def make_table(own, other):
    had = jnp.asarray(hadamard_np(BASE), jnp.bfloat16)
    return pl.pallas_call(
        table_kernel,
        out_shape=jax.ShapeDtypeStruct((TABLE, LANES), jnp.float32),
        in_specs=[pl.BlockSpec(memory_space=pltpu.VMEM)] * 3,
        out_specs=pl.BlockSpec(memory_space=pltpu.VMEM),
        scratch_shapes=[pltpu.VMEM((FOLDS, 2 * PANEL, BASE), jnp.float32)],
        compiler_params=pltpu.CompilerParams(vmem_limit_bytes=40 * 2**20),
        cost_estimate=pl.CostEstimate(flops=2 * 10**9, bytes_accessed=10 * 2**20, transcendentals=0),
        name="local_transform",
    )(own, other, had)


def gather_quarter(table, where, signs, base, out_ref):
    slot_of = (
        lax.broadcasted_iota(jnp.int32, (8, LANES), 0) * 4
        + lax.broadcasted_iota(jnp.int32, (8, LANES), 1) // PANEL
    )

    def gather(pair, _):
        for side in range(2):
            parts = [table[pl.ds(where[pair, side * 32 + k], 8), :] for k in range(32)]
            value = parts[0]
            for k in range(1, 32):
                value = jnp.where(slot_of == k, parts[k], value)
            at = 2 * pair + side
            out_ref[at] = value * signs[pl.ds(pl.multiple_of((base + at) * 8, 8), 8), :]
        return 0

    lax.fori_loop(0, QUARTER // 2, gather, 0)


def plan_kernel(me_ref, slots_ref, spread_ref, table, out_ref, where_vmem, signs, where_smem, pairs, sem):
    me, first_quarter = me_ref[0], me_ref[1]
    core = me & 1
    lane = lax.broadcasted_iota(jnp.int32, (CHUNKS, LANES), 1)
    even, odd = slots_ref[pl.ds(0, CHUNKS, stride=2), :], slots_ref[pl.ds(1, CHUNKS, stride=2), :]
    first = lane < CAP
    picks = jnp.where(first, even, pltpu.roll(odd, CAP, 1))
    owner = jnp.where(first, pltpu.roll(even, CAP, 1), odd)
    device = 2 * lax.broadcasted_iota(jnp.int32, (CHUNKS, LANES), 0) + jnp.where(first, 0, 1)
    odd_bits = device & me
    for shift in (8, 4, 2, 1):
        odd_bits = odd_bits ^ (odd_bits >> shift)
    chip = owner >> 6
    chunk = (chip & 3) * 64 + (chip >> 2)
    mine = (owner >= 0) & (((owner >> 5) & 1) == core)
    bf16 = lambda v: v.astype(jnp.float32).astype(jnp.bfloat16)
    fold = (device & 1) * FOLDS + (picks >> 8) + 1
    pairs[0] = bf16(jnp.where(mine, chunk >> 1, -1))
    pairs[1] = bf16((chunk & 1) * 32 + (owner & 31))
    pairs[2] = bf16(picks & (BASE - 1))
    pairs[3] = bf16(jnp.where((odd_bits & 1) == 1, -fold, fold))
    high_at = bf16(lax.broadcasted_iota(jnp.int32, (128, LANES), 0))
    low_at = bf16(lax.broadcasted_iota(jnp.int32, (64, LANES), 0))
    one, zero = jnp.ones((), jnp.bfloat16), jnp.zeros((), jnp.bfloat16)
    step = 16

    def invert(block, total):
        rows = pl.ds(pl.multiple_of(block * step, step), step)
        high, low, base, fold = (pairs[i, rows, :] for i in range(4))
        lhs, rhs = [], []
        for i in range(step):
            at = lambda v: v[i : i + 1, :]
            lhs.append(jnp.where(at(high) == high_at, one, zero))
            hit = at(low) == low_at
            rhs.append(jnp.concatenate([jnp.where(hit, at(v), zero) for v in (base, fold)], axis=0))
        return total + lax.dot_general(
            jnp.concatenate(lhs, axis=1),
            jnp.concatenate(rhs, axis=1),
            NT,
            preferred_element_type=jnp.float32,
        )

    total = lax.fori_loop(0, CHUNKS // step, invert, jnp.zeros((128, 128), jnp.float32))
    base, fold = total[:, :64], total[:, 64:]
    sub = lax.broadcasted_iota(jnp.int32, (128, 64), 1) % 32 // 4
    where_vmem[...] = ((jnp.abs(fold) - 1) * float(BASE) + base).astype(jnp.int32) + PAD - sub
    rows = pl.ds(pl.multiple_of(first_quarter * 32, 32), 32)
    where_copy = pltpu.make_async_copy(where_vmem.at[rows, :], where_smem, sem)
    where_copy.start()
    sign = jnp.where(fold < 0, -SCALE, SCALE).astype(jnp.bfloat16)
    for i in range(16):
        signs[pl.ds(i, 128, stride=16), :] = jnp.dot(
            sign, spread_ref[:, i * LANES : (i + 1) * LANES], preferred_element_type=jnp.float32
        )
    where_copy.wait()
    gather_quarter(table, where_smem, signs, first_quarter * QUARTER, out_ref)


def quarter_kernel(quarter_ref, where_vmem, signs, table, out_ref, where_smem, sem):
    quarter = quarter_ref[0]
    rows = pl.ds(pl.multiple_of(quarter * 32, 32), 32)
    where_copy = pltpu.make_async_copy(where_vmem.at[rows, :], where_smem, sem)
    where_copy.start()
    where_copy.wait()
    gather_quarter(table, where_smem, signs, quarter * QUARTER, out_ref)


def spread_np():
    column = np.arange(16 * LANES)
    return (np.arange(64)[:, None] == (column // LANES * 4 + column % LANES // PANEL)[None, :]).astype(np.float32)


VMEM, SMEM = pl.BlockSpec(memory_space=pltpu.VMEM), pl.BlockSpec(memory_space=pltpu.SMEM)


def plan_picks(me_and_quarter, slots, table):
    spread = jnp.asarray(spread_np(), jnp.bfloat16)
    return pl.pallas_call(
        plan_kernel,
        out_shape=(
            jax.ShapeDtypeStruct((QUARTER, 8, LANES), jnp.float32),
            jax.ShapeDtypeStruct((128, 64), jnp.int32),
            jax.ShapeDtypeStruct((CHUNKS * 8, LANES), jnp.float32),
        ),
        in_specs=[SMEM, VMEM, VMEM, VMEM],
        out_specs=(VMEM, VMEM, VMEM),
        scratch_shapes=[
            pltpu.SMEM((32, 64), jnp.int32),
            pltpu.VMEM((4, CHUNKS, LANES), jnp.bfloat16),
            pltpu.SemaphoreType.DMA,
        ],
        compiler_params=pltpu.CompilerParams(vmem_limit_bytes=40 * 2**20),
        cost_estimate=pl.CostEstimate(flops=2 * 10**9, bytes_accessed=10 * 2**20, transcendentals=0),
        name="plan_and_pick",
    )(me_and_quarter, slots, spread, table)


def pick_quarter(quarter, where, signs, table):
    return pl.pallas_call(
        quarter_kernel,
        out_shape=jax.ShapeDtypeStruct((QUARTER, 8, LANES), jnp.float32),
        in_specs=[SMEM, VMEM, VMEM, VMEM],
        out_specs=VMEM,
        scratch_shapes=[pltpu.SMEM((32, 64), jnp.int32), pltpu.SemaphoreType.DMA],
        compiler_params=pltpu.CompilerParams(vmem_limit_bytes=40 * 2**20),
        cost_estimate=pl.CostEstimate(flops=10**9, bytes_accessed=8 * 2**20, transcendentals=0),
        name="pick_quarter",
    )(quarter, where, signs, table)


def local(hidden_panel, sign_bits, pick_rows, pick_owner):
    x = lax.axis_index("x")
    me = ((lax.axis_index("gx") * 8 + lax.axis_index("gy")) * 4 + x) * 2 + lax.axis_index("core")
    slots = jnp.broadcast_to(jnp.concatenate([pick_rows, pick_owner]), (8, 1, 2 * CAP))
    slots = lax.all_to_all(slots, ("x", "core"), split_axis=0, concat_axis=0, tiled=True)
    slots = jnp.broadcast_to(slots.reshape(1, 8, 2 * CAP), (64, 8, 2 * CAP))
    slots = lax.all_to_all(slots, ("gx", "gy"), split_axis=0, concat_axis=0, tiled=True)
    slots = slots.reshape(DEVS, 2 * CAP)
    own = hidden_panel * (1 - 2 * sign_bits).astype(jnp.float32)[None, :]
    other = lax.ppermute(own, "core", [(0, 1), (1, 0)])
    table = make_table(own, other)
    quarter = lambda shift: (x + shift) % 4
    send = lambda v, shift: lax.ppermute(v, "x", [(i, (i + shift) % 4) for i in range(4)])
    picked, where, signs = plan_picks(jnp.stack([me, quarter(2)]).astype(jnp.int32), slots, table)
    arrived = [send(picked, 2)]
    for shift in (1, 3):
        at = quarter(shift).reshape(1).astype(jnp.int32)
        arrived.append(send(pick_quarter(at, where, signs, table), shift))
    columns = pick_quarter(x.reshape(1).astype(jnp.int32), where, signs, table)
    for part in arrived:
        columns = columns + part
    columns = lax.all_to_all(columns, ("gx", "gy"), split_axis=0, concat_axis=0, tiled=True)
    return columns.sum(axis=0).reshape(PANEL, PANEL).T


def solution(mesh):
    inner = Mesh(mesh.devices.reshape(8, 8, 4, 2), ("gx", "gy", "x", "core"))
    rows = ("gx", "gy", "x", "core")
    return jax.shard_map(
        local,
        mesh=inner,
        in_specs=(P(None, rows), P(rows), P(rows), P(rows)),
        out_specs=P(None, rows),
        check_vma=False,
    )
```

```python
import jax
import jax.numpy as jnp
import numpy as np
from jax import lax
from jax.experimental import pallas as pl
from jax.experimental.pallas import tpu as pltpu
from jax.sharding import Mesh, PartitionSpec as P

PANEL = 32
ROWS_DEV = 8192
CAP = 64
DEVS = 512
PART = PANEL // 2
SOURCES = 4
BASE = 256
FOLDS = ROWS_DEV // BASE
PAD = 8
TABLE = ROWS_DEV + 2 * PAD
LANES = 128
CHIPS = 256
OUT_ROWS = 4 * CHIPS
GROUP = 64
WIDE = 8 * GROUP
PIECES = 4
SCALE = 2.0**-11
NT = (((1,), (1,)), ((), ()))
VMEM, SMEM, HBM = (pl.BlockSpec(memory_space=m) for m in (pltpu.VMEM, pltpu.SMEM, pltpu.HBM))


def hadamard_np(order):
    matrix = np.ones((1, 1), np.float32)
    while matrix.shape[0] < order:
        matrix = np.block([[matrix, matrix], [matrix, -matrix]])
    return matrix


def butterflies(parts):
    half = 1
    while half < len(parts):
        for start in range(0, len(parts), 2 * half):
            for i in range(start, start + half):
                low, high = parts[i], parts[i + half]
                parts[i], parts[i + half] = low + high, low - high
        half *= 2
    return parts


def join_kernel(own_ref, near_ref, slots_ref, out_ref):
    out_ref[0] = own_ref[...]
    out_ref[1] = near_ref[...]


def join(own, near, slots):
    return pl.pallas_call(
        join_kernel,
        out_shape=jax.ShapeDtypeStruct((2, PART, ROWS_DEV), jnp.float32),
        in_specs=[VMEM, VMEM, HBM],
        out_specs=VMEM,
        compiler_params=pltpu.CompilerParams(vmem_limit_bytes=8 * 2**20),
        cost_estimate=pl.CostEstimate(flops=0, bytes_accessed=2**21, transcendentals=0),
        name="join_halves",
    )(own, near, slots)


def table_kernel(own_ref, other_ref, had_ref, table_hbm, mixed, table, sems):
    for source, (ref, chip) in enumerate((ref, chip) for ref in (own_ref, other_ref) for chip in range(2)):
        def fold_rows(step, _, ref=ref, chip=chip, source=source):
            group, half = step // 2, step % 2
            rows = pl.ds(pl.multiple_of(group * 8, 8), 8)
            column = half * LANES
            parts = [ref[chip, rows, pl.ds(pl.multiple_of(fold * BASE + column, LANES), LANES)] for fold in range(FOLDS)]
            out_rows = pl.ds(pl.multiple_of(source * PART + group * 8, 8), 8)
            for fold, part in enumerate(butterflies(parts)):
                mixed[fold, out_rows, pl.ds(pl.multiple_of(column, LANES), LANES)] = part
            return 0

        lax.fori_loop(0, PART // 8 * 2, fold_rows, 0)

    edge = jnp.zeros((PAD, LANES), jnp.float32)
    table[pl.ds(0, PAD), :] = edge
    table[pl.ds(TABLE - PAD, PAD), :] = edge

    def transform(pair, _):
        highs, lows = [], []
        for i in range(2):
            fold = 2 * pair + i
            block = jnp.concatenate(
                butterflies([mixed[fold, pl.ds(source * PART, PART), :] for source in range(SOURCES)]), axis=0
            )
            high = block.astype(jnp.bfloat16)
            low = (block - high.astype(jnp.float32)).astype(jnp.bfloat16)
            highs += [high, high]
            lows += [low, low]
        out = jnp.zeros((BASE, 2 * LANES), jnp.float32)
        for pieces in (highs, lows):
            out += lax.dot_general(
                had_ref[...], jnp.concatenate(pieces, axis=0), NT, preferred_element_type=jnp.float32
            )
        for i in range(2):
            at = pl.multiple_of((2 * pair + i) * BASE + PAD, 8)
            table[pl.ds(at, BASE), :] = out[:, i * LANES : (i + 1) * LANES]
        return 0

    copies = []
    for piece in range(PIECES):
        lax.fori_loop(piece * FOLDS // 2 // PIECES, (piece + 1) * FOLDS // 2 // PIECES, transform, 0, unroll=2)
        start = piece * (ROWS_DEV // PIECES)
        end = TABLE if piece == PIECES - 1 else start + ROWS_DEV // PIECES
        rows = pl.ds(start, end - start)
        copies.append(pltpu.make_async_copy(table.at[rows, :], table_hbm.at[rows, :], sems.at[piece]))
        copies[-1].start()
    for copy in copies:
        copy.wait()


def make_table(own, other):
    had = jnp.asarray(hadamard_np(BASE), jnp.bfloat16)
    return pl.pallas_call(
        table_kernel,
        out_shape=pltpu.HBM((TABLE, LANES), jnp.float32),
        in_specs=[VMEM] * 3,
        out_specs=HBM,
        scratch_shapes=[
            pltpu.VMEM((FOLDS, SOURCES * PART, BASE), jnp.float32),
            pltpu.VMEM((TABLE, LANES), jnp.float32),
            pltpu.SemaphoreType.DMA((PIECES,)),
        ],
        compiler_params=pltpu.CompilerParams(vmem_limit_bytes=24 * 2**20),
        cost_estimate=pl.CostEstimate(flops=10**9, bytes_accessed=10 * 2**20, transcendentals=0),
        name="local_transform",
    )(own, other, had)


def pick_kernel(
    me_ref, slots_ref, spread_ref, reduce_ref, table_hbm, out_ref, table, where_vmem, where_smem, signs, pairs, wide, sems
):
    table_copy = pltpu.make_async_copy(table_hbm, table, sems.at[0])
    table_copy.start()
    me = me_ref[0]
    core = me & 1
    lane = lax.broadcasted_iota(jnp.int32, (DEVS // 2, LANES), 1)
    even, odd = slots_ref[pl.ds(0, DEVS // 2, stride=2), :], slots_ref[pl.ds(1, DEVS // 2, stride=2), :]
    first = lane < CAP
    picks = jnp.where(first, even, pltpu.roll(odd, CAP, 1))
    owner = jnp.where(first, pltpu.roll(even, CAP, 1), odd)
    device = 2 * lax.broadcasted_iota(jnp.int32, (DEVS // 2, LANES), 0) + jnp.where(first, 0, 1)
    odd_bits = device & me
    for shift in (8, 4, 2, 1):
        odd_bits = odd_bits ^ (odd_bits >> shift)
    mine = (owner >= 0) & (((owner >> 5) & 1) == core)
    bf16 = lambda v: v.astype(jnp.float32).astype(jnp.bfloat16)
    combo = (device & 1) * 2 + ((device >> 1) & 1)
    fold = combo * FOLDS + (picks >> 8) + 1
    pairs[0] = bf16(jnp.where(mine, owner >> 7, -1))
    pairs[1] = bf16(((owner >> 6) & 1) * 32 + (owner & 31))
    pairs[2] = bf16(picks & (BASE - 1))
    pairs[3] = bf16(jnp.where((odd_bits & 1) == 1, -fold, fold))
    high_at = bf16(lax.broadcasted_iota(jnp.int32, (128, LANES), 0))
    low_at = bf16(lax.broadcasted_iota(jnp.int32, (64, LANES), 0))
    one, zero = jnp.ones((), jnp.bfloat16), jnp.zeros((), jnp.bfloat16)
    step = 16

    def invert(block, total):
        rows = pl.ds(pl.multiple_of(block * step, step), step)
        high, low, base, fold = (pairs[i, rows, :] for i in range(4))
        lhs, rhs = [], []
        for i in range(step):
            at = lambda v: v[i : i + 1, :]
            lhs.append(jnp.where(at(high) == high_at, one, zero))
            hit = at(low) == low_at
            rhs.append(jnp.concatenate([jnp.where(hit, at(v), zero) for v in (base, fold)], axis=0))
        return total + lax.dot_general(
            jnp.concatenate(lhs, axis=1),
            jnp.concatenate(rhs, axis=1),
            NT,
            preferred_element_type=jnp.float32,
        )

    total = lax.fori_loop(0, DEVS // 2 // step, invert, jnp.zeros((128, 128), jnp.float32))
    base, fold = total[:, :64].astype(jnp.int32), total[:, 64:].astype(jnp.int32)
    place = jnp.abs(fold) - 1
    sub = lax.broadcasted_iota(jnp.int32, (128, 64), 1) // 8
    where_vmem[...] = (place & (FOLDS - 1)) * BASE + base + PAD - sub
    where_copy = pltpu.make_async_copy(where_vmem, where_smem, sems.at[1])
    where_copy.start()
    combo = (place >> 5) + 1
    signed = bf16(jnp.where(fold < 0, -combo, combo))
    for i in range(8):
        spread = jnp.dot(signed, spread_ref[:, i * WIDE : (i + 1) * WIDE], preferred_element_type=jnp.float32)
        for pair in range(4):
            signs[pair, pl.ds(i, 128, stride=8), :] = spread[:, pair * LANES : (pair + 1) * LANES]
    where_copy.wait()
    table_copy.wait()
    lane = lax.broadcasted_iota(jnp.int32, (8, LANES), 1)
    slot_of = lax.broadcasted_iota(jnp.int32, (8, LANES), 0) * 2 + lane // GROUP
    match = (lane % GROUP // PART + 1).astype(jnp.float32)

    def gather(block, _):
        rows = pl.ds(pl.multiple_of(block * 8, 8), 8)
        for pair in range(4):
            parts = [
                table[pl.ds(where_smem[block, k // 2 * 8 + 2 * pair + k % 2], 8), :]
                for k in range(16)
            ]
            value = parts[0]
            for k in range(1, 16):
                value = jnp.where(slot_of == k, parts[k], value)
            lanes = pl.ds(pair * LANES, LANES)
            sign = signs[pair, rows, :]
            wide[rows, lanes] = jnp.where(sign == match, value, jnp.where(sign == -match, -value, 0.0))
        return 0

    lax.fori_loop(0, OUT_ROWS // 8, gather, 0)
    block = wide[...]
    high = block.astype(jnp.bfloat16)
    low = (block - high.astype(jnp.float32)).astype(jnp.bfloat16)
    out_ref[...] = jnp.dot(high, reduce_ref[...], preferred_element_type=jnp.float32) + jnp.dot(
        low, reduce_ref[...], preferred_element_type=jnp.float32
    )


def spread_np():
    column = np.arange(8 * WIDE)
    return (np.arange(64)[:, None] == (column // WIDE * 8 + column % WIDE // GROUP)[None, :]).astype(np.float32)


def reduce_np():
    row = np.arange(WIDE)
    return SCALE * ((row // GROUP * PART + row % PART)[:, None] == np.arange(LANES)[None, :]).astype(np.float32)


def pick_columns(me, slots, table):
    return pl.pallas_call(
        pick_kernel,
        out_shape=jax.ShapeDtypeStruct((OUT_ROWS, LANES), jnp.float32),
        in_specs=[SMEM, VMEM, VMEM, VMEM, HBM],
        out_specs=VMEM,
        scratch_shapes=[
            pltpu.VMEM((TABLE, LANES), jnp.float32),
            pltpu.VMEM((128, 64), jnp.int32),
            pltpu.SMEM((128, 64), jnp.int32),
            pltpu.VMEM((4, OUT_ROWS, LANES), jnp.float32),
            pltpu.VMEM((4, DEVS // 2, LANES), jnp.bfloat16),
            pltpu.VMEM((OUT_ROWS, WIDE), jnp.float32),
            pltpu.SemaphoreType.DMA((2,)),
        ],
        compiler_params=pltpu.CompilerParams(vmem_limit_bytes=24 * 2**20),
        cost_estimate=pl.CostEstimate(flops=2 * 10**9, bytes_accessed=10 * 2**20, transcendentals=0),
        name="pick_columns",
    )(
        me,
        slots,
        jnp.asarray(spread_np(), jnp.bfloat16),
        jnp.asarray(reduce_np(), jnp.bfloat16),
        pltpu.with_memory_space_constraint(table, pltpu.HBM),
    )


def local(hidden_panel, sign_bits, pick_rows, pick_owner):
    me = ((lax.axis_index("gx") * 8 + lax.axis_index("gy")) * 4 + lax.axis_index("x")) * 2 + lax.axis_index("core")
    slots = jnp.broadcast_to(jnp.concatenate([pick_rows, pick_owner]), (8, 1, 2 * CAP))
    first_slots = lax.all_to_all(slots, ("x", "core"), split_axis=0, concat_axis=0, tiled=True)
    slots = jnp.broadcast_to(first_slots.reshape(1, 8, 2 * CAP), (64, 8, 2 * CAP))
    slots = lax.all_to_all(slots, ("gx", "gy"), split_axis=0, concat_axis=0, tiled=True)
    slots = slots.reshape(DEVS, 2 * CAP)
    side = lax.axis_index("x") % 2
    sign = (1 - 2 * sign_bits).astype(jnp.float32)[None, :]
    half = lambda at: lax.dynamic_slice_in_dim(hidden_panel, at * PART, PART, 0) * sign
    near = lax.ppermute(half(1 - side), "x", [(i, i ^ 1) for i in range(4)])
    own = join(half(side), near, first_slots)
    table = make_table(own, lax.ppermute(own, "core", [(0, 1), (1, 0)]))
    columns = pick_columns(me.reshape(1).astype(jnp.int32), slots, table)
    columns = lax.all_to_all(
        columns.reshape(CHIPS, 4, LANES), ("gx", "gy", "x"), split_axis=0, concat_axis=0, tiled=True
    )
    columns = columns.reshape(128, 2, 4, LANES).sum(axis=0)
    return columns.reshape(2, 4, 8, PART).transpose(0, 3, 1, 2).reshape(PANEL, PANEL)


def solution(mesh):
    inner = Mesh(mesh.devices.reshape(8, 8, 4, 2), ("gx", "gy", "x", "core"))
    rows = ("gx", "gy", "x", "core")
    return jax.shard_map(
        local,
        mesh=inner,
        in_specs=(P(None, rows), P(rows), P(rows), P(rows)),
        out_specs=P(None, rows),
        check_vma=False,
    )
```

```python
import jax
import jax.numpy as jnp
import numpy as np
from jax import lax
from jax.experimental import pallas as pl
from jax.experimental.pallas import tpu as pltpu
from jax.sharding import Mesh, PartitionSpec as P

PANEL = 32
ROWS_DEV = 8192
CAP = 64
DEVS = 512
PART = PANEL // 2
SOURCES = 4
BASE = 256
FOLDS = ROWS_DEV // BASE
PAD = 8
TABLE = ROWS_DEV + 2 * PAD
LANES = 128
CHIPS = 256
OUT_ROWS = 4 * CHIPS
GROUP = 64
WIDE = 8 * GROUP
PIECES = 4
SCALE = 2.0**-11
NT = (((1,), (1,)), ((), ()))
VMEM, SMEM, HBM = (pl.BlockSpec(memory_space=m) for m in (pltpu.VMEM, pltpu.SMEM, pltpu.HBM))


def hadamard_np(order):
    matrix = np.ones((1, 1), np.float32)
    while matrix.shape[0] < order:
        matrix = np.block([[matrix, matrix], [matrix, -matrix]])
    return matrix


def butterflies(parts):
    half = 1
    while half < len(parts):
        for start in range(0, len(parts), 2 * half):
            for i in range(start, start + half):
                low, high = parts[i], parts[i + half]
                parts[i], parts[i + half] = low + high, low - high
        half *= 2
    return parts


def join_kernel(own_ref, near_ref, slots_ref, out_ref):
    out_ref[0] = own_ref[...]
    out_ref[1] = near_ref[...]


def join(own, near, slots):
    return pl.pallas_call(
        join_kernel,
        out_shape=jax.ShapeDtypeStruct((2, PART, ROWS_DEV), jnp.float32),
        in_specs=[VMEM, VMEM, HBM],
        out_specs=VMEM,
        compiler_params=pltpu.CompilerParams(vmem_limit_bytes=8 * 2**20),
        cost_estimate=pl.CostEstimate(flops=0, bytes_accessed=2**21, transcendentals=0),
        name="join_halves",
    )(own, near, slots)


def table_kernel(own_ref, other_ref, had_ref, table_hbm, mixed, table, sems):
    for source, (ref, chip) in enumerate((ref, chip) for ref in (own_ref, other_ref) for chip in range(2)):
        def fold_rows(step, _, ref=ref, chip=chip, source=source):
            group, half = step // 2, step % 2
            rows = pl.ds(pl.multiple_of(group * 8, 8), 8)
            column = half * LANES
            parts = [ref[chip, rows, pl.ds(pl.multiple_of(fold * BASE + column, LANES), LANES)] for fold in range(FOLDS)]
            out_rows = pl.ds(pl.multiple_of(source * PART + group * 8, 8), 8)
            for fold, part in enumerate(butterflies(parts)):
                mixed[fold, out_rows, pl.ds(pl.multiple_of(column, LANES), LANES)] = part
            return 0

        lax.fori_loop(0, PART // 8 * 2, fold_rows, 0)

    edge = jnp.zeros((PAD, LANES), jnp.float32)
    table[pl.ds(0, PAD), :] = edge
    table[pl.ds(TABLE - PAD, PAD), :] = edge

    def transform(pair, _):
        highs, lows = [], []
        for i in range(2):
            fold = 2 * pair + i
            block = jnp.concatenate(
                butterflies([mixed[fold, pl.ds(source * PART, PART), :] for source in range(SOURCES)]), axis=0
            )
            high = block.astype(jnp.bfloat16)
            low = (block - high.astype(jnp.float32)).astype(jnp.bfloat16)
            highs += [high, high]
            lows += [low, low]
        out = jnp.zeros((BASE, 2 * LANES), jnp.float32)
        for pieces in (highs, lows):
            out += lax.dot_general(
                had_ref[...], jnp.concatenate(pieces, axis=0), NT, preferred_element_type=jnp.float32
            )
        for i in range(2):
            at = pl.multiple_of((2 * pair + i) * BASE + PAD, 8)
            table[pl.ds(at, BASE), :] = out[:, i * LANES : (i + 1) * LANES]
        return 0

    copies = []
    for piece in range(PIECES):
        lax.fori_loop(piece * FOLDS // 2 // PIECES, (piece + 1) * FOLDS // 2 // PIECES, transform, 0, unroll=2)
        start = piece * (ROWS_DEV // PIECES)
        end = TABLE if piece == PIECES - 1 else start + ROWS_DEV // PIECES
        rows = pl.ds(start, end - start)
        copies.append(pltpu.make_async_copy(table.at[rows, :], table_hbm.at[rows, :], sems.at[piece]))
        copies[-1].start()
    for copy in copies:
        copy.wait()


def make_table(own, other):
    had = jnp.asarray(hadamard_np(BASE), jnp.bfloat16)
    return pl.pallas_call(
        table_kernel,
        out_shape=pltpu.HBM((TABLE, LANES), jnp.float32),
        in_specs=[VMEM] * 3,
        out_specs=HBM,
        scratch_shapes=[
            pltpu.VMEM((FOLDS, SOURCES * PART, BASE), jnp.float32),
            pltpu.VMEM((TABLE, LANES), jnp.float32),
            pltpu.SemaphoreType.DMA((PIECES,)),
        ],
        compiler_params=pltpu.CompilerParams(vmem_limit_bytes=24 * 2**20),
        cost_estimate=pl.CostEstimate(flops=10**9, bytes_accessed=10 * 2**20, transcendentals=0),
        name="local_transform",
    )(own, other, had)


def pick_kernel(
    me_ref, slots_ref, spread_ref, reduce_ref, table_hbm, out_ref, table, where_vmem, where_smem, signs, pairs, wide, sems
):
    table_copy = pltpu.make_async_copy(table_hbm, table, sems.at[0])
    table_copy.start()
    me = me_ref[0]
    core = me & 1
    lane = lax.broadcasted_iota(jnp.int32, (DEVS // 2, LANES), 1)
    even, odd = slots_ref[pl.ds(0, DEVS // 2, stride=2), :], slots_ref[pl.ds(1, DEVS // 2, stride=2), :]
    first = lane < CAP
    picks = jnp.where(first, even, pltpu.roll(odd, CAP, 1))
    owner = jnp.where(first, pltpu.roll(even, CAP, 1), odd)
    place = 2 * lax.broadcasted_iota(jnp.int32, (DEVS // 2, LANES), 0) + jnp.where(first, 0, 1)
    device = (place & 63) * 8 + (place >> 6)
    odd_bits = device & me
    for shift in (8, 4, 2, 1):
        odd_bits = odd_bits ^ (odd_bits >> shift)
    mine = (owner >= 0) & (((owner >> 5) & 1) == core)
    bf16 = lambda v: v.astype(jnp.float32).astype(jnp.bfloat16)
    combo = (device & 1) * 2 + ((device >> 1) & 1)
    fold = combo * FOLDS + (picks >> 8) + 1
    pairs[0] = bf16(jnp.where(mine, owner >> 7, -1))
    pairs[1] = bf16(((owner >> 6) & 1) * 32 + (owner & 31))
    pairs[2] = bf16(picks & (BASE - 1))
    pairs[3] = bf16(jnp.where((odd_bits & 1) == 1, -fold, fold))
    high_at = bf16(lax.broadcasted_iota(jnp.int32, (128, LANES), 0))
    low_at = bf16(lax.broadcasted_iota(jnp.int32, (64, LANES), 0))
    one, zero = jnp.ones((), jnp.bfloat16), jnp.zeros((), jnp.bfloat16)
    step = 16

    def invert(block, total):
        rows = pl.ds(pl.multiple_of(block * step, step), step)
        high, low, base, fold = (pairs[i, rows, :] for i in range(4))
        lhs, rhs = [], []
        for i in range(step):
            at = lambda v: v[i : i + 1, :]
            lhs.append(jnp.where(at(high) == high_at, one, zero))
            hit = at(low) == low_at
            rhs.append(jnp.concatenate([jnp.where(hit, at(v), zero) for v in (base, fold)], axis=0))
        return total + lax.dot_general(
            jnp.concatenate(lhs, axis=1),
            jnp.concatenate(rhs, axis=1),
            NT,
            preferred_element_type=jnp.float32,
        )

    total = lax.fori_loop(0, DEVS // 2 // step, invert, jnp.zeros((128, 128), jnp.float32), unroll=4)
    base, fold = total[:, :64].astype(jnp.int32), total[:, 64:].astype(jnp.int32)
    place = jnp.abs(fold) - 1
    sub = lax.broadcasted_iota(jnp.int32, (128, 64), 1) // 8
    where_vmem[...] = (place & (FOLDS - 1)) * BASE + base + PAD - sub
    where_copies = []
    for piece in range(PIECES):
        rows = pl.ds(piece * (128 // PIECES), 128 // PIECES)
        where_copies.append(
            pltpu.make_async_copy(where_vmem.at[rows, :], where_smem.at[rows, :], sems.at[1 + piece])
        )
        where_copies[-1].start()
    combo = (place >> 5) + 1
    signed = bf16(jnp.where(fold < 0, -combo, combo))
    for i in range(8):
        spread = jnp.dot(signed, spread_ref[:, i * WIDE : (i + 1) * WIDE], preferred_element_type=jnp.float32)
        for pair in range(4):
            signs[pair, pl.ds(i, 128, stride=8), :] = spread[:, pair * LANES : (pair + 1) * LANES]
    table_copy.wait()
    lane = lax.broadcasted_iota(jnp.int32, (8, LANES), 1)
    slot_of = lax.broadcasted_iota(jnp.int32, (8, LANES), 0) * 2 + lane // GROUP
    match = (lane % GROUP // PART + 1).astype(jnp.float32)

    def gather(block, _):
        rows = pl.ds(pl.multiple_of(block * 8, 8), 8)
        for pair in range(4):
            parts = [
                table[pl.ds(where_smem[block, k // 2 * 8 + 2 * pair + k % 2], 8), :]
                for k in range(16)
            ]
            value = parts[0]
            for k in range(1, 16):
                value = jnp.where(slot_of == k, parts[k], value)
            lanes = pl.ds(pair * LANES, LANES)
            sign = signs[pair, rows, :]
            wide[rows, lanes] = jnp.where(sign == match, value, jnp.where(sign == -match, -value, 0.0))
        return 0

    for piece in range(PIECES):
        where_copies[piece].wait()
        blocks = OUT_ROWS // 8 // PIECES
        lax.fori_loop(piece * blocks, (piece + 1) * blocks, gather, 0, unroll=2)
    block = wide[...]
    high = block.astype(jnp.bfloat16)
    low = (block - high.astype(jnp.float32)).astype(jnp.bfloat16)
    out_ref[...] = jnp.dot(high, reduce_ref[...], preferred_element_type=jnp.float32) + jnp.dot(
        low, reduce_ref[...], preferred_element_type=jnp.float32
    )


def spread_np():
    column = np.arange(8 * WIDE)
    return (np.arange(64)[:, None] == (column // WIDE * 8 + column % WIDE // GROUP)[None, :]).astype(np.float32)


def reduce_np():
    row = np.arange(WIDE)
    return SCALE * ((row // GROUP * PART + row % PART)[:, None] == np.arange(LANES)[None, :]).astype(np.float32)


def pick_columns(me, slots, table):
    return pl.pallas_call(
        pick_kernel,
        out_shape=jax.ShapeDtypeStruct((OUT_ROWS, LANES), jnp.float32),
        in_specs=[SMEM, VMEM, VMEM, VMEM, HBM],
        out_specs=VMEM,
        scratch_shapes=[
            pltpu.VMEM((TABLE, LANES), jnp.float32),
            pltpu.VMEM((128, 64), jnp.int32),
            pltpu.SMEM((128, 64), jnp.int32),
            pltpu.VMEM((4, OUT_ROWS, LANES), jnp.float32),
            pltpu.VMEM((4, DEVS // 2, LANES), jnp.bfloat16),
            pltpu.VMEM((OUT_ROWS, WIDE), jnp.float32),
            pltpu.SemaphoreType.DMA((1 + PIECES,)),
        ],
        compiler_params=pltpu.CompilerParams(vmem_limit_bytes=24 * 2**20),
        cost_estimate=pl.CostEstimate(flops=2 * 10**9, bytes_accessed=10 * 2**20, transcendentals=0),
        name="pick_columns",
    )(
        me,
        slots,
        jnp.asarray(spread_np(), jnp.bfloat16),
        jnp.asarray(reduce_np(), jnp.bfloat16),
        pltpu.with_memory_space_constraint(table, pltpu.HBM),
    )


def local(hidden_panel, sign_bits, pick_rows, pick_owner):
    me = ((lax.axis_index("gx") * 8 + lax.axis_index("gy")) * 4 + lax.axis_index("x")) * 2 + lax.axis_index("core")
    slots = jnp.broadcast_to(jnp.concatenate([pick_rows, pick_owner]), (64, 1, 2 * CAP))
    first_slots = lax.all_to_all(slots, ("gx", "gy"), split_axis=0, concat_axis=0, tiled=True)
    slots = jnp.broadcast_to(first_slots.reshape(1, 64, 2 * CAP), (8, 64, 2 * CAP))
    slots = lax.all_to_all(slots, ("x", "core"), split_axis=0, concat_axis=0, tiled=True)
    slots = slots.reshape(DEVS, 2 * CAP)
    side = lax.axis_index("x") % 2
    sign = (1 - 2 * sign_bits).astype(jnp.float32)[None, :]
    half = lambda at: lax.dynamic_slice_in_dim(hidden_panel, at * PART, PART, 0) * sign
    near = lax.ppermute(half(1 - side), "x", [(i, i ^ 1) for i in range(4)])
    own = join(half(side), near, first_slots)
    table = make_table(own, lax.ppermute(own, "core", [(0, 1), (1, 0)]))
    columns = pick_columns(me.reshape(1).astype(jnp.int32), slots, table)
    columns = lax.all_to_all(
        columns.reshape(CHIPS, 4, LANES), ("gx", "gy", "x"), split_axis=0, concat_axis=0, tiled=True
    )
    columns = columns.reshape(128, 2, 4, LANES).sum(axis=0)
    return columns.reshape(2, 4, 8, PART).transpose(0, 3, 1, 2).reshape(PANEL, PANEL)


def solution(mesh):
    inner = Mesh(mesh.devices.reshape(8, 8, 4, 2), ("gx", "gy", "x", "core"))
    rows = ("gx", "gy", "x", "core")
    return jax.shard_map(
        local,
        mesh=inner,
        in_specs=(P(None, rows), P(rows), P(rows), P(rows)),
        out_specs=P(None, rows),
        check_vma=False,
    )
```

```python
import jax
import jax.numpy as jnp
import numpy as np
from jax import lax
from jax.experimental import pallas as pl
from jax.experimental.pallas import tpu as pltpu
from jax.sharding import Mesh, PartitionSpec as P

PANEL = 32
ROWS_DEV = 8192
CAP = 64
DEVS = 512
PART = PANEL // 2
SOURCES = 4
BASE = 256
FOLDS = ROWS_DEV // BASE
PAD = 8
TABLE = ROWS_DEV + 2 * PAD
LANES = 128
CHIPS = 256
OUT_ROWS = 4 * CHIPS
GROUP = 64
WIDE = 8 * GROUP
PIECES = 4
SCALE = 2.0**-11
NT = (((1,), (1,)), ((), ()))
VMEM, SMEM, HBM = (pl.BlockSpec(memory_space=m) for m in (pltpu.VMEM, pltpu.SMEM, pltpu.HBM))


def hadamard_np(order):
    matrix = np.ones((1, 1), np.float32)
    while matrix.shape[0] < order:
        matrix = np.block([[matrix, matrix], [matrix, -matrix]])
    return matrix


def butterflies(parts):
    half = 1
    while half < len(parts):
        for start in range(0, len(parts), 2 * half):
            for i in range(start, start + half):
                low, high = parts[i], parts[i + half]
                parts[i], parts[i + half] = low + high, low - high
        half *= 2
    return parts


def join_kernel(own_ref, near_ref, slots_ref, out_ref):
    out_ref[0] = own_ref[...]
    out_ref[1] = near_ref[...]


def join(own, near, slots):
    return pl.pallas_call(
        join_kernel,
        out_shape=jax.ShapeDtypeStruct((2, PART, ROWS_DEV), jnp.float32),
        in_specs=[VMEM, VMEM, HBM],
        out_specs=VMEM,
        compiler_params=pltpu.CompilerParams(vmem_limit_bytes=8 * 2**20),
        cost_estimate=pl.CostEstimate(flops=0, bytes_accessed=2**21, transcendentals=0),
        name="join_halves",
    )(own, near, slots)


def table_kernel(own_ref, other_ref, had_ref, table_hbm, mixed, table, sems):
    for source, (ref, chip) in enumerate((ref, chip) for ref in (own_ref, other_ref) for chip in range(2)):
        def fold_rows(step, _, ref=ref, chip=chip, source=source):
            group, half = step // 2, step % 2
            rows = pl.ds(pl.multiple_of(group * 8, 8), 8)
            column = half * LANES
            parts = [ref[chip, rows, pl.ds(pl.multiple_of(fold * BASE + column, LANES), LANES)] for fold in range(FOLDS)]
            out_rows = pl.ds(pl.multiple_of(source * PART + group * 8, 8), 8)
            for fold, part in enumerate(butterflies(parts)):
                mixed[fold, out_rows, pl.ds(pl.multiple_of(column, LANES), LANES)] = part
            return 0

        lax.fori_loop(0, PART // 8 * 2, fold_rows, 0)

    edge = jnp.zeros((PAD, LANES), jnp.float32)
    table[pl.ds(0, PAD), :] = edge
    table[pl.ds(TABLE - PAD, PAD), :] = edge

    def transform(pair, _):
        highs, lows = [], []
        for i in range(2):
            fold = 2 * pair + i
            block = jnp.concatenate(
                butterflies([mixed[fold, pl.ds(source * PART, PART), :] for source in range(SOURCES)]), axis=0
            )
            high = block.astype(jnp.bfloat16)
            low = (block - high.astype(jnp.float32)).astype(jnp.bfloat16)
            highs += [high, high]
            lows += [low, low]
        out = jnp.zeros((BASE, 2 * LANES), jnp.float32)
        for pieces in (highs, lows):
            out += lax.dot_general(
                had_ref[...], jnp.concatenate(pieces, axis=0), NT, preferred_element_type=jnp.float32
            )
        for i in range(2):
            at = pl.multiple_of((2 * pair + i) * BASE + PAD, 8)
            table[pl.ds(at, BASE), :] = out[:, i * LANES : (i + 1) * LANES]
        return 0

    copies = []
    for piece in range(PIECES):
        lax.fori_loop(piece * FOLDS // 2 // PIECES, (piece + 1) * FOLDS // 2 // PIECES, transform, 0, unroll=2)
        start = piece * (ROWS_DEV // PIECES)
        end = TABLE if piece == PIECES - 1 else start + ROWS_DEV // PIECES
        rows = pl.ds(start, end - start)
        copies.append(pltpu.make_async_copy(table.at[rows, :], table_hbm.at[rows, :], sems.at[piece]))
        copies[-1].start()
    for copy in copies:
        copy.wait()


def make_table(own, other):
    had = jnp.asarray(hadamard_np(BASE), jnp.bfloat16)
    return pl.pallas_call(
        table_kernel,
        out_shape=pltpu.HBM((TABLE, LANES), jnp.float32),
        in_specs=[VMEM] * 3,
        out_specs=HBM,
        scratch_shapes=[
            pltpu.VMEM((FOLDS, SOURCES * PART, BASE), jnp.float32),
            pltpu.VMEM((TABLE, LANES), jnp.float32),
            pltpu.SemaphoreType.DMA((PIECES,)),
        ],
        compiler_params=pltpu.CompilerParams(vmem_limit_bytes=24 * 2**20),
        cost_estimate=pl.CostEstimate(flops=10**9, bytes_accessed=10 * 2**20, transcendentals=0),
        name="local_transform",
    )(own, other, had)


def pick_kernel(
    me_ref, slots_ref, spread_ref, reduce_ref, table_hbm, out_ref, table, where_vmem, where_smem, signs, pairs, wide, sems
):
    table_copy = pltpu.make_async_copy(table_hbm, table, sems.at[0])
    table_copy.start()
    me = me_ref[0]
    core = me & 1
    lane = lax.broadcasted_iota(jnp.int32, (DEVS // 2, LANES), 1)
    even, odd = slots_ref[pl.ds(0, DEVS // 2, stride=2), :], slots_ref[pl.ds(1, DEVS // 2, stride=2), :]
    first = lane < CAP
    picks = jnp.where(first, even, pltpu.roll(odd, CAP, 1))
    owner = jnp.where(first, pltpu.roll(even, CAP, 1), odd)
    place = 2 * lax.broadcasted_iota(jnp.int32, (DEVS // 2, LANES), 0) + jnp.where(first, 0, 1)
    device = (place & 63) * 8 + (place >> 6)
    odd_bits = device & me
    for shift in (8, 4, 2, 1):
        odd_bits = odd_bits ^ (odd_bits >> shift)
    mine = (owner >= 0) & (((owner >> 5) & 1) == core)
    bf16 = lambda v: v.astype(jnp.float32).astype(jnp.bfloat16)
    combo = (device & 1) * 2 + ((device >> 1) & 1)
    fold = combo * FOLDS + (picks >> 8) + 1
    pairs[0] = bf16(jnp.where(mine, owner >> 7, -1))
    pairs[1] = bf16(((owner >> 6) & 1) * 32 + (owner & 31))
    pairs[2] = bf16(picks & (BASE - 1))
    pairs[3] = bf16(jnp.where((odd_bits & 1) == 1, -fold, fold))
    high_at = bf16(lax.broadcasted_iota(jnp.int32, (128, LANES), 0))
    low_at = bf16(lax.broadcasted_iota(jnp.int32, (64, LANES), 0))
    one, zero = jnp.ones((), jnp.bfloat16), jnp.zeros((), jnp.bfloat16)
    step = 16

    def invert(block, total):
        rows = pl.ds(pl.multiple_of(block * step, step), step)
        high, low, base, fold = (pairs[i, rows, :] for i in range(4))
        lhs, rhs = [], []
        for i in range(step):
            at = lambda v: v[i : i + 1, :]
            lhs.append(jnp.where(at(high) == high_at, one, zero))
            hit = at(low) == low_at
            rhs.append(jnp.concatenate([jnp.where(hit, at(v), zero) for v in (base, fold)], axis=0))
        return total + lax.dot_general(
            jnp.concatenate(lhs, axis=1),
            jnp.concatenate(rhs, axis=1),
            NT,
            preferred_element_type=jnp.float32,
        )

    total = lax.fori_loop(0, DEVS // 2 // step, invert, jnp.zeros((128, 128), jnp.float32), unroll=4)
    base, fold = total[:, :64].astype(jnp.int32), total[:, 64:].astype(jnp.int32)
    place = jnp.abs(fold) - 1
    sub = lax.broadcasted_iota(jnp.int32, (128, 64), 1) // 8
    where_vmem[...] = (place & (FOLDS - 1)) * BASE + base + PAD - sub
    where_copies = []
    for piece in range(PIECES):
        rows = pl.ds(piece * (128 // PIECES), 128 // PIECES)
        where_copies.append(
            pltpu.make_async_copy(where_vmem.at[rows, :], where_smem.at[rows, :], sems.at[1 + piece])
        )
        where_copies[-1].start()
    combo = (place >> 5) + 1
    signed = bf16(jnp.where(fold < 0, -combo, combo))
    for i in range(8):
        spread = jnp.dot(signed, spread_ref[:, i * WIDE : (i + 1) * WIDE], preferred_element_type=jnp.float32)
        for pair in range(4):
            signs[pair, pl.ds(i, 128, stride=8), :] = spread[:, pair * LANES : (pair + 1) * LANES]
    table_copy.wait()
    lane = lax.broadcasted_iota(jnp.int32, (8, LANES), 1)
    slot_of = lax.broadcasted_iota(jnp.int32, (8, LANES), 0) * 2 + lane // GROUP
    match = (lane % GROUP // PART + 1).astype(jnp.float32)

    def gather(block, _):
        rows = pl.ds(pl.multiple_of(block * 8, 8), 8)
        for pair in range(4):
            parts = [
                table[pl.ds(where_smem[block, k // 2 * 8 + 2 * pair + k % 2], 8), :]
                for k in range(16)
            ]
            value = parts[0]
            for k in range(1, 16):
                value = jnp.where(slot_of == k, parts[k], value)
            lanes = pl.ds(pair * LANES, LANES)
            sign = signs[pair, rows, :]
            wide[rows, lanes] = jnp.where(sign == match, value, jnp.where(sign == -match, -value, 0.0))
        return 0

    for piece in range(PIECES):
        where_copies[piece].wait()
        blocks = OUT_ROWS // 8 // PIECES
        lax.fori_loop(piece * blocks, (piece + 1) * blocks, gather, 0, unroll=2)
    block = wide[...]
    high = block.astype(jnp.bfloat16)
    low = (block - high.astype(jnp.float32)).astype(jnp.bfloat16)
    out_ref[...] = jnp.dot(high, reduce_ref[...], preferred_element_type=jnp.float32) + jnp.dot(
        low, reduce_ref[...], preferred_element_type=jnp.float32
    )


def spread_np():
    column = np.arange(8 * WIDE)
    return (np.arange(64)[:, None] == (column // WIDE * 8 + column % WIDE // GROUP)[None, :]).astype(np.float32)


def reduce_np():
    row = np.arange(WIDE)
    return SCALE * ((row // GROUP * PART + row % PART)[:, None] == np.arange(LANES)[None, :]).astype(np.float32)


def pick_columns(me, slots, table):
    return pl.pallas_call(
        pick_kernel,
        out_shape=jax.ShapeDtypeStruct((OUT_ROWS, LANES), jnp.float32),
        in_specs=[SMEM, VMEM, VMEM, VMEM, HBM],
        out_specs=VMEM,
        scratch_shapes=[
            pltpu.VMEM((TABLE, LANES), jnp.float32),
            pltpu.VMEM((128, 64), jnp.int32),
            pltpu.SMEM((128, 64), jnp.int32),
            pltpu.VMEM((4, OUT_ROWS, LANES), jnp.float32),
            pltpu.VMEM((4, DEVS // 2, LANES), jnp.bfloat16),
            pltpu.VMEM((OUT_ROWS, WIDE), jnp.float32),
            pltpu.SemaphoreType.DMA((1 + PIECES,)),
        ],
        compiler_params=pltpu.CompilerParams(vmem_limit_bytes=24 * 2**20),
        cost_estimate=pl.CostEstimate(flops=2 * 10**9, bytes_accessed=10 * 2**20, transcendentals=0),
        name="pick_columns",
    )(
        me,
        slots,
        jnp.asarray(spread_np(), jnp.bfloat16),
        jnp.asarray(reduce_np(), jnp.bfloat16),
        pltpu.with_memory_space_constraint(table, pltpu.HBM),
    )


def finish_kernel(parts_ref, chosen_ref, out_ref):
    total = parts_ref[pl.ds(0, 8), :]
    for block in range(1, OUT_ROWS // 8):
        total += parts_ref[pl.ds(block * 8, 8), :]
    group = lax.broadcasted_iota(jnp.int32, (8, LANES), 1) // PART == lax.broadcasted_iota(jnp.int32, (8, LANES), 0)
    spread = [jnp.where(group, jnp.broadcast_to(total[i : i + 1], (8, LANES)), 0.0) for i in range(8)]
    out = lax.dot_general(
        chosen_ref[...],
        jnp.concatenate(spread, axis=0),
        NT,
        precision=lax.Precision.HIGHEST,
        preferred_element_type=jnp.float32,
    )
    out_ref[pl.ds(0, PART), :] = out[:, :PANEL]
    out_ref[pl.ds(PART, PART), :] = out[:, PANEL:]


def finish(parts):
    chosen = (np.arange(PART)[:, None] == np.arange(LANES)[None, :] % PART).astype(np.float32)
    return pl.pallas_call(
        finish_kernel,
        out_shape=jax.ShapeDtypeStruct((PANEL, PANEL), jnp.float32),
        in_specs=[VMEM, VMEM],
        out_specs=VMEM,
        compiler_params=pltpu.CompilerParams(vmem_limit_bytes=4 * 2**20),
        cost_estimate=pl.CostEstimate(flops=10**6, bytes_accessed=2**19, transcendentals=0),
        name="finish",
    )(parts, jnp.asarray(chosen))


def prepare_kernel(side_ref, panel_hbm, sign_hbm, rows_ref, owner_ref, send_ref, own_ref, slots_ref, panel, sign, sems):
    side = side_ref[0]
    half = lambda at: panel_hbm.at[pl.ds(pl.multiple_of(at * PART, PART), PART), :]
    copies = [
        pltpu.make_async_copy(source, target, sems.at[i])
        for i, (source, target) in enumerate(
            (
                (sign_hbm, sign),
                (half(1 - side), panel.at[0]),
                (half(side), panel.at[1]),
            )
        )
    ]
    for copy in copies:
        copy.start()
    copies[0].wait()
    for at, out_ref in enumerate((send_ref, own_ref)):
        copies[1 + at].wait()
        for block in range(ROWS_DEV // LANES):
            lanes = pl.ds(block * LANES, LANES)
            factor = (1 - 2 * sign[pl.ds(block, 1), :]).astype(jnp.float32)
            out_ref[:, lanes] = panel[at, :, lanes] * factor
    slots = jnp.concatenate([rows_ref[...], owner_ref[...]], axis=1)
    slots_ref[...] = jnp.broadcast_to(slots, (64, LANES))


def prepare(side, hidden_panel, sign_bits, pick_rows, pick_owner):
    half = jax.ShapeDtypeStruct((PART, ROWS_DEV), jnp.float32)
    return pl.pallas_call(
        prepare_kernel,
        out_shape=(half, half, jax.ShapeDtypeStruct((64, LANES), jnp.int32)),
        in_specs=[SMEM, HBM, HBM, VMEM, VMEM],
        out_specs=(VMEM, VMEM, VMEM),
        scratch_shapes=[
            pltpu.VMEM((2, PART, ROWS_DEV), jnp.float32),
            pltpu.VMEM((ROWS_DEV // LANES, LANES), jnp.int32),
            pltpu.SemaphoreType.DMA((3,)),
        ],
        compiler_params=pltpu.CompilerParams(vmem_limit_bytes=8 * 2**20),
        cost_estimate=pl.CostEstimate(flops=10**6, bytes_accessed=2**21, transcendentals=0),
        name="prepare",
    )(
        side,
        pltpu.with_memory_space_constraint(hidden_panel, pltpu.HBM),
        pltpu.with_memory_space_constraint(sign_bits.reshape(ROWS_DEV // LANES, LANES), pltpu.HBM),
        pick_rows.reshape(1, CAP),
        pick_owner.reshape(1, CAP),
    )


def local(hidden_panel, sign_bits, pick_rows, pick_owner):
    me = ((lax.axis_index("gx") * 8 + lax.axis_index("gy")) * 4 + lax.axis_index("x")) * 2 + lax.axis_index("core")
    side = (lax.axis_index("x") % 2).reshape(1).astype(jnp.int32)
    send, own, slots = prepare(side, hidden_panel, sign_bits, pick_rows, pick_owner)
    near = lax.ppermute(send, "x", [(i, i ^ 1) for i in range(4)])
    first_slots = lax.all_to_all(
        slots.reshape(64, 1, LANES), ("gx", "gy"), split_axis=0, concat_axis=0, tiled=True
    )
    slots = jnp.broadcast_to(first_slots.reshape(1, 64, LANES), (8, 64, LANES))
    slots = lax.all_to_all(slots, ("x", "core"), split_axis=0, concat_axis=0, tiled=True)
    slots = slots.reshape(DEVS, LANES)
    own = join(own, near, first_slots)
    table = make_table(own, lax.ppermute(own, "core", [(0, 1), (1, 0)]))
    columns = pick_columns(me.reshape(1).astype(jnp.int32), slots, table)
    columns = lax.all_to_all(
        columns.reshape(CHIPS, 4, LANES), ("gx", "gy", "x"), split_axis=0, concat_axis=0, tiled=True
    )
    return finish(columns.reshape(OUT_ROWS, LANES))


def solution(mesh):
    inner = Mesh(mesh.devices.reshape(8, 8, 4, 2), ("gx", "gy", "x", "core"))
    rows = ("gx", "gy", "x", "core")
    return jax.shard_map(
        local,
        mesh=inner,
        in_specs=(P(None, rows), P(rows), P(rows), P(rows)),
        out_specs=P(None, rows),
        check_vma=False,
    )
```

```python
import jax
import jax.numpy as jnp
import numpy as np
from jax import lax
from jax.experimental import pallas as pl
from jax.experimental.pallas import tpu as pltpu
from jax.sharding import Mesh, PartitionSpec as P

PANEL = 32
ROWS_DEV = 8192
CAP = 64
DEVS = 512
PART = PANEL // 2
SOURCES = 4
BASE = 256
FOLDS = ROWS_DEV // BASE
PAD = 8
TABLE = ROWS_DEV + 2 * PAD
LANES = 128
CHIPS = 256
OUT_ROWS = 4 * CHIPS
GROUPED = 4
GROUP = 64
PIECES = 4
SCALE = 2.0**-11
NT = (((1,), (1,)), ((), ()))
VMEM, SMEM, HBM = (pl.BlockSpec(memory_space=m) for m in (pltpu.VMEM, pltpu.SMEM, pltpu.HBM))


def hadamard_np(order):
    matrix = np.ones((1, 1), np.float32)
    while matrix.shape[0] < order:
        matrix = np.block([[matrix, matrix], [matrix, -matrix]])
    return matrix


def butterflies(parts):
    half = 1
    while half < len(parts):
        for start in range(0, len(parts), 2 * half):
            for i in range(start, start + half):
                low, high = parts[i], parts[i + half]
                parts[i], parts[i + half] = low + high, low - high
        half *= 2
    return parts


def join_kernel(own_ref, near_ref, slots_ref, out_ref, spread_ref):
    for i in range(8):
        spread_ref[i] = slots_ref[...]
    out_ref[0] = own_ref[...]
    out_ref[1] = near_ref[...]


def join(own, near, slots):
    return pl.pallas_call(
        join_kernel,
        out_shape=(
            jax.ShapeDtypeStruct((2, PART, ROWS_DEV), jnp.float32),
            jax.ShapeDtypeStruct((8, 64, LANES), jnp.int32),
        ),
        in_specs=[VMEM, VMEM, VMEM],
        out_specs=(VMEM, VMEM),
        compiler_params=pltpu.CompilerParams(vmem_limit_bytes=8 * 2**20),
        cost_estimate=pl.CostEstimate(flops=0, bytes_accessed=2**21, transcendentals=0),
        name="join_halves",
    )(own, near, slots)


def table_kernel(own_ref, other_ref, had_ref, table_hbm, mixed, table, sems):
    for source, (ref, chip) in enumerate((ref, chip) for ref in (own_ref, other_ref) for chip in range(2)):
        def fold_rows(step, _, ref=ref, chip=chip, source=source):
            group, half = step // 2, step % 2
            rows = pl.ds(pl.multiple_of(group * 8, 8), 8)
            column = half * LANES
            parts = [ref[chip, rows, pl.ds(pl.multiple_of(fold * BASE + column, LANES), LANES)] for fold in range(FOLDS)]
            out_rows = pl.ds(pl.multiple_of(source * PART + group * 8, 8), 8)
            for fold, part in enumerate(butterflies(parts)):
                mixed[fold, out_rows, pl.ds(pl.multiple_of(column, LANES), LANES)] = part
            return 0

        lax.fori_loop(0, PART // 8 * 2, fold_rows, 0)

    edge = jnp.zeros((PAD, LANES), jnp.float32)
    table[pl.ds(0, PAD), :] = edge
    table[pl.ds(TABLE - PAD, PAD), :] = edge

    def transform(pair, _):
        highs, lows = [], []
        for i in range(2):
            fold = 2 * pair + i
            block = jnp.concatenate(
                butterflies([mixed[fold, pl.ds(source * PART, PART), :] for source in range(SOURCES)]), axis=0
            )
            high = block.astype(jnp.bfloat16)
            low = (block - high.astype(jnp.float32)).astype(jnp.bfloat16)
            highs += [high, high]
            lows += [low, low]
        out = jnp.zeros((BASE, 2 * LANES), jnp.float32)
        for pieces in (highs, lows):
            out += lax.dot_general(
                had_ref[...], jnp.concatenate(pieces, axis=0), NT, preferred_element_type=jnp.float32
            )
        for i in range(2):
            at = pl.multiple_of((2 * pair + i) * BASE + PAD, 8)
            table[pl.ds(at, BASE), :] = out[:, i * LANES : (i + 1) * LANES]
        return 0

    copies = []
    for piece in range(PIECES):
        lax.fori_loop(piece * FOLDS // 2 // PIECES, (piece + 1) * FOLDS // 2 // PIECES, transform, 0, unroll=2)
        start = piece * (ROWS_DEV // PIECES)
        end = TABLE if piece == PIECES - 1 else start + ROWS_DEV // PIECES
        rows = pl.ds(start, end - start)
        copies.append(pltpu.make_async_copy(table.at[rows, :], table_hbm.at[rows, :], sems.at[piece]))
        copies[-1].start()
    for copy in copies:
        copy.wait()


def make_table(own, other):
    had = jnp.asarray(hadamard_np(BASE), jnp.bfloat16)
    return pl.pallas_call(
        table_kernel,
        out_shape=pltpu.HBM((TABLE, LANES), jnp.float32),
        in_specs=[VMEM] * 3,
        out_specs=HBM,
        scratch_shapes=[
            pltpu.VMEM((FOLDS, SOURCES * PART, BASE), jnp.float32),
            pltpu.VMEM((TABLE, LANES), jnp.float32),
            pltpu.SemaphoreType.DMA((PIECES,)),
        ],
        compiler_params=pltpu.CompilerParams(vmem_limit_bytes=24 * 2**20),
        cost_estimate=pl.CostEstimate(flops=10**9, bytes_accessed=10 * 2**20, transcendentals=0),
        name="local_transform",
    )(own, other, had)


def pick_kernel(
    me_ref, slots_ref, spread_ref, table_hbm, out_ref, table, where_vmem, signed, wide, pairs, sems, *where_smem
):
    table_copy = pltpu.make_async_copy(table_hbm, table, sems.at[0])
    table_copy.start()
    me = me_ref[0]
    core = me & 1
    lane = lax.broadcasted_iota(jnp.int32, (DEVS // 2, LANES), 1)
    even, odd = slots_ref[pl.ds(0, DEVS // 2, stride=2), :], slots_ref[pl.ds(1, DEVS // 2, stride=2), :]
    first = lane < CAP
    picks = jnp.where(first, even, pltpu.roll(odd, CAP, 1))
    owner = jnp.where(first, pltpu.roll(even, CAP, 1), odd)
    place = 2 * lax.broadcasted_iota(jnp.int32, (DEVS // 2, LANES), 0) + jnp.where(first, 0, 1)
    device = (place & 63) * 8 + (place >> 6)
    odd_bits = device & me
    for shift in (8, 4, 2, 1):
        odd_bits = odd_bits ^ (odd_bits >> shift)
    mine = (owner >= 0) & (((owner >> 5) & 1) == core)
    bf16 = lambda v: v.astype(jnp.float32).astype(jnp.bfloat16)
    combo = (device & 1) * 2 + ((device >> 1) & 1)
    fold = combo * FOLDS + (picks >> 8) + 1
    pairs[0] = bf16(jnp.where(mine, owner >> 7, -1))
    pairs[1] = bf16((owner & 7) * 8 + ((owner >> 6) & 1) * 4 + ((owner >> 3) & 3))
    pairs[2] = bf16(picks & (BASE - 1))
    pairs[3] = bf16(jnp.where((odd_bits & 1) == 1, -fold, fold))
    high_at = bf16(lax.broadcasted_iota(jnp.int32, (128, LANES), 0))
    low_at = bf16(lax.broadcasted_iota(jnp.int32, (64, LANES), 0))
    one, zero = jnp.ones((), jnp.bfloat16), jnp.zeros((), jnp.bfloat16)
    step = 16

    def invert(block, total):
        rows = pl.ds(pl.multiple_of(block * step, step), step)
        high, low, base, fold = (pairs[i, rows, :] for i in range(4))
        lhs, rhs = [], []
        for i in range(step):
            at = lambda v: v[i : i + 1, :]
            lhs.append(jnp.where(at(high) == high_at, one, zero))
            hit = at(low) == low_at
            rhs.append(jnp.concatenate([jnp.where(hit, at(v), zero) for v in (base, fold)], axis=0))
        return total + lax.dot_general(
            jnp.concatenate(rhs, axis=1),
            jnp.concatenate(lhs, axis=1),
            NT,
            preferred_element_type=jnp.float32,
        )

    total = lax.fori_loop(0, DEVS // 2 // step, invert, jnp.zeros((128, 128), jnp.float32), unroll=4)
    base, fold = total[:64].astype(jnp.int32), total[64:].astype(jnp.int32)
    place = jnp.abs(fold) - 1
    sub = lax.broadcasted_iota(jnp.int32, (64, 128), 0) % 8
    where_vmem[...] = (place & (FOLDS - 1)) * BASE + base + PAD - sub
    where_copies = [
        pltpu.make_async_copy(where_vmem.at[pl.ds(g * 8, 8), :], where_smem[g], sems.at[1 + g]) for g in range(8)
    ]
    for copy in where_copies:
        copy.start()
    combo = bf16(jnp.where(fold < 0, -1 - (place >> 5), 1 + (place >> 5)).T)
    for i in range(8):
        signed[pl.ds(i, 128, stride=8), :] = jnp.dot(
            combo, spread_ref[:, i * LANES : (i + 1) * LANES], preferred_element_type=jnp.float32
        )
    lane = lax.broadcasted_iota(jnp.int32, (8, LANES), 1)
    slot_of = lax.broadcasted_iota(jnp.int32, (8, LANES), 0) * 2 + lane // GROUP
    row_of = lane // PART
    lane_of = row_of % 2 * GROUP + lane % PART - PART
    turn = lambda v, index: jnp.take_along_axis(v, index, axis=1, mode="promise_in_bounds")
    table_copy.wait()
    for copy in where_copies:
        copy.wait()

    def gather(block):
        rows = pl.ds(pl.multiple_of(block * 8, 8), 8)
        for pair in range(4):
            parts = [table[pl.ds(where_smem[2 * pair + k % 2][k // 2, block], 8), :] for k in range(16)]
            value = parts[0]
            for k in range(1, 16):
                value = jnp.where(slot_of == k, parts[k], value)
            wide[rows, pl.ds(pair * LANES, LANES)] = value

    def choose(block):
        rows = pl.ds(pl.multiple_of(block * 8, 8), 8)
        combo = signed[rows, :]
        index = lane_of + PART * jnp.abs(combo).astype(jnp.int32)
        out = turn(wide[rows, pl.ds(0, LANES)], index)
        for pair in range(1, 4):
            out = jnp.where(row_of // 2 == pair, turn(wide[rows, pl.ds(pair * LANES, LANES)], index), out)
        out_ref[rows, :] = out * jnp.where(combo < 0, -SCALE, SCALE)

    def both(group, _):
        for i in range(GROUPED):
            choose((group - 1) * GROUPED + i)
        for i in range(GROUPED):
            gather(group * GROUPED + i)
        return 0

    groups = OUT_ROWS // 8 // GROUPED
    for i in range(GROUPED):
        gather(i)
    lax.fori_loop(1, groups, both, 0)
    for i in range(GROUPED):
        choose((groups - 1) * GROUPED + i)


def spread_np():
    column = np.arange(8 * LANES)
    return (np.arange(64)[:, None] == (column % LANES // PART * 8 + column // LANES)[None, :]).astype(np.float32)


def pick_columns(me, slots, table):
    return pl.pallas_call(
        pick_kernel,
        out_shape=jax.ShapeDtypeStruct((OUT_ROWS, LANES), jnp.float32),
        in_specs=[SMEM, VMEM, VMEM, HBM],
        out_specs=VMEM,
        scratch_shapes=[
            pltpu.VMEM((TABLE, LANES), jnp.float32),
            pltpu.VMEM((64, 128), jnp.int32),
            pltpu.VMEM((OUT_ROWS, LANES), jnp.float32),
            pltpu.VMEM((OUT_ROWS, 4 * LANES), jnp.float32),
            pltpu.VMEM((4, DEVS // 2, LANES), jnp.bfloat16),
            pltpu.SemaphoreType.DMA((9,)),
            *[pltpu.SMEM((8, 128), jnp.int32)] * 8,
        ],
        compiler_params=pltpu.CompilerParams(vmem_limit_bytes=24 * 2**20),
        cost_estimate=pl.CostEstimate(flops=2 * 10**9, bytes_accessed=10 * 2**20, transcendentals=0),
        name="pick_columns",
    )(
        me,
        slots,
        jnp.asarray(spread_np(), jnp.bfloat16),
        pltpu.with_memory_space_constraint(table, pltpu.HBM),
    )


def finish_kernel(parts_ref, chosen_ref, out_ref):
    total = parts_ref[pl.ds(0, 8), :]
    for block in range(1, OUT_ROWS // 8):
        total += parts_ref[pl.ds(block * 8, 8), :]
    group = lax.broadcasted_iota(jnp.int32, (8, LANES), 1) // PART == lax.broadcasted_iota(jnp.int32, (8, LANES), 0)
    spread = [jnp.where(group, jnp.broadcast_to(total[i : i + 1], (8, LANES)), 0.0) for i in range(8)]
    out = lax.dot_general(
        chosen_ref[...],
        jnp.concatenate(spread, axis=0),
        NT,
        precision=lax.Precision.HIGHEST,
        preferred_element_type=jnp.float32,
    )
    out_ref[pl.ds(0, PART), :] = out[:, :PANEL]
    out_ref[pl.ds(PART, PART), :] = out[:, PANEL:]


def finish(parts):
    chosen = (np.arange(PART)[:, None] == np.arange(LANES)[None, :] % PART).astype(np.float32)
    return pl.pallas_call(
        finish_kernel,
        out_shape=jax.ShapeDtypeStruct((PANEL, PANEL), jnp.float32),
        in_specs=[VMEM, VMEM],
        out_specs=VMEM,
        compiler_params=pltpu.CompilerParams(vmem_limit_bytes=4 * 2**20),
        cost_estimate=pl.CostEstimate(flops=10**6, bytes_accessed=2**19, transcendentals=0),
        name="finish",
    )(parts, jnp.asarray(chosen))


def prepare_kernel(side_ref, panel_hbm, sign_hbm, send_ref, own_ref, panel, sign, sems):
    side = side_ref[0]
    half = lambda at: panel_hbm.at[pl.ds(pl.multiple_of(at * PART, PART), PART), :]
    copies = [
        pltpu.make_async_copy(source, target, sems.at[i])
        for i, (source, target) in enumerate(
            (
                (sign_hbm, sign),
                (half(1 - side), panel.at[0]),
                (half(side), panel.at[1]),
            )
        )
    ]
    for copy in copies:
        copy.start()
    copies[0].wait()
    for at, out_ref in enumerate((send_ref, own_ref)):
        copies[1 + at].wait()
        for block in range(ROWS_DEV // LANES):
            lanes = pl.ds(block * LANES, LANES)
            factor = (1 - 2 * sign[pl.ds(block, 1), :]).astype(jnp.float32)
            out_ref[:, lanes] = panel[at, :, lanes] * factor


def prepare(side, hidden_panel, sign_bits):
    half = jax.ShapeDtypeStruct((PART, ROWS_DEV), jnp.float32)
    return pl.pallas_call(
        prepare_kernel,
        out_shape=(half, half),
        in_specs=[SMEM, HBM, HBM],
        out_specs=(VMEM, VMEM),
        scratch_shapes=[
            pltpu.VMEM((2, PART, ROWS_DEV), jnp.float32),
            pltpu.VMEM((ROWS_DEV // LANES, LANES), jnp.int32),
            pltpu.SemaphoreType.DMA((3,)),
        ],
        compiler_params=pltpu.CompilerParams(vmem_limit_bytes=8 * 2**20),
        cost_estimate=pl.CostEstimate(flops=10**6, bytes_accessed=2**21, transcendentals=0),
        name="prepare",
    )(
        side,
        pltpu.with_memory_space_constraint(hidden_panel, pltpu.HBM),
        pltpu.with_memory_space_constraint(sign_bits.reshape(ROWS_DEV // LANES, LANES), pltpu.HBM),
    )


def local(hidden_panel, sign_bits, pick_rows, pick_owner):
    me = ((lax.axis_index("gx") * 8 + lax.axis_index("gy")) * 4 + lax.axis_index("x")) * 2 + lax.axis_index("core")
    side = (lax.axis_index("x") % 2).reshape(1).astype(jnp.int32)
    slots = jnp.concatenate([pick_rows, pick_owner])
    send, own = prepare(side, hidden_panel, sign_bits)
    near = lax.ppermute(send, "x", [(i, i ^ 1) for i in range(4)])
    first_slots = lax.all_to_all(
        jnp.broadcast_to(slots, (64, 1, LANES)), ("gx", "gy"), split_axis=0, concat_axis=0, tiled=True
    )
    own, slots = join(own, near, first_slots.reshape(64, LANES))
    slots = lax.all_to_all(slots, ("x", "core"), split_axis=0, concat_axis=0, tiled=True)
    slots = slots.reshape(DEVS, LANES)
    table = make_table(own, lax.ppermute(own, "core", [(0, 1), (1, 0)]))
    columns = pick_columns(me.reshape(1).astype(jnp.int32), slots, table)
    columns = lax.all_to_all(
        columns.reshape(CHIPS, 4, LANES), ("gx", "gy", "x"), split_axis=0, concat_axis=0, tiled=True
    )
    return finish(columns.reshape(OUT_ROWS, LANES))


def solution(mesh):
    inner = Mesh(mesh.devices.reshape(8, 8, 4, 2), ("gx", "gy", "x", "core"))
    rows = ("gx", "gy", "x", "core")
    return jax.shard_map(
        local,
        mesh=inner,
        in_specs=(P(None, rows), P(rows), P(rows), P(rows)),
        out_specs=P(None, rows),
        check_vma=False,
    )
```

```python
import jax
import jax.numpy as jnp
import numpy as np
from jax import lax
from jax.experimental import pallas as pl
from jax.experimental.pallas import tpu as pltpu
from jax.sharding import Mesh, PartitionSpec as P

PANEL = 32
ROWS_DEV = 8192
CAP = 64
DEVS = 512
PART = PANEL // 2
SOURCES = 4
BASE = 256
FOLDS = ROWS_DEV // BASE
PAD = 8
TABLE = ROWS_DEV + 2 * PAD
LANES = 128
CHIPS = 256
OUT_ROWS = 4 * CHIPS
GROUPED = 4
GROUP = 64
PIECES = 8
SCALE = 2.0**-11
NT = (((1,), (1,)), ((), ()))
VMEM, SMEM, HBM = (pl.BlockSpec(memory_space=m) for m in (pltpu.VMEM, pltpu.SMEM, pltpu.HBM))


def hadamard_np(order):
    matrix = np.ones((1, 1), np.float32)
    while matrix.shape[0] < order:
        matrix = np.block([[matrix, matrix], [matrix, -matrix]])
    return matrix


def butterflies(parts):
    half = 1
    while half < len(parts):
        for start in range(0, len(parts), 2 * half):
            for i in range(start, start + half):
                low, high = parts[i], parts[i + half]
                parts[i], parts[i + half] = low + high, low - high
        half *= 2
    return parts


def join_kernel(own_ref, near_ref, slots_ref, out_ref):
    out_ref[0] = own_ref[...]
    out_ref[1] = near_ref[...]


def join(own, near, slots):
    return pl.pallas_call(
        join_kernel,
        out_shape=jax.ShapeDtypeStruct((2, PART, ROWS_DEV), jnp.float32),
        in_specs=[VMEM, VMEM, HBM],
        out_specs=VMEM,
        compiler_params=pltpu.CompilerParams(vmem_limit_bytes=8 * 2**20),
        cost_estimate=pl.CostEstimate(flops=0, bytes_accessed=2**21, transcendentals=0),
        name="join_halves",
    )(own, near, slots)


def table_rows(piece):
    start = piece * (ROWS_DEV // PIECES)
    end = TABLE if piece == PIECES - 1 else start + ROWS_DEV // PIECES
    return pl.ds(start, end - start)


def table_kernel(own_ref, other_ref, had_hbm, table_hbm, mixed, table, had_ref, sems):
    had_copy = pltpu.make_async_copy(had_hbm, had_ref, sems.at[PIECES])
    had_copy.start()
    for source, (ref, chip) in enumerate((ref, chip) for ref in (own_ref, other_ref) for chip in range(2)):
        def fold_rows(step, _, ref=ref, chip=chip, source=source):
            group, half = step // 2, step % 2
            rows = pl.ds(pl.multiple_of(group * 8, 8), 8)
            column = half * LANES
            parts = [ref[chip, rows, pl.ds(pl.multiple_of(fold * BASE + column, LANES), LANES)] for fold in range(FOLDS)]
            out_rows = pl.ds(pl.multiple_of(source * PART + group * 8, 8), 8)
            for fold, part in enumerate(butterflies(parts)):
                mixed[fold, out_rows, pl.ds(pl.multiple_of(column, LANES), LANES)] = part
            return 0

        lax.fori_loop(0, PART // 8 * 2, fold_rows, 0)

    had_copy.wait()
    edge = jnp.zeros((PAD, LANES), jnp.float32)
    table[pl.ds(0, PAD), :] = edge
    table[pl.ds(TABLE - PAD, PAD), :] = edge

    def transform(pair, _):
        highs, lows = [], []
        for i in range(2):
            fold = 2 * pair + i
            block = jnp.concatenate(
                butterflies([mixed[fold, pl.ds(source * PART, PART), :] for source in range(SOURCES)]), axis=0
            )
            high = block.astype(jnp.bfloat16)
            low = (block - high.astype(jnp.float32)).astype(jnp.bfloat16)
            highs += [high, high]
            lows += [low, low]
        out = jnp.zeros((BASE, 2 * LANES), jnp.float32)
        for pieces in (highs, lows):
            out += lax.dot_general(
                had_ref[...], jnp.concatenate(pieces, axis=0), NT, preferred_element_type=jnp.float32
            )
        for i in range(2):
            at = pl.multiple_of((2 * pair + i) * BASE + PAD, 8)
            table[pl.ds(at, BASE), :] = out[:, i * LANES : (i + 1) * LANES]
        return 0

    copies = []
    for piece in range(PIECES):
        lax.fori_loop(piece * FOLDS // 2 // PIECES, (piece + 1) * FOLDS // 2 // PIECES, transform, 0, unroll=2)
        rows = table_rows(piece)
        copies.append(pltpu.make_async_copy(table.at[rows, :], table_hbm.at[rows, :], sems.at[piece]))
        copies[-1].start()
    for copy in copies:
        copy.wait()


def make_table(own, other):
    had = jnp.asarray(hadamard_np(BASE), jnp.bfloat16)
    return pl.pallas_call(
        table_kernel,
        out_shape=pltpu.HBM((TABLE, LANES), jnp.float32),
        in_specs=[VMEM, VMEM, HBM],
        out_specs=HBM,
        scratch_shapes=[
            pltpu.VMEM((FOLDS, SOURCES * PART, BASE), jnp.float32),
            pltpu.VMEM((TABLE, LANES), jnp.float32),
            pltpu.VMEM((BASE, BASE), jnp.bfloat16),
            pltpu.SemaphoreType.DMA((PIECES + 1,)),
        ],
        compiler_params=pltpu.CompilerParams(vmem_limit_bytes=24 * 2**20),
        cost_estimate=pl.CostEstimate(flops=10**9, bytes_accessed=10 * 2**20, transcendentals=0),
        name="local_transform",
    )(own, other, pltpu.with_memory_space_constraint(had, pltpu.HBM))


def invert_kernel(group_ref, slots_ref, out_ref):
    lane = lax.broadcasted_iota(jnp.int32, (32, LANES), 1)
    even, odd = slots_ref[pl.ds(0, 32, stride=2), :], slots_ref[pl.ds(1, 32, stride=2), :]
    first = lane < CAP
    picks = jnp.where(first, even, pltpu.roll(odd, CAP, 1))
    owner = jnp.where(first, pltpu.roll(even, CAP, 1), odd)
    place = 2 * lax.broadcasted_iota(jnp.int32, (32, LANES), 0) + jnp.where(first, 0, 1)
    bf16 = lambda v: v.astype(jnp.float32).astype(jnp.bfloat16)
    high = bf16(jnp.where(owner >= 0, ((owner >> 5) & 1) * 128 + (owner >> 7), -1))
    low = bf16((owner & 7) * 8 + ((owner >> 6) & 1) * 4 + ((owner >> 3) & 3))
    values = bf16(picks & (BASE - 1)), bf16(picks >> 8), bf16(place + 1)
    high_at = bf16(lax.broadcasted_iota(jnp.int32, (256, LANES), 0))
    low_at = bf16(lax.broadcasted_iota(jnp.int32, (64, LANES), 0))
    one, zero = jnp.ones((), jnp.bfloat16), jnp.zeros((), jnp.bfloat16)
    total = jnp.zeros((192, 256), jnp.float32)
    for start in range(0, 32, 16):
        lhs, rhs = [], []
        for i in range(start, start + 16):
            at = lambda v: v[i : i + 1, :]
            rhs.append(jnp.where(at(high) == high_at, one, zero))
            hit = at(low) == low_at
            lhs.append(jnp.concatenate([jnp.where(hit, at(v), zero) for v in values], axis=0))
        total += lax.dot_general(
            jnp.concatenate(lhs, axis=1), jnp.concatenate(rhs, axis=1), NT, preferred_element_type=jnp.float32
        )
    base, fold, place = (total[i * 64 : (i + 1) * 64].astype(jnp.int32) for i in range(3))
    row = ((place - 1) * 8 + group_ref[0]) * ROWS_DEV + fold * BASE + base
    found = jnp.where(place > 0, row + 1, 0)
    for i in range(8):
        out_ref[i] = found[:, i % 2 * LANES : (i % 2 + 1) * LANES]


def invert(group, slots):
    return pl.pallas_call(
        invert_kernel,
        out_shape=jax.ShapeDtypeStruct((8, 64, LANES), jnp.int32),
        in_specs=[SMEM, VMEM],
        out_specs=VMEM,
        compiler_params=pltpu.CompilerParams(vmem_limit_bytes=8 * 2**20),
        cost_estimate=pl.CostEstimate(flops=4 * 10**8, bytes_accessed=2**19, transcendentals=0),
        name="invert_slots",
    )(group, slots)


def pick_kernel(
    me_ref, sources_ref, spread_ref, table_hbm, out_ref, table, where_vmem, signed, wide, sems, *where_smem
):
    table_copies = []
    for piece in range(PIECES):
        rows = table_rows(piece)
        table_copies.append(pltpu.make_async_copy(table_hbm.at[rows, :], table.at[rows, :], sems.at[8 + piece]))
        table_copies[-1].start()
    bf16 = lambda v: v.astype(jnp.float32).astype(jnp.bfloat16)
    source = sources_ref[0]
    for i in range(1, 8):
        source += sources_ref[i]
    source = source - 1
    device = source >> 13
    odd_bits = device & me_ref[0]
    for shift in (8, 4, 2, 1):
        odd_bits = odd_bits ^ (odd_bits >> shift)
    combo = (device & 1) * 2 + ((device >> 1) & 1) + 1
    sub = lax.broadcasted_iota(jnp.int32, (64, 128), 0) % 8
    where_vmem[...] = (source & (ROWS_DEV - 1)) + PAD - sub
    where_copies = [
        pltpu.make_async_copy(where_vmem.at[pl.ds(g * 8, 8), :], where_smem[g], sems.at[g]) for g in range(8)
    ]
    for copy in where_copies:
        copy.start()
    combo = bf16(jnp.where(odd_bits & 1 == 1, -combo, combo).T)
    for i in range(8):
        signed[pl.ds(i, 128, stride=8), :] = jnp.dot(
            combo, spread_ref[:, i * LANES : (i + 1) * LANES], preferred_element_type=jnp.float32
        )
    lane = lax.broadcasted_iota(jnp.int32, (8, LANES), 1)
    slot_of = lax.broadcasted_iota(jnp.int32, (8, LANES), 0) * 2 + lane // GROUP
    row_of = lane // PART
    lane_of = row_of % 2 * GROUP + lane % PART - PART
    turn = lambda v, index: jnp.take_along_axis(v, index, axis=1, mode="promise_in_bounds")
    for copy in table_copies:
        copy.wait()
    for copy in where_copies:
        copy.wait()

    def gather(block):
        rows = pl.ds(pl.multiple_of(block * 8, 8), 8)
        for pair in range(4):
            parts = [table[pl.ds(where_smem[2 * pair + k % 2][k // 2, block], 8), :] for k in range(16)]
            value = parts[0]
            for k in range(1, 16):
                value = jnp.where(slot_of == k, parts[k], value)
            wide[rows, pl.ds(pair * LANES, LANES)] = value

    def choose(block):
        rows = pl.ds(pl.multiple_of(block * 8, 8), 8)
        combo = signed[rows, :]
        index = lane_of + PART * jnp.abs(combo).astype(jnp.int32)
        out = turn(wide[rows, pl.ds(0, LANES)], index)
        for pair in range(1, 4):
            out = jnp.where(row_of // 2 == pair, turn(wide[rows, pl.ds(pair * LANES, LANES)], index), out)
        out_ref[rows, :] = out * jnp.where(combo < 0, -SCALE, SCALE)

    def both(group, _):
        for i in range(GROUPED):
            choose((group - 1) * GROUPED + i)
        for i in range(GROUPED):
            gather(group * GROUPED + i)
        return 0

    groups = OUT_ROWS // 8 // GROUPED
    for i in range(GROUPED):
        gather(i)
    lax.fori_loop(1, groups, both, 0)
    for i in range(GROUPED):
        choose((groups - 1) * GROUPED + i)


def spread_np():
    column = np.arange(8 * LANES)
    return (np.arange(64)[:, None] == (column % LANES // PART * 8 + column // LANES)[None, :]).astype(np.float32)


def pick_columns(me, sources, table):
    return pl.pallas_call(
        pick_kernel,
        out_shape=jax.ShapeDtypeStruct((OUT_ROWS, LANES), jnp.float32),
        in_specs=[SMEM, VMEM, VMEM, HBM],
        out_specs=VMEM,
        scratch_shapes=[
            pltpu.VMEM((TABLE, LANES), jnp.float32),
            pltpu.VMEM((64, 128), jnp.int32),
            pltpu.VMEM((OUT_ROWS, LANES), jnp.float32),
            pltpu.VMEM((OUT_ROWS, 4 * LANES), jnp.float32),
            pltpu.SemaphoreType.DMA((8 + PIECES,)),
            *[pltpu.SMEM((8, 128), jnp.int32)] * 8,
        ],
        compiler_params=pltpu.CompilerParams(vmem_limit_bytes=24 * 2**20),
        cost_estimate=pl.CostEstimate(flops=10**8, bytes_accessed=10 * 2**20, transcendentals=0),
        name="pick_columns",
    )(
        me,
        sources,
        jnp.asarray(spread_np(), jnp.bfloat16),
        pltpu.with_memory_space_constraint(table, pltpu.HBM),
    )


def finish_kernel(parts_ref, chosen_ref, out_ref):
    total = parts_ref[pl.ds(0, 8), :]
    for block in range(1, OUT_ROWS // 8):
        total += parts_ref[pl.ds(block * 8, 8), :]
    group = lax.broadcasted_iota(jnp.int32, (8, LANES), 1) // PART == lax.broadcasted_iota(jnp.int32, (8, LANES), 0)
    spread = [jnp.where(group, jnp.broadcast_to(total[i : i + 1], (8, LANES)), 0.0) for i in range(8)]
    out = lax.dot_general(
        chosen_ref[...],
        jnp.concatenate(spread, axis=0),
        NT,
        precision=lax.Precision.HIGHEST,
        preferred_element_type=jnp.float32,
    )
    out_ref[pl.ds(0, PART), :] = out[:, :PANEL]
    out_ref[pl.ds(PART, PART), :] = out[:, PANEL:]


def finish(parts):
    chosen = (np.arange(PART)[:, None] == np.arange(LANES)[None, :] % PART).astype(np.float32)
    return pl.pallas_call(
        finish_kernel,
        out_shape=jax.ShapeDtypeStruct((PANEL, PANEL), jnp.float32),
        in_specs=[VMEM, VMEM],
        out_specs=VMEM,
        compiler_params=pltpu.CompilerParams(vmem_limit_bytes=4 * 2**20),
        cost_estimate=pl.CostEstimate(flops=10**6, bytes_accessed=2**19, transcendentals=0),
        name="finish",
    )(parts, jnp.asarray(chosen))


def prepare_kernel(side_ref, panel_hbm, sign_hbm, send_ref, own_ref, panel, sign, sems):
    side = side_ref[0]
    half = lambda at: panel_hbm.at[pl.ds(pl.multiple_of(at * PART, PART), PART), :]
    copies = [
        pltpu.make_async_copy(source, target, sems.at[i])
        for i, (source, target) in enumerate(
            (
                (sign_hbm, sign),
                (half(1 - side), panel.at[0]),
                (half(side), panel.at[1]),
            )
        )
    ]
    for copy in copies:
        copy.start()
    copies[0].wait()
    for at, out_ref in enumerate((send_ref, own_ref)):
        copies[1 + at].wait()
        for block in range(ROWS_DEV // LANES):
            lanes = pl.ds(block * LANES, LANES)
            factor = (1 - 2 * sign[pl.ds(block, 1), :]).astype(jnp.float32)
            out_ref[:, lanes] = panel[at, :, lanes] * factor


def prepare(side, hidden_panel, sign_bits):
    half = jax.ShapeDtypeStruct((PART, ROWS_DEV), jnp.float32)
    return pl.pallas_call(
        prepare_kernel,
        out_shape=(half, half),
        in_specs=[SMEM, HBM, HBM],
        out_specs=(VMEM, VMEM),
        scratch_shapes=[
            pltpu.VMEM((2, PART, ROWS_DEV), jnp.float32),
            pltpu.VMEM((ROWS_DEV // LANES, LANES), jnp.int32),
            pltpu.SemaphoreType.DMA((3,)),
        ],
        compiler_params=pltpu.CompilerParams(vmem_limit_bytes=8 * 2**20),
        cost_estimate=pl.CostEstimate(flops=10**6, bytes_accessed=2**21, transcendentals=0),
        name="prepare",
    )(
        side,
        pltpu.with_memory_space_constraint(hidden_panel, pltpu.HBM),
        pltpu.with_memory_space_constraint(sign_bits.reshape(ROWS_DEV // LANES, LANES), pltpu.HBM),
    )


def local(hidden_panel, sign_bits, pick_rows, pick_owner):
    me = ((lax.axis_index("gx") * 8 + lax.axis_index("gy")) * 4 + lax.axis_index("x")) * 2 + lax.axis_index("core")
    side = (lax.axis_index("x") % 2).reshape(1).astype(jnp.int32)
    slots = jnp.concatenate([pick_rows, pick_owner])
    send, own = prepare(side, hidden_panel, sign_bits)
    near = lax.ppermute(send, "x", [(i, i ^ 1) for i in range(4)])
    first_slots = lax.all_to_all(
        jnp.broadcast_to(slots, (64, 1, LANES)), ("gx", "gy"), split_axis=0, concat_axis=0, tiled=True
    )
    own = join(own, near, first_slots)
    sources = invert((me % 8).reshape(1).astype(jnp.int32), first_slots.reshape(64, LANES))
    sources = lax.all_to_all(sources, ("x", "core"), split_axis=0, concat_axis=0, tiled=True)
    table = make_table(own, lax.ppermute(own, "core", [(0, 1), (1, 0)]))
    columns = pick_columns(me.reshape(1).astype(jnp.int32), sources, table)
    columns = lax.all_to_all(
        columns.reshape(CHIPS, 4, LANES), ("gx", "gy", "x"), split_axis=0, concat_axis=0, tiled=True
    )
    return finish(columns.reshape(OUT_ROWS, LANES))


def solution(mesh):
    inner = Mesh(mesh.devices.reshape(8, 8, 4, 2), ("gx", "gy", "x", "core"))
    rows = ("gx", "gy", "x", "core")
    return jax.shard_map(
        local,
        mesh=inner,
        in_specs=(P(None, rows), P(rows), P(rows), P(rows)),
        out_specs=P(None, rows),
        check_vma=False,
    )
```

```python
import jax
import jax.numpy as jnp
import numpy as np
from jax import lax
from jax.experimental import pallas as pl
from jax.experimental.pallas import tpu as pltpu
from jax.sharding import Mesh, PartitionSpec as P

PANEL = 32
ROWS_DEV = 8192
CAP = 64
DEVS = 512
PART = PANEL // 2
SOURCES = 4
BASE = 256
FOLDS = ROWS_DEV // BASE
PAD = 8
TABLE = ROWS_DEV + 2 * PAD
LANES = 128
CHIPS = 256
OUT_ROWS = 4 * CHIPS
GROUPED = 4
GROUP = 64
PIECES = 8
SCALE = 2.0**-11
NT = (((1,), (1,)), ((), ()))
VMEM, SMEM, HBM = (pl.BlockSpec(memory_space=m) for m in (pltpu.VMEM, pltpu.SMEM, pltpu.HBM))


def hadamard_np(order):
    matrix = np.ones((1, 1), np.float32)
    while matrix.shape[0] < order:
        matrix = np.block([[matrix, matrix], [matrix, -matrix]])
    return matrix


def butterflies(parts):
    half = 1
    while half < len(parts):
        for start in range(0, len(parts), 2 * half):
            for i in range(start, start + half):
                low, high = parts[i], parts[i + half]
                parts[i], parts[i + half] = low + high, low - high
        half *= 2
    return parts


def join_kernel(own_ref, near_ref, sources_ref, out_ref):
    out_ref[0] = own_ref[...]
    out_ref[1] = near_ref[...]


def join(own, near, sources):
    return pl.pallas_call(
        join_kernel,
        out_shape=jax.ShapeDtypeStruct((2, PART, ROWS_DEV), jnp.float32),
        in_specs=[VMEM, VMEM, HBM],
        out_specs=VMEM,
        compiler_params=pltpu.CompilerParams(vmem_limit_bytes=8 * 2**20),
        cost_estimate=pl.CostEstimate(flops=0, bytes_accessed=2**21, transcendentals=0),
        name="join_halves",
    )(own, near, sources)


def table_rows(piece):
    start = piece * (ROWS_DEV // PIECES)
    end = TABLE if piece == PIECES - 1 else start + ROWS_DEV // PIECES
    return pl.ds(start, end - start)


def table_kernel(own_ref, other_ref, had_hbm, table_hbm, mixed, table, had_ref, sems):
    had_copy = pltpu.make_async_copy(had_hbm, had_ref, sems.at[PIECES])
    had_copy.start()
    for source, (ref, chip) in enumerate((ref, chip) for ref in (own_ref, other_ref) for chip in range(2)):
        def fold_rows(step, _, ref=ref, chip=chip, source=source):
            group, half = step // 2, step % 2
            rows = pl.ds(pl.multiple_of(group * 8, 8), 8)
            column = half * LANES
            parts = [ref[chip, rows, pl.ds(pl.multiple_of(fold * BASE + column, LANES), LANES)] for fold in range(FOLDS)]
            out_rows = pl.ds(pl.multiple_of(source * PART + group * 8, 8), 8)
            for fold, part in enumerate(butterflies(parts)):
                mixed[fold, out_rows, pl.ds(pl.multiple_of(column, LANES), LANES)] = part
            return 0

        lax.fori_loop(0, PART // 8 * 2, fold_rows, 0)

    had_copy.wait()
    edge = jnp.zeros((PAD, LANES), jnp.float32)
    table[pl.ds(0, PAD), :] = edge
    table[pl.ds(TABLE - PAD, PAD), :] = edge

    def transform(pair, _):
        highs, lows = [], []
        for i in range(2):
            fold = 2 * pair + i
            block = jnp.concatenate(
                butterflies([mixed[fold, pl.ds(source * PART, PART), :] for source in range(SOURCES)]), axis=0
            )
            high = block.astype(jnp.bfloat16)
            low = (block - high.astype(jnp.float32)).astype(jnp.bfloat16)
            highs += [high, high]
            lows += [low, low]
        out = jnp.zeros((BASE, 2 * LANES), jnp.float32)
        for pieces in (highs, lows):
            out += lax.dot_general(
                had_ref[...], jnp.concatenate(pieces, axis=0), NT, preferred_element_type=jnp.float32
            )
        for i in range(2):
            at = pl.multiple_of((2 * pair + i) * BASE + PAD, 8)
            table[pl.ds(at, BASE), :] = out[:, i * LANES : (i + 1) * LANES]
        return 0

    copies = []
    for piece in range(PIECES):
        lax.fori_loop(piece * FOLDS // 2 // PIECES, (piece + 1) * FOLDS // 2 // PIECES, transform, 0, unroll=2)
        rows = table_rows(piece)
        copies.append(pltpu.make_async_copy(table.at[rows, :], table_hbm.at[rows, :], sems.at[piece]))
        copies[-1].start()
    for copy in copies:
        copy.wait()


def make_table(own, other):
    had = jnp.asarray(hadamard_np(BASE), jnp.bfloat16)
    return pl.pallas_call(
        table_kernel,
        out_shape=pltpu.HBM((TABLE, LANES), jnp.float32),
        in_specs=[VMEM, VMEM, HBM],
        out_specs=HBM,
        scratch_shapes=[
            pltpu.VMEM((FOLDS, SOURCES * PART, BASE), jnp.float32),
            pltpu.VMEM((TABLE, LANES), jnp.float32),
            pltpu.VMEM((BASE, BASE), jnp.bfloat16),
            pltpu.SemaphoreType.DMA((PIECES + 1,)),
        ],
        compiler_params=pltpu.CompilerParams(vmem_limit_bytes=24 * 2**20),
        cost_estimate=pl.CostEstimate(flops=10**9, bytes_accessed=10 * 2**20, transcendentals=0),
        name="local_transform",
    )(own, other, pltpu.with_memory_space_constraint(had, pltpu.HBM))


def invert_kernel(group_ref, slots_ref, out_ref):
    lane = lax.broadcasted_iota(jnp.int32, (32, LANES), 1)
    even, odd = slots_ref[pl.ds(0, 32, stride=2), :], slots_ref[pl.ds(1, 32, stride=2), :]
    first = lane < CAP
    picks = jnp.where(first, even, pltpu.roll(odd, CAP, 1))
    owner = jnp.where(first, pltpu.roll(even, CAP, 1), odd)
    place = 2 * lax.broadcasted_iota(jnp.int32, (32, LANES), 0) + jnp.where(first, 0, 1)
    bf16 = lambda v: v.astype(jnp.float32).astype(jnp.bfloat16)
    high = bf16(jnp.where(owner >= 0, ((owner >> 5) & 1) * 128 + (owner >> 7), -1))
    low = bf16((owner & 7) * 8 + ((owner >> 6) & 1) * 4 + ((owner >> 3) & 3))
    values = bf16(picks & (BASE - 1)), bf16(picks >> 8), bf16(place + 1)
    high_at = bf16(lax.broadcasted_iota(jnp.int32, (256, LANES), 0))
    low_at = bf16(lax.broadcasted_iota(jnp.int32, (64, LANES), 0))
    one, zero = jnp.ones((), jnp.bfloat16), jnp.zeros((), jnp.bfloat16)
    total = jnp.zeros((192, 256), jnp.float32)
    for start in range(0, 32, 16):
        lhs, rhs = [], []
        for i in range(start, start + 16):
            at = lambda v: v[i : i + 1, :]
            rhs.append(jnp.where(at(high) == high_at, one, zero))
            hit = at(low) == low_at
            lhs.append(jnp.concatenate([jnp.where(hit, at(v), zero) for v in values], axis=0))
        total += lax.dot_general(
            jnp.concatenate(lhs, axis=1), jnp.concatenate(rhs, axis=1), NT, preferred_element_type=jnp.float32
        )
    base, fold, place = (total[i * 64 : (i + 1) * 64].astype(jnp.int32) for i in range(3))
    row = ((place - 1) * 8 + group_ref[0]) * ROWS_DEV + fold * BASE + base
    found = jnp.where(place > 0, row + 1, 0)
    for i in range(8):
        out_ref[i] = found[:, i % 2 * LANES : (i % 2 + 1) * LANES]


def invert(group, slots):
    return pl.pallas_call(
        invert_kernel,
        out_shape=jax.ShapeDtypeStruct((8, 64, LANES), jnp.int32),
        in_specs=[SMEM, VMEM],
        out_specs=VMEM,
        compiler_params=pltpu.CompilerParams(vmem_limit_bytes=8 * 2**20),
        cost_estimate=pl.CostEstimate(flops=4 * 10**8, bytes_accessed=2**19, transcendentals=0),
        name="invert_slots",
    )(group, slots)


def pick_kernel(
    me_ref, sources_ref, spread_ref, table_hbm, out_ref, table, where_vmem, signed, wide, sems, *where_smem
):
    table_copies = []
    for piece in range(PIECES):
        rows = table_rows(piece)
        table_copies.append(pltpu.make_async_copy(table_hbm.at[rows, :], table.at[rows, :], sems.at[8 + piece]))
        table_copies[-1].start()
    bf16 = lambda v: v.astype(jnp.float32).astype(jnp.bfloat16)
    source = sources_ref[0]
    for i in range(1, 8):
        source += sources_ref[i]
    source = source - 1
    device = source >> 13
    odd_bits = device & me_ref[0]
    for shift in (8, 4, 2, 1):
        odd_bits = odd_bits ^ (odd_bits >> shift)
    combo = (device & 1) * 2 + ((device >> 1) & 1) + 1
    sub = lax.broadcasted_iota(jnp.int32, (64, 128), 0) % 8
    where_vmem[...] = (source & (ROWS_DEV - 1)) + PAD - sub
    where_copies = [
        pltpu.make_async_copy(where_vmem.at[pl.ds(g * 8, 8), :], where_smem[g], sems.at[g]) for g in range(8)
    ]
    for copy in where_copies:
        copy.start()
    combo = bf16(jnp.where(odd_bits & 1 == 1, -combo, combo).T)
    for i in range(8):
        signed[pl.ds(i, 128, stride=8), :] = jnp.dot(
            combo, spread_ref[:, i * LANES : (i + 1) * LANES], preferred_element_type=jnp.float32
        )
    lane = lax.broadcasted_iota(jnp.int32, (8, LANES), 1)
    slot_of = lax.broadcasted_iota(jnp.int32, (8, LANES), 0) * 2 + lane // GROUP
    row_of = lane // PART
    lane_of = row_of % 2 * GROUP + lane % PART - PART
    turn = lambda v, index: jnp.take_along_axis(v, index, axis=1, mode="promise_in_bounds")
    for copy in table_copies:
        copy.wait()
    for copy in where_copies:
        copy.wait()

    def gather(block):
        rows = pl.ds(pl.multiple_of(block * 8, 8), 8)
        for pair in range(4):
            parts = [table[pl.ds(where_smem[2 * pair + k % 2][k // 2, block], 8), :] for k in range(16)]
            value = parts[0]
            for k in range(1, 16):
                value = jnp.where(slot_of == k, parts[k], value)
            wide[rows, pl.ds(pair * LANES, LANES)] = value

    def choose(block):
        rows = pl.ds(pl.multiple_of(block * 8, 8), 8)
        combo = signed[rows, :]
        index = lane_of + PART * jnp.abs(combo).astype(jnp.int32)
        out = turn(wide[rows, pl.ds(0, LANES)], index)
        for pair in range(1, 4):
            out = jnp.where(row_of // 2 == pair, turn(wide[rows, pl.ds(pair * LANES, LANES)], index), out)
        out_ref[rows, :] = out * jnp.where(combo < 0, -SCALE, SCALE)

    def both(group, _):
        for i in range(GROUPED):
            choose((group - 1) * GROUPED + i)
        for i in range(GROUPED):
            gather(group * GROUPED + i)
        return 0

    groups = OUT_ROWS // 8 // GROUPED
    for i in range(GROUPED):
        gather(i)
    lax.fori_loop(1, groups, both, 0)
    for i in range(GROUPED):
        choose((groups - 1) * GROUPED + i)


def spread_np():
    column = np.arange(8 * LANES)
    return (np.arange(64)[:, None] == (column % LANES // PART * 8 + column // LANES)[None, :]).astype(np.float32)


def pick_columns(me, sources, table):
    return pl.pallas_call(
        pick_kernel,
        out_shape=jax.ShapeDtypeStruct((OUT_ROWS, LANES), jnp.float32),
        in_specs=[SMEM, VMEM, VMEM, HBM],
        out_specs=VMEM,
        scratch_shapes=[
            pltpu.VMEM((TABLE, LANES), jnp.float32),
            pltpu.VMEM((64, 128), jnp.int32),
            pltpu.VMEM((OUT_ROWS, LANES), jnp.float32),
            pltpu.VMEM((OUT_ROWS, 4 * LANES), jnp.float32),
            pltpu.SemaphoreType.DMA((8 + PIECES,)),
            *[pltpu.SMEM((8, 128), jnp.int32)] * 8,
        ],
        compiler_params=pltpu.CompilerParams(vmem_limit_bytes=24 * 2**20),
        cost_estimate=pl.CostEstimate(flops=10**8, bytes_accessed=10 * 2**20, transcendentals=0),
        name="pick_columns",
    )(
        me,
        sources,
        jnp.asarray(spread_np(), jnp.bfloat16),
        pltpu.with_memory_space_constraint(table, pltpu.HBM),
    )


def finish_kernel(parts_ref, chosen_ref, out_ref):
    totals = [parts_ref[pl.ds(i * 8, 8), :] for i in range(8)]
    for block in range(8, OUT_ROWS // 8):
        totals[block % 8] += parts_ref[pl.ds(block * 8, 8), :]
    while len(totals) > 1:
        totals = [low + high for low, high in zip(totals[::2], totals[1::2])]
    total = totals[0]
    group = lax.broadcasted_iota(jnp.int32, (8, LANES), 1) // PART == lax.broadcasted_iota(jnp.int32, (8, LANES), 0)
    spread = [jnp.where(group, jnp.broadcast_to(total[i : i + 1], (8, LANES)), 0.0) for i in range(8)]
    out = lax.dot_general(
        chosen_ref[...],
        jnp.concatenate(spread, axis=0),
        NT,
        precision=lax.Precision.HIGHEST,
        preferred_element_type=jnp.float32,
    )
    out_ref[pl.ds(0, PART), :] = out[:, :PANEL]
    out_ref[pl.ds(PART, PART), :] = out[:, PANEL:]


def finish(parts):
    chosen = (np.arange(PART)[:, None] == np.arange(LANES)[None, :] % PART).astype(np.float32)
    return pl.pallas_call(
        finish_kernel,
        out_shape=jax.ShapeDtypeStruct((PANEL, PANEL), jnp.float32),
        in_specs=[VMEM, VMEM],
        out_specs=VMEM,
        compiler_params=pltpu.CompilerParams(vmem_limit_bytes=4 * 2**20),
        cost_estimate=pl.CostEstimate(flops=10**6, bytes_accessed=2**19, transcendentals=0),
        name="finish",
    )(parts, jnp.asarray(chosen))


def prepare_kernel(
    side_ref, panel_hbm, sign_hbm, rows_hbm, owner_hbm, send_ref, own_ref, slots_ref, panel, sign, rows, owner, sems
):
    side = side_ref[0]
    half = lambda at: panel_hbm.at[pl.ds(pl.multiple_of(at * PART, PART), PART), :]
    copies = [
        pltpu.make_async_copy(source, target, sems.at[i])
        for i, (source, target) in enumerate(
            (
                (sign_hbm, sign),
                (half(1 - side), panel.at[0]),
                (half(side), panel.at[1]),
                (rows_hbm, rows),
                (owner_hbm, owner),
            )
        )
    ]
    for copy in copies:
        copy.start()
    copies[0].wait()
    for at, out_ref in enumerate((send_ref, own_ref)):
        copies[1 + at].wait()
        for block in range(ROWS_DEV // LANES):
            lanes = pl.ds(block * LANES, LANES)
            factor = (1 - 2 * sign[pl.ds(block, 1), :]).astype(jnp.float32)
            out_ref[:, lanes] = panel[at, :, lanes] * factor
    copies[3].wait()
    copies[4].wait()
    lane = lax.broadcasted_iota(jnp.int32, (8, LANES), 1)
    slots = jnp.zeros((8, LANES), jnp.int32)
    for i in range(CAP):
        slots = jnp.where(lane == i, rows[i], slots)
        slots = jnp.where(lane == CAP + i, owner[i], slots)
    for i in range(8):
        slots_ref[pl.ds(i * 8, 8), :] = slots


def prepare(side, hidden_panel, sign_bits, pick_rows, pick_owner):
    half = jax.ShapeDtypeStruct((PART, ROWS_DEV), jnp.float32)
    return pl.pallas_call(
        prepare_kernel,
        out_shape=(half, half, jax.ShapeDtypeStruct((64, LANES), jnp.int32)),
        in_specs=[SMEM, HBM, HBM, HBM, HBM],
        out_specs=(VMEM, VMEM, VMEM),
        scratch_shapes=[
            pltpu.VMEM((2, PART, ROWS_DEV), jnp.float32),
            pltpu.VMEM((ROWS_DEV // LANES, LANES), jnp.int32),
            pltpu.SMEM((CAP,), jnp.int32),
            pltpu.SMEM((CAP,), jnp.int32),
            pltpu.SemaphoreType.DMA((5,)),
        ],
        compiler_params=pltpu.CompilerParams(vmem_limit_bytes=8 * 2**20),
        cost_estimate=pl.CostEstimate(flops=10**6, bytes_accessed=2**21, transcendentals=0),
        name="prepare",
    )(
        side,
        pltpu.with_memory_space_constraint(hidden_panel, pltpu.HBM),
        pltpu.with_memory_space_constraint(sign_bits.reshape(ROWS_DEV // LANES, LANES), pltpu.HBM),
        pltpu.with_memory_space_constraint(pick_rows, pltpu.HBM),
        pltpu.with_memory_space_constraint(pick_owner, pltpu.HBM),
    )


def local(hidden_panel, sign_bits, pick_rows, pick_owner):
    me = ((lax.axis_index("gx") * 8 + lax.axis_index("gy")) * 4 + lax.axis_index("x")) * 2 + lax.axis_index("core")
    side = (lax.axis_index("x") % 2).reshape(1).astype(jnp.int32)
    send, own, slots = prepare(side, hidden_panel, sign_bits, pick_rows, pick_owner)
    near = lax.ppermute(send, "x", [(i, i ^ 1) for i in range(4)])
    first_slots = lax.all_to_all(
        slots.reshape(64, 1, LANES), ("gx", "gy"), split_axis=0, concat_axis=0, tiled=True
    )
    sources = invert((me % 8).reshape(1).astype(jnp.int32), first_slots.reshape(64, LANES))
    own = join(own, near, sources)
    sources = lax.all_to_all(sources, ("x", "core"), split_axis=0, concat_axis=0, tiled=True)
    table = make_table(own, lax.ppermute(own, "core", [(0, 1), (1, 0)]))
    columns = pick_columns(me.reshape(1).astype(jnp.int32), sources, table)
    columns = lax.all_to_all(
        columns.reshape(CHIPS, 4, LANES), ("gx", "gy", "x"), split_axis=0, concat_axis=0, tiled=True
    )
    return finish(columns.reshape(OUT_ROWS, LANES))


def solution(mesh):
    inner = Mesh(mesh.devices.reshape(8, 8, 4, 2), ("gx", "gy", "x", "core"))
    rows = ("gx", "gy", "x", "core")
    return jax.shard_map(
        local,
        mesh=inner,
        in_specs=(P(None, rows), P(rows), P(rows), P(rows)),
        out_specs=P(None, rows),
        check_vma=False,
    )
```

```python
import jax
import jax.numpy as jnp
import numpy as np
from jax import lax
from jax.experimental import pallas as pl
from jax.experimental.pallas import tpu as pltpu
from jax.sharding import Mesh, PartitionSpec as P

PANEL = 32
ROWS_DEV = 8192
CAP = 64
DEVS = 512
PART = PANEL // 2
SOURCES = 4
BASE = 256
FOLDS = ROWS_DEV // BASE
PAD = 8
HALF = ROWS_DEV // 2
TABLE = HALF + 2 * PAD
LANES = 128
CHIPS = 256
OUT_ROWS = 4 * CHIPS
GROUPED = 8
PIECES = 8
SCALE = 2.0**-11
NT = (((1,), (1,)), ((), ()))
VMEM, SMEM, HBM = (pl.BlockSpec(memory_space=m) for m in (pltpu.VMEM, pltpu.SMEM, pltpu.HBM))


def hadamard_np(order):
    matrix = np.ones((1, 1), np.float32)
    while matrix.shape[0] < order:
        matrix = np.block([[matrix, matrix], [matrix, -matrix]])
    return matrix


def butterflies(parts):
    half = 1
    while half < len(parts):
        for start in range(0, len(parts), 2 * half):
            for i in range(start, start + half):
                low, high = parts[i], parts[i + half]
                parts[i], parts[i + half] = low + high, low - high
        half *= 2
    return parts


def join_kernel(own_ref, near_ref, sources_ref, out_ref):
    out_ref[0] = own_ref[...]
    out_ref[1] = near_ref[...]


def join(own, near, sources):
    return pl.pallas_call(
        join_kernel,
        out_shape=jax.ShapeDtypeStruct((2, PART, ROWS_DEV), jnp.float32),
        in_specs=[VMEM, VMEM, HBM],
        out_specs=VMEM,
        compiler_params=pltpu.CompilerParams(vmem_limit_bytes=8 * 2**20),
        cost_estimate=pl.CostEstimate(flops=0, bytes_accessed=2**21, transcendentals=0),
        name="join_halves",
    )(own, near, sources)


def table_rows(piece):
    start = piece * (HALF // PIECES)
    end = TABLE if piece == PIECES - 1 else start + HALF // PIECES
    return pl.ds(start, end - start)


def table_kernel(own_ref, other_ref, had_hbm, table_hbm, mixed, table, had_ref, sems):
    had_copy = pltpu.make_async_copy(had_hbm, had_ref, sems.at[PIECES])
    had_copy.start()
    for source, (ref, chip) in enumerate((ref, chip) for ref in (own_ref, other_ref) for chip in range(2)):
        def fold_rows(step, _, ref=ref, chip=chip, source=source):
            group, half = step // 2, step % 2
            rows = pl.ds(pl.multiple_of(group * 8, 8), 8)
            column = half * LANES
            parts = [ref[chip, rows, pl.ds(pl.multiple_of(fold * BASE + column, LANES), LANES)] for fold in range(FOLDS)]
            out_rows = pl.ds(pl.multiple_of(source * PART + group * 8, 8), 8)
            for fold, part in enumerate(butterflies(parts)):
                mixed[fold, out_rows, pl.ds(pl.multiple_of(column, LANES), LANES)] = part
            return 0

        lax.fori_loop(0, PART // 8 * 2, fold_rows, 0)

    had_copy.wait()
    edge = jnp.zeros((PAD, LANES), jnp.float32)
    table[pl.ds(0, PAD), :] = edge
    table[pl.ds(TABLE - PAD, PAD), :] = edge

    def transform(piece):
        highs, lows = [], []
        for fold in (2 * piece, 2 * piece + FOLDS // 2, 2 * piece + 1, 2 * piece + 1 + FOLDS // 2):
            block = jnp.concatenate(
                butterflies([mixed[fold, pl.ds(source * PART, PART), :] for source in range(SOURCES)]), axis=0
            )
            highs.append(block.astype(jnp.bfloat16))
            lows.append((block - highs[-1].astype(jnp.float32)).astype(jnp.bfloat16))
        out = jnp.zeros((BASE, 2 * LANES), jnp.float32)
        for pieces in (highs, lows):
            out += lax.dot_general(
                had_ref[...], jnp.concatenate(pieces, axis=0), NT, preferred_element_type=jnp.float32
            )
        for i in range(2):
            table[pl.ds((2 * piece + i) * BASE + PAD, BASE), :] = out[:, i * LANES : (i + 1) * LANES]

    copies = []
    for piece in range(PIECES):
        transform(piece)
        rows = table_rows(piece)
        copies.append(pltpu.make_async_copy(table.at[rows, :], table_hbm.at[rows, :], sems.at[piece]))
        copies[-1].start()
    for copy in copies:
        copy.wait()


def make_table(own, other):
    had = jnp.asarray(hadamard_np(BASE), jnp.bfloat16)
    return pl.pallas_call(
        table_kernel,
        out_shape=pltpu.HBM((TABLE, LANES), jnp.float32),
        in_specs=[VMEM, VMEM, HBM],
        out_specs=HBM,
        scratch_shapes=[
            pltpu.VMEM((FOLDS, SOURCES * PART, BASE), jnp.float32),
            pltpu.VMEM((TABLE, LANES), jnp.float32),
            pltpu.VMEM((BASE, BASE), jnp.bfloat16),
            pltpu.SemaphoreType.DMA((PIECES + 1,)),
        ],
        compiler_params=pltpu.CompilerParams(vmem_limit_bytes=24 * 2**20),
        cost_estimate=pl.CostEstimate(flops=10**9, bytes_accessed=10 * 2**20, transcendentals=0),
        name="local_transform",
    )(own, other, pltpu.with_memory_space_constraint(had, pltpu.HBM))


def invert_kernel(group_ref, slots_ref, out_ref):
    lane = lax.broadcasted_iota(jnp.int32, (32, LANES), 1)
    even, odd = slots_ref[pl.ds(0, 32, stride=2), :], slots_ref[pl.ds(1, 32, stride=2), :]
    first = lane < CAP
    picks = jnp.where(first, even, pltpu.roll(odd, CAP, 1))
    owner = jnp.where(first, pltpu.roll(even, CAP, 1), odd)
    place = 2 * lax.broadcasted_iota(jnp.int32, (32, LANES), 0) + jnp.where(first, 0, 1)
    bf16 = lambda v: v.astype(jnp.float32).astype(jnp.bfloat16)
    high = bf16(jnp.where(owner >= 0, ((owner >> 5) & 1) * 128 + (owner >> 7), -1))
    low = bf16((owner & 7) * 8 + ((owner >> 6) & 1) * 4 + ((owner >> 3) & 3))
    values = bf16(picks & (BASE - 1)), bf16(picks >> 8), bf16(place + 1)
    high_at = bf16(lax.broadcasted_iota(jnp.int32, (256, LANES), 0))
    low_at = bf16(lax.broadcasted_iota(jnp.int32, (64, LANES), 0))
    one, zero = jnp.ones((), jnp.bfloat16), jnp.zeros((), jnp.bfloat16)
    total = jnp.zeros((192, 256), jnp.float32)
    for start in range(0, 32, 16):
        lhs, rhs = [], []
        for i in range(start, start + 16):
            at = lambda v: v[i : i + 1, :]
            rhs.append(jnp.where(at(high) == high_at, one, zero))
            hit = at(low) == low_at
            lhs.append(jnp.concatenate([jnp.where(hit, at(v), zero) for v in values], axis=0))
        total += lax.dot_general(
            jnp.concatenate(lhs, axis=1), jnp.concatenate(rhs, axis=1), NT, preferred_element_type=jnp.float32
        )
    base, fold, place = (total[i * 64 : (i + 1) * 64].astype(jnp.int32) for i in range(3))
    row = ((place - 1) * 8 + group_ref[0]) * ROWS_DEV + fold * BASE + base
    found = jnp.where(place > 0, row + 1, 0)
    for i in range(8):
        out_ref[i] = found[:, i % 2 * LANES : (i % 2 + 1) * LANES]


def invert(group, slots):
    return pl.pallas_call(
        invert_kernel,
        out_shape=jax.ShapeDtypeStruct((8, 64, LANES), jnp.int32),
        in_specs=[SMEM, VMEM],
        out_specs=VMEM,
        compiler_params=pltpu.CompilerParams(vmem_limit_bytes=8 * 2**20),
        cost_estimate=pl.CostEstimate(flops=4 * 10**8, bytes_accessed=2**19, transcendentals=0),
        name="invert_slots",
    )(group, slots)


def pick_kernel(
    me_ref, sources_ref, spread_ref, table_hbm, out_ref, table, where_vmem, signed, wide, sems, *where_smem
):
    table_copies = []
    for piece in range(PIECES):
        rows = table_rows(piece)
        table_copies.append(pltpu.make_async_copy(table_hbm.at[rows, :], table.at[rows, :], sems.at[8 + piece]))
        table_copies[-1].start()
    bf16 = lambda v: v.astype(jnp.float32).astype(jnp.bfloat16)
    source = sources_ref[0]
    for i in range(1, 8):
        source += sources_ref[i]
    source = source - 1
    device = source >> 13
    odd_bits = device & me_ref[0]
    for shift in (8, 4, 2, 1):
        odd_bits = odd_bits ^ (odd_bits >> shift)
    combo = ((source >> 12) & 1) * 4 + (device & 1) * 2 + ((device >> 1) & 1) + 1
    sub = lax.broadcasted_iota(jnp.int32, (64, 128), 0) % 8
    where_vmem[...] = (source & (HALF - 1)) + PAD - sub
    where_copies = [
        pltpu.make_async_copy(where_vmem.at[pl.ds(g * 8, 8), :], where_smem[g], sems.at[g]) for g in range(8)
    ]
    for copy in where_copies:
        copy.start()
    combo = bf16(jnp.where(odd_bits & 1 == 1, -combo, combo).T)
    for i in range(8):
        signed[pl.ds(i, 128, stride=8), :] = jnp.dot(
            combo, spread_ref[:, i * LANES : (i + 1) * LANES], preferred_element_type=jnp.float32
        )
    lane = lax.broadcasted_iota(jnp.int32, (8, LANES), 1)
    sub = lax.broadcasted_iota(jnp.int32, (8, LANES), 0)
    row_of = lane // PART
    lane_of = lane % PART - PART
    turn = lambda v, index: jnp.take_along_axis(v, index, axis=1, mode="promise_in_bounds")
    for copy in table_copies:
        copy.wait()
    for copy in where_copies:
        copy.wait()

    def gather(group, place):
        block = group * GROUPED + place
        rows = pl.ds(pl.multiple_of(block * 8, 8), 8)
        for g in range(8):
            at = lambda i: where_smem[g].at[i, pl.ds(place, LANES - GROUPED + 1)][group * GROUPED]
            value = table[pl.ds(at(0), 8), :]
            for i in range(1, 8):
                value = jnp.where(sub == i, table[pl.ds(at(i), 8), :], value)
            wide[rows, pl.ds(g * LANES, LANES)] = value

    def choose(block):
        rows = pl.ds(pl.multiple_of(block * 8, 8), 8)
        combo = signed[rows, :]
        index = lane_of + PART * jnp.abs(combo).astype(jnp.int32)
        out = turn(wide[rows, pl.ds(0, LANES)], index)
        for g in range(1, 8):
            out = jnp.where(row_of == g, turn(wide[rows, pl.ds(g * LANES, LANES)], index), out)
        out_ref[rows, :] = out * jnp.where(combo < 0, -SCALE, SCALE)

    def both(group, _):
        for i in range(GROUPED):
            choose((group - 1) * GROUPED + i)
        for i in range(GROUPED):
            gather(group, i)
        return 0

    groups = OUT_ROWS // 8 // GROUPED
    for i in range(GROUPED):
        gather(0, i)
    lax.fori_loop(1, groups, both, 0)
    for i in range(GROUPED):
        choose((groups - 1) * GROUPED + i)


def spread_np():
    column = np.arange(8 * LANES)
    return (np.arange(64)[:, None] == (column % LANES // PART * 8 + column // LANES)[None, :]).astype(np.float32)


def pick_columns(me, sources, table):
    return pl.pallas_call(
        pick_kernel,
        out_shape=jax.ShapeDtypeStruct((OUT_ROWS, LANES), jnp.float32),
        in_specs=[SMEM, VMEM, VMEM, HBM],
        out_specs=VMEM,
        scratch_shapes=[
            pltpu.VMEM((TABLE, LANES), jnp.float32),
            pltpu.VMEM((64, 128), jnp.int32),
            pltpu.VMEM((OUT_ROWS, LANES), jnp.float32),
            pltpu.VMEM((OUT_ROWS, 8 * LANES), jnp.float32),
            pltpu.SemaphoreType.DMA((8 + PIECES,)),
            *[pltpu.SMEM((8, 128), jnp.int32)] * 8,
        ],
        compiler_params=pltpu.CompilerParams(vmem_limit_bytes=24 * 2**20),
        cost_estimate=pl.CostEstimate(flops=10**8, bytes_accessed=10 * 2**20, transcendentals=0),
        name="pick_columns",
    )(
        me,
        sources,
        jnp.asarray(spread_np(), jnp.bfloat16),
        pltpu.with_memory_space_constraint(table, pltpu.HBM),
    )


def finish_kernel(parts_ref, chosen_ref, out_ref):
    totals = [parts_ref[pl.ds(i * 8, 8), :] for i in range(8)]
    for block in range(8, OUT_ROWS // 8):
        totals[block % 8] += parts_ref[pl.ds(block * 8, 8), :]
    while len(totals) > 1:
        totals = [low + high for low, high in zip(totals[::2], totals[1::2])]
    total = totals[0]
    group = lax.broadcasted_iota(jnp.int32, (8, LANES), 1) // PART == lax.broadcasted_iota(jnp.int32, (8, LANES), 0)
    spread = [jnp.where(group, jnp.broadcast_to(total[i : i + 1], (8, LANES)), 0.0) for i in range(8)]
    out = lax.dot_general(
        chosen_ref[...],
        jnp.concatenate(spread, axis=0),
        NT,
        precision=lax.Precision.HIGHEST,
        preferred_element_type=jnp.float32,
    )
    out_ref[pl.ds(0, PART), :] = out[:, :PANEL]
    out_ref[pl.ds(PART, PART), :] = out[:, PANEL:]


def finish(parts):
    chosen = (np.arange(PART)[:, None] == np.arange(LANES)[None, :] % PART).astype(np.float32)
    return pl.pallas_call(
        finish_kernel,
        out_shape=jax.ShapeDtypeStruct((PANEL, PANEL), jnp.float32),
        in_specs=[VMEM, VMEM],
        out_specs=VMEM,
        compiler_params=pltpu.CompilerParams(vmem_limit_bytes=4 * 2**20),
        cost_estimate=pl.CostEstimate(flops=10**6, bytes_accessed=2**19, transcendentals=0),
        name="finish",
    )(parts, jnp.asarray(chosen))


def prepare_kernel(
    side_ref, panel_hbm, sign_hbm, rows_hbm, owner_hbm, send_ref, own_ref, slots_ref, panel, sign, rows, owner, sems
):
    side = side_ref[0]
    half = lambda at: panel_hbm.at[pl.ds(pl.multiple_of(at * PART, PART), PART), :]
    copies = [
        pltpu.make_async_copy(source, target, sems.at[i])
        for i, (source, target) in enumerate(
            (
                (sign_hbm, sign),
                (half(1 - side), panel.at[0]),
                (half(side), panel.at[1]),
                (rows_hbm, rows),
                (owner_hbm, owner),
            )
        )
    ]
    for copy in copies[3:] + copies[:3]:
        copy.start()
    copies[3].wait()
    copies[4].wait()
    lane = lax.broadcasted_iota(jnp.int32, (8, LANES), 1)
    parts = [jnp.zeros((8, LANES), jnp.int32)] * 8
    for i in range(CAP):
        parts[i % 8] = jnp.where(lane == i, rows[i], parts[i % 8])
        parts[i % 8] = jnp.where(lane == CAP + i, owner[i], parts[i % 8])
    slots = parts[0]
    for part in parts[1:]:
        slots = slots + part
    for i in range(8):
        slots_ref[pl.ds(i * 8, 8), :] = slots
    copies[0].wait()
    for at, out_ref in enumerate((send_ref, own_ref)):
        copies[1 + at].wait()
        for block in range(ROWS_DEV // LANES):
            lanes = pl.ds(block * LANES, LANES)
            factor = (1 - 2 * sign[pl.ds(block, 1), :]).astype(jnp.float32)
            out_ref[:, lanes] = panel[at, :, lanes] * factor


def prepare(side, hidden_panel, sign_bits, pick_rows, pick_owner):
    half = jax.ShapeDtypeStruct((PART, ROWS_DEV), jnp.float32)
    return pl.pallas_call(
        prepare_kernel,
        out_shape=(half, half, jax.ShapeDtypeStruct((64, LANES), jnp.int32)),
        in_specs=[SMEM, HBM, HBM, HBM, HBM],
        out_specs=(VMEM, VMEM, VMEM),
        scratch_shapes=[
            pltpu.VMEM((2, PART, ROWS_DEV), jnp.float32),
            pltpu.VMEM((ROWS_DEV // LANES, LANES), jnp.int32),
            pltpu.SMEM((CAP,), jnp.int32),
            pltpu.SMEM((CAP,), jnp.int32),
            pltpu.SemaphoreType.DMA((5,)),
        ],
        compiler_params=pltpu.CompilerParams(vmem_limit_bytes=8 * 2**20),
        cost_estimate=pl.CostEstimate(flops=10**6, bytes_accessed=2**21, transcendentals=0),
        name="prepare",
    )(
        side,
        pltpu.with_memory_space_constraint(hidden_panel, pltpu.HBM),
        pltpu.with_memory_space_constraint(sign_bits.reshape(ROWS_DEV // LANES, LANES), pltpu.HBM),
        pltpu.with_memory_space_constraint(pick_rows, pltpu.HBM),
        pltpu.with_memory_space_constraint(pick_owner, pltpu.HBM),
    )


def local(hidden_panel, sign_bits, pick_rows, pick_owner):
    me = ((lax.axis_index("gx") * 8 + lax.axis_index("gy")) * 4 + lax.axis_index("x")) * 2 + lax.axis_index("core")
    side = (lax.axis_index("x") % 2).reshape(1).astype(jnp.int32)
    send, own, slots = prepare(side, hidden_panel, sign_bits, pick_rows, pick_owner)
    near = lax.ppermute(send, "x", [(i, i ^ 1) for i in range(4)])
    first_slots = lax.all_to_all(
        slots.reshape(64, 1, LANES), ("gx", "gy"), split_axis=0, concat_axis=0, tiled=True
    )
    sources = invert((me % 8).reshape(1).astype(jnp.int32), first_slots.reshape(64, LANES))
    own = join(own, near, sources)
    sources = lax.all_to_all(sources, ("x", "core"), split_axis=0, concat_axis=0, tiled=True)
    table = make_table(own, lax.ppermute(own, "core", [(0, 1), (1, 0)]))
    columns = pick_columns(me.reshape(1).astype(jnp.int32), sources, table)
    columns = lax.all_to_all(
        columns.reshape(CHIPS, 4, LANES), ("gx", "gy", "x"), split_axis=0, concat_axis=0, tiled=True
    )
    return finish(columns.reshape(OUT_ROWS, LANES))


def solution(mesh):
    inner = Mesh(mesh.devices.reshape(8, 8, 4, 2), ("gx", "gy", "x", "core"))
    rows = ("gx", "gy", "x", "core")
    return jax.shard_map(
        local,
        mesh=inner,
        in_specs=(P(None, rows), P(rows), P(rows), P(rows)),
        out_specs=P(None, rows),
        check_vma=False,
    )
```

```python
import jax
import jax.numpy as jnp
import numpy as np
from jax import lax
from jax.experimental import pallas as pl
from jax.experimental.pallas import tpu as pltpu
from jax.sharding import Mesh, PartitionSpec as P

PANEL = 32
ROWS_DEV = 8192
CAP = 64
DEVS = 512
PART = PANEL // 2
SOURCES = 4
BASE = 256
FOLDS = ROWS_DEV // BASE
PAD = 8
HALF = ROWS_DEV // 2
TABLE = HALF + 2 * PAD
LANES = 128
CHIPS = 256
OUT_ROWS = 4 * CHIPS
GROUPED = 8
PIECES = 8
SCALE = 2.0**-11
NT = (((1,), (1,)), ((), ()))
VMEM, SMEM, HBM = (pl.BlockSpec(memory_space=m) for m in (pltpu.VMEM, pltpu.SMEM, pltpu.HBM))


def hadamard_np(order):
    matrix = np.ones((1, 1), np.float32)
    while matrix.shape[0] < order:
        matrix = np.block([[matrix, matrix], [matrix, -matrix]])
    return matrix


def butterflies(parts):
    half = 1
    while half < len(parts):
        for start in range(0, len(parts), 2 * half):
            for i in range(start, start + half):
                low, high = parts[i], parts[i + half]
                parts[i], parts[i + half] = low + high, low - high
        half *= 2
    return parts


def join_kernel(own_ref, near_ref, sources_ref, out_ref):
    out_ref[0] = own_ref[...]
    out_ref[1] = near_ref[...]


def join(own, near, sources):
    return pl.pallas_call(
        join_kernel,
        out_shape=jax.ShapeDtypeStruct((2, PART, ROWS_DEV), jnp.float32),
        in_specs=[VMEM, VMEM, HBM],
        out_specs=VMEM,
        compiler_params=pltpu.CompilerParams(vmem_limit_bytes=8 * 2**20),
        cost_estimate=pl.CostEstimate(flops=0, bytes_accessed=2**21, transcendentals=0),
        name="join_halves",
    )(own, near, sources)


def table_rows(piece):
    start = piece * (HALF // PIECES)
    end = TABLE if piece == PIECES - 1 else start + HALF // PIECES
    return pl.ds(start, end - start)


def table_kernel(own_ref, other_ref, had_hbm, table_hbm, mixed, table, had_ref, sems):
    had_copy = pltpu.make_async_copy(had_hbm, had_ref, sems.at[PIECES])
    had_copy.start()
    for source, (ref, chip) in enumerate((ref, chip) for ref in (own_ref, other_ref) for chip in range(2)):
        def fold_rows(step, _, ref=ref, chip=chip, source=source):
            group, half = step // 2, step % 2
            rows = pl.ds(pl.multiple_of(group * 8, 8), 8)
            column = half * LANES
            parts = [ref[chip, rows, pl.ds(pl.multiple_of(fold * BASE + column, LANES), LANES)] for fold in range(FOLDS)]
            out_rows = pl.ds(pl.multiple_of(source * PART + group * 8, 8), 8)
            for fold, part in enumerate(butterflies(parts)):
                mixed[fold, out_rows, pl.ds(pl.multiple_of(column, LANES), LANES)] = part
            return 0

        lax.fori_loop(0, PART // 8 * 2, fold_rows, 0)

    had_copy.wait()
    edge = jnp.zeros((PAD, LANES), jnp.float32)
    table[pl.ds(0, PAD), :] = edge
    table[pl.ds(TABLE - PAD, PAD), :] = edge

    def transform(piece):
        highs, middles, lows = [], [], []
        for fold in (2 * piece, 2 * piece + FOLDS // 2, 2 * piece + 1, 2 * piece + 1 + FOLDS // 2):
            block = jnp.concatenate(
                butterflies([mixed[fold, pl.ds(source * PART, PART), :] for source in range(SOURCES)]), axis=0
            )
            highs.append(block.astype(jnp.bfloat16))
            rest = block - highs[-1].astype(jnp.float32)
            middles.append(rest.astype(jnp.bfloat16))
            lows.append((rest - middles[-1].astype(jnp.float32)).astype(jnp.bfloat16))
        out = jnp.zeros((BASE, 2 * LANES), jnp.float32)
        for pieces in (lows, middles, highs):
            out += lax.dot_general(
                had_ref[...], jnp.concatenate(pieces, axis=0), NT, preferred_element_type=jnp.float32
            )
        for i in range(2):
            table[pl.ds((2 * piece + i) * BASE + PAD, BASE), :] = out[:, i * LANES : (i + 1) * LANES]

    copies = []
    for piece in range(PIECES):
        transform(piece)
        rows = table_rows(piece)
        copies.append(pltpu.make_async_copy(table.at[rows, :], table_hbm.at[rows, :], sems.at[piece]))
        copies[-1].start()
    for copy in copies:
        copy.wait()


def make_table(own, other):
    had = jnp.asarray(hadamard_np(BASE), jnp.bfloat16)
    return pl.pallas_call(
        table_kernel,
        out_shape=pltpu.HBM((TABLE, LANES), jnp.float32),
        in_specs=[VMEM, VMEM, HBM],
        out_specs=HBM,
        scratch_shapes=[
            pltpu.VMEM((FOLDS, SOURCES * PART, BASE), jnp.float32),
            pltpu.VMEM((TABLE, LANES), jnp.float32),
            pltpu.VMEM((BASE, BASE), jnp.bfloat16),
            pltpu.SemaphoreType.DMA((PIECES + 1,)),
        ],
        compiler_params=pltpu.CompilerParams(vmem_limit_bytes=24 * 2**20),
        cost_estimate=pl.CostEstimate(flops=10**9, bytes_accessed=10 * 2**20, transcendentals=0),
        name="local_transform",
    )(own, other, pltpu.with_memory_space_constraint(had, pltpu.HBM))


def invert_kernel(group_ref, slots_ref, out_ref):
    lane = lax.broadcasted_iota(jnp.int32, (32, LANES), 1)
    even, odd = slots_ref[pl.ds(0, 32, stride=2), :], slots_ref[pl.ds(1, 32, stride=2), :]
    first = lane < CAP
    picks = jnp.where(first, even, pltpu.roll(odd, CAP, 1))
    owner = jnp.where(first, pltpu.roll(even, CAP, 1), odd)
    place = 2 * lax.broadcasted_iota(jnp.int32, (32, LANES), 0) + jnp.where(first, 0, 1)
    bf16 = lambda v: v.astype(jnp.float32).astype(jnp.bfloat16)
    high = bf16(jnp.where(owner >= 0, ((owner >> 5) & 1) * 128 + (owner >> 7), -1))
    low = bf16((owner & 7) * 8 + ((owner >> 6) & 1) * 4 + ((owner >> 3) & 3))
    values = bf16(picks & (BASE - 1)), bf16(picks >> 8), bf16(place + 1)
    high_at = bf16(lax.broadcasted_iota(jnp.int32, (256, LANES), 0))
    low_at = bf16(lax.broadcasted_iota(jnp.int32, (64, LANES), 0))
    one, zero = jnp.ones((), jnp.bfloat16), jnp.zeros((), jnp.bfloat16)
    total = jnp.zeros((192, 256), jnp.float32)
    for start in range(0, 32, 16):
        lhs, rhs = [], []
        for i in range(start, start + 16):
            at = lambda v: v[i : i + 1, :]
            rhs.append(jnp.where(at(high) == high_at, one, zero))
            hit = at(low) == low_at
            lhs.append(jnp.concatenate([jnp.where(hit, at(v), zero) for v in values], axis=0))
        total += lax.dot_general(
            jnp.concatenate(lhs, axis=1), jnp.concatenate(rhs, axis=1), NT, preferred_element_type=jnp.float32
        )
    base, fold, place = (total[i * 64 : (i + 1) * 64].astype(jnp.int32) for i in range(3))
    row = ((place - 1) * 8 + group_ref[0]) * ROWS_DEV + fold * BASE + base
    found = jnp.where(place > 0, row + 1, 0)
    for i in range(8):
        out_ref[i] = found[:, i % 2 * LANES : (i % 2 + 1) * LANES]


def invert(group, slots):
    return pl.pallas_call(
        invert_kernel,
        out_shape=jax.ShapeDtypeStruct((8, 64, LANES), jnp.int32),
        in_specs=[SMEM, VMEM],
        out_specs=VMEM,
        compiler_params=pltpu.CompilerParams(vmem_limit_bytes=8 * 2**20),
        cost_estimate=pl.CostEstimate(flops=4 * 10**8, bytes_accessed=2**19, transcendentals=0),
        name="invert_slots",
    )(group, slots)


def pick_kernel(
    me_ref, sources_ref, spread_ref, table_hbm, out_ref, table, where_vmem, signed, wide, sems, *where_smem
):
    table_copies = []
    for piece in range(PIECES):
        rows = table_rows(piece)
        table_copies.append(pltpu.make_async_copy(table_hbm.at[rows, :], table.at[rows, :], sems.at[8 + piece]))
        table_copies[-1].start()
    bf16 = lambda v: v.astype(jnp.float32).astype(jnp.bfloat16)
    source = sources_ref[0]
    for i in range(1, 8):
        source += sources_ref[i]
    source = source - 1
    device = source >> 13
    odd_bits = device & me_ref[0]
    for shift in (8, 4, 2, 1):
        odd_bits = odd_bits ^ (odd_bits >> shift)
    combo = ((source >> 12) & 1) * 4 + (device & 1) * 2 + ((device >> 1) & 1) + 1
    sub = lax.broadcasted_iota(jnp.int32, (64, 128), 0) % 8
    where_vmem[...] = (source & (HALF - 1)) + PAD - sub
    where_copies = [
        pltpu.make_async_copy(where_vmem.at[pl.ds(g * 8, 8), :], where_smem[g], sems.at[g]) for g in range(8)
    ]
    for copy in where_copies:
        copy.start()
    combo = bf16(jnp.where(odd_bits & 1 == 1, -combo, combo).T)
    for i in range(8):
        signed[pl.ds(i, 128, stride=8), :] = jnp.dot(
            combo, spread_ref[:, i * LANES : (i + 1) * LANES], preferred_element_type=jnp.float32
        )
    lane = lax.broadcasted_iota(jnp.int32, (8, LANES), 1)
    sub = lax.broadcasted_iota(jnp.int32, (8, LANES), 0)
    row_of = lane // PART
    lane_of = lane % PART - PART
    turn = lambda v, index: jnp.take_along_axis(v, index, axis=1, mode="promise_in_bounds")
    for copy in table_copies:
        copy.wait()
    for copy in where_copies:
        copy.wait()

    def gather(group, place):
        block = group * GROUPED + place
        rows = pl.ds(pl.multiple_of(block * 8, 8), 8)
        for g in range(8):
            at = lambda i: where_smem[g].at[i, pl.ds(place, LANES - GROUPED + 1)][group * GROUPED]
            value = table[pl.ds(at(0), 8), :]
            for i in range(1, 8):
                value = jnp.where(sub == i, table[pl.ds(at(i), 8), :], value)
            wide[rows, pl.ds(g * LANES, LANES)] = value

    def choose(block):
        rows = pl.ds(pl.multiple_of(block * 8, 8), 8)
        combo = signed[rows, :]
        index = lane_of + PART * jnp.abs(combo).astype(jnp.int32)
        out = turn(wide[rows, pl.ds(0, LANES)], index)
        for g in range(1, 8):
            out = jnp.where(row_of == g, turn(wide[rows, pl.ds(g * LANES, LANES)], index), out)
        out_ref[rows, :] = out * jnp.where(combo < 0, -SCALE, SCALE)

    def both(group, _):
        for i in range(GROUPED):
            choose((group - 1) * GROUPED + i)
        for i in range(GROUPED):
            gather(group, i)
        return 0

    groups = OUT_ROWS // 8 // GROUPED
    for i in range(GROUPED):
        gather(0, i)
    lax.fori_loop(1, groups, both, 0)
    for i in range(GROUPED):
        choose((groups - 1) * GROUPED + i)


def spread_np():
    column = np.arange(8 * LANES)
    return (np.arange(64)[:, None] == (column % LANES // PART * 8 + column // LANES)[None, :]).astype(np.float32)


def pick_columns(me, sources, table):
    return pl.pallas_call(
        pick_kernel,
        out_shape=jax.ShapeDtypeStruct((OUT_ROWS, LANES), jnp.float32),
        in_specs=[SMEM, VMEM, VMEM, HBM],
        out_specs=VMEM,
        scratch_shapes=[
            pltpu.VMEM((TABLE, LANES), jnp.float32),
            pltpu.VMEM((64, 128), jnp.int32),
            pltpu.VMEM((OUT_ROWS, LANES), jnp.float32),
            pltpu.VMEM((OUT_ROWS, 8 * LANES), jnp.float32),
            pltpu.SemaphoreType.DMA((8 + PIECES,)),
            *[pltpu.SMEM((8, 128), jnp.int32)] * 8,
        ],
        compiler_params=pltpu.CompilerParams(vmem_limit_bytes=24 * 2**20),
        cost_estimate=pl.CostEstimate(flops=10**8, bytes_accessed=10 * 2**20, transcendentals=0),
        name="pick_columns",
    )(
        me,
        sources,
        jnp.asarray(spread_np(), jnp.bfloat16),
        pltpu.with_memory_space_constraint(table, pltpu.HBM),
    )


def finish_kernel(parts_ref, chosen_ref, out_ref):
    totals = [parts_ref[pl.ds(i * 8, 8), :] for i in range(8)]
    for block in range(8, OUT_ROWS // 8):
        totals[block % 8] += parts_ref[pl.ds(block * 8, 8), :]
    while len(totals) > 1:
        totals = [low + high for low, high in zip(totals[::2], totals[1::2])]
    total = totals[0]
    group = lax.broadcasted_iota(jnp.int32, (8, LANES), 1) // PART == lax.broadcasted_iota(jnp.int32, (8, LANES), 0)
    spread = [jnp.where(group, jnp.broadcast_to(total[i : i + 1], (8, LANES)), 0.0) for i in range(8)]
    out = lax.dot_general(
        chosen_ref[...],
        jnp.concatenate(spread, axis=0),
        NT,
        precision=lax.Precision.HIGHEST,
        preferred_element_type=jnp.float32,
    )
    out_ref[pl.ds(0, PART), :] = out[:, :PANEL]
    out_ref[pl.ds(PART, PART), :] = out[:, PANEL:]


def finish(parts):
    chosen = (np.arange(PART)[:, None] == np.arange(LANES)[None, :] % PART).astype(np.float32)
    return pl.pallas_call(
        finish_kernel,
        out_shape=jax.ShapeDtypeStruct((PANEL, PANEL), jnp.float32),
        in_specs=[VMEM, VMEM],
        out_specs=VMEM,
        compiler_params=pltpu.CompilerParams(vmem_limit_bytes=4 * 2**20),
        cost_estimate=pl.CostEstimate(flops=10**6, bytes_accessed=2**19, transcendentals=0),
        name="finish",
    )(parts, jnp.asarray(chosen))


def prepare_kernel(
    side_ref, panel_hbm, sign_hbm, rows_hbm, owner_hbm, send_ref, own_ref, slots_ref, panel, sign, rows, owner, sems
):
    side = side_ref[0]
    half = lambda at: panel_hbm.at[pl.ds(pl.multiple_of(at * PART, PART), PART), :]
    copies = [
        pltpu.make_async_copy(source, target, sems.at[i])
        for i, (source, target) in enumerate(
            (
                (sign_hbm, sign),
                (half(1 - side), panel.at[0]),
                (half(side), panel.at[1]),
                (rows_hbm, rows),
                (owner_hbm, owner),
            )
        )
    ]
    for copy in copies[3:] + copies[:3]:
        copy.start()
    copies[3].wait()
    copies[4].wait()
    lane = lax.broadcasted_iota(jnp.int32, (8, LANES), 1)
    parts = [jnp.zeros((8, LANES), jnp.int32)] * 8
    for i in range(CAP):
        parts[i % 8] = jnp.where(lane == i, rows[i], parts[i % 8])
        parts[i % 8] = jnp.where(lane == CAP + i, owner[i], parts[i % 8])
    slots = parts[0]
    for part in parts[1:]:
        slots = slots + part
    for i in range(8):
        slots_ref[pl.ds(i * 8, 8), :] = slots
    copies[0].wait()
    for at, out_ref in enumerate((send_ref, own_ref)):
        copies[1 + at].wait()
        for block in range(ROWS_DEV // LANES):
            lanes = pl.ds(block * LANES, LANES)
            factor = (1 - 2 * sign[pl.ds(block, 1), :]).astype(jnp.float32)
            out_ref[:, lanes] = panel[at, :, lanes] * factor


def prepare(side, hidden_panel, sign_bits, pick_rows, pick_owner):
    half = jax.ShapeDtypeStruct((PART, ROWS_DEV), jnp.float32)
    return pl.pallas_call(
        prepare_kernel,
        out_shape=(half, half, jax.ShapeDtypeStruct((64, LANES), jnp.int32)),
        in_specs=[SMEM, HBM, HBM, HBM, HBM],
        out_specs=(VMEM, VMEM, VMEM),
        scratch_shapes=[
            pltpu.VMEM((2, PART, ROWS_DEV), jnp.float32),
            pltpu.VMEM((ROWS_DEV // LANES, LANES), jnp.int32),
            pltpu.SMEM((CAP,), jnp.int32),
            pltpu.SMEM((CAP,), jnp.int32),
            pltpu.SemaphoreType.DMA((5,)),
        ],
        compiler_params=pltpu.CompilerParams(vmem_limit_bytes=8 * 2**20),
        cost_estimate=pl.CostEstimate(flops=10**6, bytes_accessed=2**21, transcendentals=0),
        name="prepare",
    )(
        side,
        pltpu.with_memory_space_constraint(hidden_panel, pltpu.HBM),
        pltpu.with_memory_space_constraint(sign_bits.reshape(ROWS_DEV // LANES, LANES), pltpu.HBM),
        pltpu.with_memory_space_constraint(pick_rows, pltpu.HBM),
        pltpu.with_memory_space_constraint(pick_owner, pltpu.HBM),
    )


def local(hidden_panel, sign_bits, pick_rows, pick_owner):
    me = ((lax.axis_index("gx") * 8 + lax.axis_index("gy")) * 4 + lax.axis_index("x")) * 2 + lax.axis_index("core")
    side = (lax.axis_index("x") % 2).reshape(1).astype(jnp.int32)
    send, own, slots = prepare(side, hidden_panel, sign_bits, pick_rows, pick_owner)
    near = lax.ppermute(send, "x", [(i, i ^ 1) for i in range(4)])
    first_slots = lax.all_to_all(
        slots.reshape(64, 1, LANES), ("gx", "gy"), split_axis=0, concat_axis=0, tiled=True
    )
    sources = invert((me % 8).reshape(1).astype(jnp.int32), first_slots.reshape(64, LANES))
    own = join(own, near, sources)
    sources = lax.all_to_all(sources, ("x", "core"), split_axis=0, concat_axis=0, tiled=True)
    table = make_table(own, lax.ppermute(own, "core", [(0, 1), (1, 0)]))
    columns = pick_columns(me.reshape(1).astype(jnp.int32), sources, table)
    columns = lax.all_to_all(
        columns.reshape(CHIPS, 4, LANES), ("gx", "gy", "x"), split_axis=0, concat_axis=0, tiled=True
    )
    return finish(columns.reshape(OUT_ROWS, LANES))


def solution(mesh):
    inner = Mesh(mesh.devices.reshape(8, 8, 4, 2), ("gx", "gy", "x", "core"))
    rows = ("gx", "gy", "x", "core")
    return jax.shard_map(
        local,
        mesh=inner,
        in_specs=(P(None, rows), P(rows), P(rows), P(rows)),
        out_specs=P(None, rows),
        check_vma=False,
    )
```

```python
import jax
import jax.numpy as jnp
import numpy as np
from jax import lax
from jax.experimental import pallas as pl
from jax.experimental.pallas import tpu as pltpu
from jax.sharding import Mesh, PartitionSpec as P

PANEL = 32
ROWS_DEV = 8192
CAP = 64
DEVS = 512
PART = PANEL // 2
SOURCES = 4
BASE = 256
FOLDS = ROWS_DEV // BASE
PAD = 8
HALF = ROWS_DEV // 2
TABLE = HALF + 2 * PAD
LANES = 128
CHIPS = 256
OUT_ROWS = 4 * CHIPS
GROUPED = 8
PIECES = 8
SCALE = 2.0**-11
NT = (((1,), (1,)), ((), ()))
VMEM, SMEM, HBM = (pl.BlockSpec(memory_space=m) for m in (pltpu.VMEM, pltpu.SMEM, pltpu.HBM))


def hadamard_np(order):
    matrix = np.ones((1, 1), np.float32)
    while matrix.shape[0] < order:
        matrix = np.block([[matrix, matrix], [matrix, -matrix]])
    return matrix


def butterflies(parts):
    half = 1
    while half < len(parts):
        for start in range(0, len(parts), 2 * half):
            for i in range(start, start + half):
                low, high = parts[i], parts[i + half]
                parts[i], parts[i + half] = low + high, low - high
        half *= 2
    return parts


def join_kernel(own_ref, near_ref, sources_ref, out_ref):
    out_ref[0] = own_ref[...]
    out_ref[1] = near_ref[...]


def join(own, near, sources):
    return pl.pallas_call(
        join_kernel,
        out_shape=jax.ShapeDtypeStruct((2, PART, ROWS_DEV), jnp.float32),
        in_specs=[VMEM, VMEM, HBM],
        out_specs=VMEM,
        compiler_params=pltpu.CompilerParams(vmem_limit_bytes=8 * 2**20),
        cost_estimate=pl.CostEstimate(flops=0, bytes_accessed=2**21, transcendentals=0),
        name="join_halves",
    )(own, near, sources)


def table_rows(piece):
    start = piece * (HALF // PIECES)
    end = TABLE if piece == PIECES - 1 else start + HALF // PIECES
    return pl.ds(start, end - start)


def table_kernel(own_ref, other_ref, had_hbm, table_hbm, mixed, table, had_ref, sems):
    had_copy = pltpu.make_async_copy(had_hbm, had_ref, sems.at[PIECES])
    had_copy.start()
    for source, (ref, chip) in enumerate((ref, chip) for ref in (own_ref, other_ref) for chip in range(2)):
        def fold_rows(step, _, ref=ref, chip=chip, source=source):
            group, half = step // 2, step % 2
            rows = pl.ds(pl.multiple_of(group * 8, 8), 8)
            column = half * LANES
            parts = [ref[chip, rows, pl.ds(pl.multiple_of(fold * BASE + column, LANES), LANES)] for fold in range(FOLDS)]
            out_rows = pl.ds(pl.multiple_of(source * PART + group * 8, 8), 8)
            for fold, part in enumerate(butterflies(parts)):
                mixed[fold, out_rows, pl.ds(pl.multiple_of(column, LANES), LANES)] = part
            return 0

        lax.fori_loop(0, PART // 8 * 2, fold_rows, 0)

    had_copy.wait()
    edge = jnp.zeros((PAD, LANES), jnp.float32)
    table[pl.ds(0, PAD), :] = edge
    table[pl.ds(TABLE - PAD, PAD), :] = edge

    def transform(piece):
        highs, middles, lows = [], [], []
        for fold in (2 * piece, 2 * piece + FOLDS // 2, 2 * piece + 1, 2 * piece + 1 + FOLDS // 2):
            block = jnp.concatenate(
                butterflies([mixed[fold, pl.ds(source * PART, PART), :] for source in range(SOURCES)]), axis=0
            )
            highs.append(block.astype(jnp.bfloat16))
            rest = block - highs[-1].astype(jnp.float32)
            middles.append(rest.astype(jnp.bfloat16))
            lows.append((rest - middles[-1].astype(jnp.float32)).astype(jnp.bfloat16))
        out = jnp.zeros((BASE, 2 * LANES), jnp.float32)
        for pieces in (lows, middles, highs):
            out += lax.dot_general(
                had_ref[...], jnp.concatenate(pieces, axis=0), NT, preferred_element_type=jnp.float32
            )
        for i in range(2):
            table[pl.ds((2 * piece + i) * BASE + PAD, BASE), :] = out[:, i * LANES : (i + 1) * LANES]

    copies = []
    for piece in range(PIECES):
        transform(piece)
        rows = table_rows(piece)
        copies.append(pltpu.make_async_copy(table.at[rows, :], table_hbm.at[rows, :], sems.at[piece]))
        copies[-1].start()
    for copy in copies:
        copy.wait()


def make_table(own, other):
    had = jnp.asarray(hadamard_np(BASE), jnp.bfloat16)
    return pl.pallas_call(
        table_kernel,
        out_shape=pltpu.HBM((TABLE, LANES), jnp.float32),
        in_specs=[VMEM, VMEM, HBM],
        out_specs=HBM,
        scratch_shapes=[
            pltpu.VMEM((FOLDS, SOURCES * PART, BASE), jnp.float32),
            pltpu.VMEM((TABLE, LANES), jnp.float32),
            pltpu.VMEM((BASE, BASE), jnp.bfloat16),
            pltpu.SemaphoreType.DMA((PIECES + 1,)),
        ],
        compiler_params=pltpu.CompilerParams(vmem_limit_bytes=24 * 2**20),
        cost_estimate=pl.CostEstimate(flops=10**9, bytes_accessed=10 * 2**20, transcendentals=0),
        name="local_transform",
    )(own, other, pltpu.with_memory_space_constraint(had, pltpu.HBM))


def invert_kernel(group_ref, slots_ref, out_ref):
    lane = lax.broadcasted_iota(jnp.int32, (32, LANES), 1)
    even, odd = slots_ref[pl.ds(0, 32, stride=2), :], slots_ref[pl.ds(1, 32, stride=2), :]
    first = lane < CAP
    picks = jnp.where(first, even, pltpu.roll(odd, CAP, 1))
    owner = jnp.where(first, pltpu.roll(even, CAP, 1), odd)
    place = 2 * lax.broadcasted_iota(jnp.int32, (32, LANES), 0) + jnp.where(first, 0, 1)
    bf16 = lambda v: v.astype(jnp.float32).astype(jnp.bfloat16)
    high = bf16(jnp.where(owner >= 0, ((owner >> 5) & 1) * 128 + (owner >> 7), -1))
    low = bf16((owner & 7) * 8 + ((owner >> 6) & 1) * 4 + ((owner >> 3) & 3))
    values = bf16(picks & (BASE - 1)), bf16(picks >> 8), bf16(place + 1)
    high_at = bf16(lax.broadcasted_iota(jnp.int32, (256, LANES), 0))
    low_at = bf16(lax.broadcasted_iota(jnp.int32, (64, LANES), 0))
    one, zero = jnp.ones((), jnp.bfloat16), jnp.zeros((), jnp.bfloat16)
    total = jnp.zeros((192, 256), jnp.float32)
    for start in range(0, 32, 16):
        lhs, rhs = [], []
        for i in range(start, start + 16):
            at = lambda v: v[i : i + 1, :]
            rhs.append(jnp.where(at(high) == high_at, one, zero))
            hit = at(low) == low_at
            lhs.append(jnp.concatenate([jnp.where(hit, at(v), zero) for v in values], axis=0))
        total += lax.dot_general(
            jnp.concatenate(lhs, axis=1), jnp.concatenate(rhs, axis=1), NT, preferred_element_type=jnp.float32
        )
    base, fold, place = (total[i * 64 : (i + 1) * 64].astype(jnp.int32) for i in range(3))
    row = ((place - 1) * 8 + group_ref[0]) * ROWS_DEV + fold * BASE + base
    found = jnp.where(place > 0, row + 1, 0)
    for i in range(8):
        out_ref[i] = found[:, i % 2 * LANES : (i % 2 + 1) * LANES]


def invert(group, slots):
    return pl.pallas_call(
        invert_kernel,
        out_shape=jax.ShapeDtypeStruct((8, 64, LANES), jnp.int32),
        in_specs=[SMEM, VMEM],
        out_specs=VMEM,
        compiler_params=pltpu.CompilerParams(vmem_limit_bytes=8 * 2**20),
        cost_estimate=pl.CostEstimate(flops=4 * 10**8, bytes_accessed=2**19, transcendentals=0),
        name="invert_slots",
    )(group, slots)


def pick_kernel(
    me_ref, sources_ref, spread_ref, table_hbm, out_ref, table, where_vmem, signed, wide, sems, *where_smem
):
    table_copies = []
    for piece in range(PIECES):
        rows = table_rows(piece)
        table_copies.append(pltpu.make_async_copy(table_hbm.at[rows, :], table.at[rows, :], sems.at[8 + piece]))
        table_copies[-1].start()
    bf16 = lambda v: v.astype(jnp.float32).astype(jnp.bfloat16)
    source = sources_ref[0]
    for i in range(1, 8):
        source += sources_ref[i]
    source = source - 1
    device = source >> 13
    odd_bits = device & me_ref[0]
    for shift in (8, 4, 2, 1):
        odd_bits = odd_bits ^ (odd_bits >> shift)
    combo = ((source >> 12) & 1) * 4 + (device & 1) * 2 + ((device >> 1) & 1) + 1
    sub = lax.broadcasted_iota(jnp.int32, (64, 128), 0) % 8
    where_vmem[...] = (source & (HALF - 1)) + PAD - sub
    where_copies = [
        pltpu.make_async_copy(where_vmem.at[pl.ds(g * 8, 8), :], where_smem[g], sems.at[g]) for g in range(8)
    ]
    for copy in where_copies:
        copy.start()
    combo = bf16(jnp.where(odd_bits & 1 == 1, -combo, combo).T)
    for i in range(8):
        signed[pl.ds(i, 128, stride=8), :] = jnp.dot(
            combo, spread_ref[:, i * LANES : (i + 1) * LANES], preferred_element_type=jnp.float32
        )
    lane = lax.broadcasted_iota(jnp.int32, (8, LANES), 1)
    sub = lax.broadcasted_iota(jnp.int32, (8, LANES), 0)
    row_of = lane // PART
    lane_of = lane % PART - PART
    turn = lambda v, index: jnp.take_along_axis(v, index, axis=1, mode="promise_in_bounds")
    for copy in table_copies:
        copy.wait()
    for copy in where_copies:
        copy.wait()

    def gather(group, place):
        block = group * GROUPED + place
        rows = pl.ds(pl.multiple_of(block * 8, 8), 8)
        for g in range(8):
            at = lambda i: where_smem[g].at[i, pl.ds(place, LANES - GROUPED + 1)][group * GROUPED]
            value = table[pl.ds(at(0), 8), :]
            for i in range(1, 8):
                value = jnp.where(sub == i, table[pl.ds(at(i), 8), :], value)
            wide[rows, pl.ds(g * LANES, LANES)] = value

    def choose(block):
        rows = pl.ds(pl.multiple_of(block * 8, 8), 8)
        combo = signed[rows, :]
        index = lane_of + PART * jnp.abs(combo).astype(jnp.int32)
        out = turn(wide[rows, pl.ds(0, LANES)], index)
        for g in range(1, 8):
            out = jnp.where(row_of == g, turn(wide[rows, pl.ds(g * LANES, LANES)], index), out)
        out_ref[rows, :] = out * jnp.where(combo < 0, -SCALE, SCALE)

    def both(group, _):
        for i in range(GROUPED):
            choose((group - 1) * GROUPED + i)
        for i in range(GROUPED):
            gather(group, i)
        return 0

    groups = OUT_ROWS // 8 // GROUPED
    for i in range(GROUPED):
        gather(0, i)
    lax.fori_loop(1, groups, both, 0)
    for i in range(GROUPED):
        choose((groups - 1) * GROUPED + i)


def spread_np():
    column = np.arange(8 * LANES)
    return (np.arange(64)[:, None] == (column % LANES // PART * 8 + column // LANES)[None, :]).astype(np.float32)


def pick_columns(me, sources, table):
    return pl.pallas_call(
        pick_kernel,
        out_shape=jax.ShapeDtypeStruct((OUT_ROWS, LANES), jnp.float32),
        in_specs=[SMEM, VMEM, VMEM, HBM],
        out_specs=VMEM,
        scratch_shapes=[
            pltpu.VMEM((TABLE, LANES), jnp.float32),
            pltpu.VMEM((64, 128), jnp.int32),
            pltpu.VMEM((OUT_ROWS, LANES), jnp.float32),
            pltpu.VMEM((OUT_ROWS, 8 * LANES), jnp.float32),
            pltpu.SemaphoreType.DMA((8 + PIECES,)),
            *[pltpu.SMEM((8, 128), jnp.int32)] * 8,
        ],
        compiler_params=pltpu.CompilerParams(vmem_limit_bytes=24 * 2**20),
        cost_estimate=pl.CostEstimate(flops=10**8, bytes_accessed=10 * 2**20, transcendentals=0),
        name="pick_columns",
    )(
        me,
        sources,
        jnp.asarray(spread_np(), jnp.bfloat16),
        pltpu.with_memory_space_constraint(table, pltpu.HBM),
    )


def finish_kernel(parts_ref, chosen_ref, out_ref):
    totals = [parts_ref[pl.ds(i * 8, 8), :] for i in range(8)]
    for block in range(8, OUT_ROWS // 8):
        totals[block % 8] += parts_ref[pl.ds(block * 8, 8), :]
    while len(totals) > 1:
        totals = [low + high for low, high in zip(totals[::2], totals[1::2])]
    total = totals[0]
    group = lax.broadcasted_iota(jnp.int32, (8, LANES), 1) // PART == lax.broadcasted_iota(jnp.int32, (8, LANES), 0)
    spread = [jnp.where(group, jnp.broadcast_to(total[i : i + 1], (8, LANES)), 0.0) for i in range(8)]
    out = lax.dot_general(
        chosen_ref[...],
        jnp.concatenate(spread, axis=0),
        NT,
        precision=lax.Precision.HIGHEST,
        preferred_element_type=jnp.float32,
    )
    out_ref[pl.ds(0, PART), :] = out[:, :PANEL]
    out_ref[pl.ds(PART, PART), :] = out[:, PANEL:]


def finish(parts):
    chosen = (np.arange(PART)[:, None] == np.arange(LANES)[None, :] % PART).astype(np.float32)
    return pl.pallas_call(
        finish_kernel,
        out_shape=jax.ShapeDtypeStruct((PANEL, PANEL), jnp.float32),
        in_specs=[VMEM, VMEM],
        out_specs=VMEM,
        compiler_params=pltpu.CompilerParams(vmem_limit_bytes=4 * 2**20),
        cost_estimate=pl.CostEstimate(flops=10**6, bytes_accessed=2**19, transcendentals=0),
        name="finish",
    )(parts, jnp.asarray(chosen))


def prepare_kernel(
    side_ref, panel_hbm, sign_hbm, rows_hbm, owner_hbm, send_ref, own_ref, slots_hbm, panel, sign, rows, owner, slots_vmem, sems
):
    side = side_ref[0]
    half = lambda at: panel_hbm.at[pl.ds(pl.multiple_of(at * PART, PART), PART), :]
    copies = [
        pltpu.make_async_copy(source, target, sems.at[i])
        for i, (source, target) in enumerate(
            (
                (sign_hbm, sign),
                (half(1 - side), panel.at[0]),
                (half(side), panel.at[1]),
                (rows_hbm, rows),
                (owner_hbm, owner),
            )
        )
    ]
    for copy in copies[3:] + copies[:3]:
        copy.start()
    copies[3].wait()
    copies[4].wait()
    lane = lax.broadcasted_iota(jnp.int32, (8, LANES), 1)
    parts = [jnp.zeros((8, LANES), jnp.int32)] * 8
    for i in range(CAP):
        parts[i % 8] = jnp.where(lane == i, rows[i], parts[i % 8])
        parts[i % 8] = jnp.where(lane == CAP + i, owner[i], parts[i % 8])
    slots = parts[0]
    for part in parts[1:]:
        slots = slots + part
    for i in range(8):
        slots_vmem[pl.ds(i * 8, 8), :] = slots
    slots_copy = pltpu.make_async_copy(slots_vmem, slots_hbm, sems.at[5])
    slots_copy.start()
    copies[0].wait()
    for at, out_ref in enumerate((send_ref, own_ref)):
        copies[1 + at].wait()
        for block in range(ROWS_DEV // LANES):
            lanes = pl.ds(block * LANES, LANES)
            factor = (1 - 2 * sign[pl.ds(block, 1), :]).astype(jnp.float32)
            out_ref[:, lanes] = panel[at, :, lanes] * factor
    slots_copy.wait()


def prepare(side, hidden_panel, sign_bits, pick_rows, pick_owner):
    half = jax.ShapeDtypeStruct((PART, ROWS_DEV), jnp.float32)
    return pl.pallas_call(
        prepare_kernel,
        out_shape=(half, half, pltpu.HBM((64, LANES), jnp.int32)),
        in_specs=[SMEM, HBM, HBM, HBM, HBM],
        out_specs=(VMEM, VMEM, HBM),
        scratch_shapes=[
            pltpu.VMEM((2, PART, ROWS_DEV), jnp.float32),
            pltpu.VMEM((ROWS_DEV // LANES, LANES), jnp.int32),
            pltpu.SMEM((CAP,), jnp.int32),
            pltpu.SMEM((CAP,), jnp.int32),
            pltpu.VMEM((64, LANES), jnp.int32),
            pltpu.SemaphoreType.DMA((6,)),
        ],
        compiler_params=pltpu.CompilerParams(vmem_limit_bytes=8 * 2**20),
        cost_estimate=pl.CostEstimate(flops=10**6, bytes_accessed=2**21, transcendentals=0),
        name="prepare",
    )(
        side,
        pltpu.with_memory_space_constraint(hidden_panel, pltpu.HBM),
        pltpu.with_memory_space_constraint(sign_bits.reshape(ROWS_DEV // LANES, LANES), pltpu.HBM),
        pltpu.with_memory_space_constraint(pick_rows, pltpu.HBM),
        pltpu.with_memory_space_constraint(pick_owner, pltpu.HBM),
    )


def local(hidden_panel, sign_bits, pick_rows, pick_owner):
    me = ((lax.axis_index("gx") * 8 + lax.axis_index("gy")) * 4 + lax.axis_index("x")) * 2 + lax.axis_index("core")
    side = (lax.axis_index("x") % 2).reshape(1).astype(jnp.int32)
    send, own, slots = prepare(side, hidden_panel, sign_bits, pick_rows, pick_owner)
    near = lax.ppermute(send, "x", [(i, i ^ 1) for i in range(4)])
    first_slots = lax.all_to_all(
        slots.reshape(64, 1, LANES), ("gx", "gy"), split_axis=0, concat_axis=0, tiled=True
    )
    sources = invert((me % 8).reshape(1).astype(jnp.int32), first_slots.reshape(64, LANES))
    own = join(own, near, sources)
    sources = lax.all_to_all(sources, ("x", "core"), split_axis=0, concat_axis=0, tiled=True)
    table = make_table(own, lax.ppermute(own, "core", [(0, 1), (1, 0)]))
    columns = pick_columns(me.reshape(1).astype(jnp.int32), sources, table)
    columns = lax.all_to_all(
        columns.reshape(CHIPS, 4, LANES), ("gx", "gy", "x"), split_axis=0, concat_axis=0, tiled=True
    )
    return finish(columns.reshape(OUT_ROWS, LANES))


def solution(mesh):
    inner = Mesh(mesh.devices.reshape(8, 8, 4, 2), ("gx", "gy", "x", "core"))
    rows = ("gx", "gy", "x", "core")
    return jax.shard_map(
        local,
        mesh=inner,
        in_specs=(P(None, rows), P(rows), P(rows), P(rows)),
        out_specs=P(None, rows),
        check_vma=False,
    )
```

```python
import jax
import jax.numpy as jnp
import numpy as np
from jax import lax
from jax.experimental import pallas as pl
from jax.experimental.pallas import tpu as pltpu
from jax.sharding import Mesh, PartitionSpec as P

PANEL = 32
ROWS_DEV = 8192
CAP = 64
DEVS = 512
PART = PANEL // 2
SOURCES = 4
BASE = 256
FOLDS = ROWS_DEV // BASE
PAD = 8
HALF = ROWS_DEV // 2
TABLE = HALF + 2 * PAD
LANES = 128
CHIPS = 256
OUT_ROWS = 4 * CHIPS
GROUPED = 8
PIECES = FOLDS // 4
SCALE = 2.0**-11
NT = (((1,), (1,)), ((), ()))
VMEM, SMEM, HBM = (pl.BlockSpec(memory_space=m) for m in (pltpu.VMEM, pltpu.SMEM, pltpu.HBM))


def hadamard_np(order):
    matrix = np.ones((1, 1), np.float32)
    while matrix.shape[0] < order:
        matrix = np.block([[matrix, matrix], [matrix, -matrix]])
    return matrix


def butterflies(parts):
    half = 1
    while half < len(parts):
        for start in range(0, len(parts), 2 * half):
            for i in range(start, start + half):
                low, high = parts[i], parts[i + half]
                parts[i], parts[i + half] = low + high, low - high
        half *= 2
    return parts


def join_kernel(own_ref, near_ref, sources_ref, out_ref):
    out_ref[0] = own_ref[...]
    out_ref[1] = near_ref[...]


def join(own, near, sources):
    return pl.pallas_call(
        join_kernel,
        out_shape=jax.ShapeDtypeStruct((2, PART, ROWS_DEV), jnp.float32),
        in_specs=[VMEM, VMEM, HBM],
        out_specs=VMEM,
        compiler_params=pltpu.CompilerParams(vmem_limit_bytes=8 * 2**20),
        cost_estimate=pl.CostEstimate(flops=0, bytes_accessed=2**21, transcendentals=0),
        name="join_halves",
    )(own, near, sources)


def table_kernel(own_ref, other_hbm, had_hbm, table, mixed, other_ref, had_ref, sems):
    other_copy = pltpu.make_async_copy(other_hbm, other_ref, sems.at[0])
    other_copy.start()
    had_copy = pltpu.make_async_copy(had_hbm, had_ref, sems.at[1])
    had_copy.start()
    for source, (ref, chip) in enumerate((ref, chip) for ref in (own_ref, other_ref) for chip in range(2)):
        if source == 2:
            other_copy.wait()

        def fold_rows(step, _, ref=ref, chip=chip, source=source):
            group, half = step // 2, step % 2
            rows = pl.ds(pl.multiple_of(group * 8, 8), 8)
            column = half * LANES
            parts = [ref[chip, rows, pl.ds(pl.multiple_of(fold * BASE + column, LANES), LANES)] for fold in range(FOLDS)]
            out_rows = pl.ds(pl.multiple_of(source * PART + group * 8, 8), 8)
            for fold, part in enumerate(butterflies(parts)):
                mixed[fold, out_rows, pl.ds(pl.multiple_of(column, LANES), LANES)] = part
            return 0

        lax.fori_loop(0, PART // 8 * 2, fold_rows, 0)

    had_copy.wait()
    edge = jnp.zeros((PAD, LANES), jnp.float32)
    table[pl.ds(0, PAD), :] = edge
    table[pl.ds(TABLE - PAD, PAD), :] = edge

    def transform(piece):
        highs, middles, lows = [], [], []
        for fold in (2 * piece, 2 * piece + FOLDS // 2, 2 * piece + 1, 2 * piece + 1 + FOLDS // 2):
            block = jnp.concatenate(
                butterflies([mixed[fold, pl.ds(source * PART, PART), :] for source in range(SOURCES)]), axis=0
            )
            highs.append(block.astype(jnp.bfloat16))
            rest = block - highs[-1].astype(jnp.float32)
            middles.append(rest.astype(jnp.bfloat16))
            lows.append((rest - middles[-1].astype(jnp.float32)).astype(jnp.bfloat16))
        out = jnp.zeros((BASE, 2 * LANES), jnp.float32)
        for pieces in (lows, middles, highs):
            out += lax.dot_general(
                had_ref[...], jnp.concatenate(pieces, axis=0), NT, preferred_element_type=jnp.float32
            )
        for i in range(2):
            table[pl.ds((2 * piece + i) * BASE + PAD, BASE), :] = out[:, i * LANES : (i + 1) * LANES]

    for piece in range(PIECES):
        transform(piece)


def make_table(own, other):
    had = jnp.asarray(hadamard_np(BASE), jnp.bfloat16)
    return pl.pallas_call(
        table_kernel,
        out_shape=jax.ShapeDtypeStruct((TABLE, LANES), jnp.float32),
        in_specs=[VMEM, HBM, HBM],
        out_specs=VMEM,
        scratch_shapes=[
            pltpu.VMEM((FOLDS, SOURCES * PART, BASE), jnp.float32),
            pltpu.VMEM((2, PART, ROWS_DEV), jnp.float32),
            pltpu.VMEM((BASE, BASE), jnp.bfloat16),
            pltpu.SemaphoreType.DMA((2,)),
        ],
        compiler_params=pltpu.CompilerParams(vmem_limit_bytes=24 * 2**20),
        cost_estimate=pl.CostEstimate(flops=10**9, bytes_accessed=10 * 2**20, transcendentals=0),
        name="local_transform",
    )(own, *(pltpu.with_memory_space_constraint(v, pltpu.HBM) for v in (other, had)))


def invert_kernel(group_ref, slots_ref, out_ref):
    lane = lax.broadcasted_iota(jnp.int32, (32, LANES), 1)
    even, odd = slots_ref[pl.ds(0, 32, stride=2), :], slots_ref[pl.ds(1, 32, stride=2), :]
    first = lane < CAP
    picks = jnp.where(first, even, pltpu.roll(odd, CAP, 1))
    owner = jnp.where(first, pltpu.roll(even, CAP, 1), odd)
    place = 2 * lax.broadcasted_iota(jnp.int32, (32, LANES), 0) + jnp.where(first, 0, 1)
    bf16 = lambda v: v.astype(jnp.float32).astype(jnp.bfloat16)
    high = bf16(jnp.where(owner >= 0, ((owner >> 5) & 1) * 128 + (owner >> 7), -1))
    low = bf16((owner & 7) * 8 + ((owner >> 6) & 1) * 4 + ((owner >> 3) & 3))
    values = bf16(picks & (BASE - 1)), bf16(picks >> 8), bf16(place + 1)
    high_at = bf16(lax.broadcasted_iota(jnp.int32, (256, LANES), 0))
    low_at = bf16(lax.broadcasted_iota(jnp.int32, (64, LANES), 0))
    one, zero = jnp.ones((), jnp.bfloat16), jnp.zeros((), jnp.bfloat16)
    total = jnp.zeros((192, 256), jnp.float32)
    for start in range(0, 32, 16):
        lhs, rhs = [], []
        for i in range(start, start + 16):
            at = lambda v: v[i : i + 1, :]
            rhs.append(jnp.where(at(high) == high_at, one, zero))
            hit = at(low) == low_at
            lhs.append(jnp.concatenate([jnp.where(hit, at(v), zero) for v in values], axis=0))
        total += lax.dot_general(
            jnp.concatenate(lhs, axis=1), jnp.concatenate(rhs, axis=1), NT, preferred_element_type=jnp.float32
        )
    base, fold, place = (total[i * 64 : (i + 1) * 64].astype(jnp.int32) for i in range(3))
    row = ((place - 1) * 8 + group_ref[0]) * ROWS_DEV + fold * BASE + base
    found = jnp.where(place > 0, row + 1, 0)
    for i in range(8):
        out_ref[i] = found[:, i % 2 * LANES : (i % 2 + 1) * LANES]


def invert(group, slots):
    return pl.pallas_call(
        invert_kernel,
        out_shape=jax.ShapeDtypeStruct((8, 64, LANES), jnp.int32),
        in_specs=[SMEM, VMEM],
        out_specs=VMEM,
        compiler_params=pltpu.CompilerParams(vmem_limit_bytes=8 * 2**20),
        cost_estimate=pl.CostEstimate(flops=4 * 10**8, bytes_accessed=2**19, transcendentals=0),
        name="invert_slots",
    )(group, slots)


def pick_kernel(
    me_ref, sources_ref, spread_ref, table, out_ref, where_vmem, signed, wide, sems, *where_smem
):
    bf16 = lambda v: v.astype(jnp.float32).astype(jnp.bfloat16)
    source = sources_ref[0]
    for i in range(1, 8):
        source += sources_ref[i]
    source = source - 1
    device = source >> 13
    odd_bits = device & me_ref[0]
    for shift in (8, 4, 2, 1):
        odd_bits = odd_bits ^ (odd_bits >> shift)
    combo = ((source >> 12) & 1) * 4 + (device & 1) * 2 + ((device >> 1) & 1) + 1
    sub = lax.broadcasted_iota(jnp.int32, (64, 128), 0) % 8
    where_vmem[...] = (source & (HALF - 1)) + PAD - sub
    where_copies = [
        pltpu.make_async_copy(where_vmem.at[pl.ds(g * 8, 8), :], where_smem[g], sems.at[g]) for g in range(8)
    ]
    for copy in where_copies:
        copy.start()
    combo = bf16(jnp.where(odd_bits & 1 == 1, -combo, combo).T)
    for i in range(8):
        signed[pl.ds(i, 128, stride=8), :] = jnp.dot(
            combo, spread_ref[:, i * LANES : (i + 1) * LANES], preferred_element_type=jnp.float32
        )
    lane = lax.broadcasted_iota(jnp.int32, (8, LANES), 1)
    sub = lax.broadcasted_iota(jnp.int32, (8, LANES), 0)
    row_of = lane // PART
    lane_of = lane % PART - PART
    turn = lambda v, index: jnp.take_along_axis(v, index, axis=1, mode="promise_in_bounds")
    for copy in where_copies:
        copy.wait()

    def gather(group, place):
        block = group * GROUPED + place
        rows = pl.ds(pl.multiple_of(block * 8, 8), 8)
        for g in range(8):
            at = lambda i: where_smem[g].at[i, pl.ds(place, LANES - GROUPED + 1)][group * GROUPED]
            value = table[pl.ds(at(0), 8), :]
            for i in range(1, 8):
                value = jnp.where(sub == i, table[pl.ds(at(i), 8), :], value)
            wide[rows, pl.ds(g * LANES, LANES)] = value

    def choose(block):
        rows = pl.ds(pl.multiple_of(block * 8, 8), 8)
        combo = signed[rows, :]
        index = lane_of + PART * jnp.abs(combo).astype(jnp.int32)
        out = turn(wide[rows, pl.ds(0, LANES)], index)
        for g in range(1, 8):
            out = jnp.where(row_of == g, turn(wide[rows, pl.ds(g * LANES, LANES)], index), out)
        out_ref[rows, :] = out * jnp.where(combo < 0, -SCALE, SCALE)

    def both(group, _):
        for i in range(GROUPED):
            choose((group - 1) * GROUPED + i)
        for i in range(GROUPED):
            gather(group, i)
        return 0

    groups = OUT_ROWS // 8 // GROUPED
    for i in range(GROUPED):
        gather(0, i)
    lax.fori_loop(1, groups, both, 0)
    for i in range(GROUPED):
        choose((groups - 1) * GROUPED + i)


def spread_np():
    column = np.arange(8 * LANES)
    return (np.arange(64)[:, None] == (column % LANES // PART * 8 + column // LANES)[None, :]).astype(np.float32)


def pick_columns(me, sources, table):
    return pl.pallas_call(
        pick_kernel,
        out_shape=jax.ShapeDtypeStruct((OUT_ROWS, LANES), jnp.float32),
        in_specs=[SMEM, VMEM, VMEM, VMEM],
        out_specs=VMEM,
        scratch_shapes=[
            pltpu.VMEM((64, 128), jnp.int32),
            pltpu.VMEM((OUT_ROWS, LANES), jnp.float32),
            pltpu.VMEM((OUT_ROWS, 8 * LANES), jnp.float32),
            pltpu.SemaphoreType.DMA((8,)),
            *[pltpu.SMEM((8, 128), jnp.int32)] * 8,
        ],
        compiler_params=pltpu.CompilerParams(vmem_limit_bytes=24 * 2**20),
        cost_estimate=pl.CostEstimate(flops=10**8, bytes_accessed=10 * 2**20, transcendentals=0),
        name="pick_columns",
    )(
        me,
        sources,
        jnp.asarray(spread_np(), jnp.bfloat16),
        table,
    )


def finish_kernel(parts_ref, chosen_ref, out_ref):
    totals = [parts_ref[pl.ds(i * 8, 8), :] for i in range(8)]
    for block in range(8, OUT_ROWS // 8):
        totals[block % 8] += parts_ref[pl.ds(block * 8, 8), :]
    while len(totals) > 1:
        totals = [low + high for low, high in zip(totals[::2], totals[1::2])]
    total = totals[0]
    group = lax.broadcasted_iota(jnp.int32, (8, LANES), 1) // PART == lax.broadcasted_iota(jnp.int32, (8, LANES), 0)
    spread = [jnp.where(group, jnp.broadcast_to(total[i : i + 1], (8, LANES)), 0.0) for i in range(8)]
    out = lax.dot_general(
        chosen_ref[...],
        jnp.concatenate(spread, axis=0),
        NT,
        precision=lax.Precision.HIGHEST,
        preferred_element_type=jnp.float32,
    )
    out_ref[pl.ds(0, PART), :] = out[:, :PANEL]
    out_ref[pl.ds(PART, PART), :] = out[:, PANEL:]


def finish(parts):
    chosen = (np.arange(PART)[:, None] == np.arange(LANES)[None, :] % PART).astype(np.float32)
    return pl.pallas_call(
        finish_kernel,
        out_shape=jax.ShapeDtypeStruct((PANEL, PANEL), jnp.float32),
        in_specs=[VMEM, VMEM],
        out_specs=VMEM,
        compiler_params=pltpu.CompilerParams(vmem_limit_bytes=4 * 2**20),
        cost_estimate=pl.CostEstimate(flops=10**6, bytes_accessed=2**19, transcendentals=0),
        name="finish",
    )(parts, jnp.asarray(chosen))


def prepare_kernel(
    side_ref, panel_hbm, sign_hbm, rows_hbm, owner_hbm, send_ref, own_ref, slots_hbm, panel, sign, rows, owner, slots_vmem, sems
):
    side = side_ref[0]
    half = lambda at: panel_hbm.at[pl.ds(pl.multiple_of(at * PART, PART), PART), :]
    copies = [
        pltpu.make_async_copy(source, target, sems.at[i])
        for i, (source, target) in enumerate(
            (
                (sign_hbm, sign),
                (half(1 - side), panel.at[0]),
                (half(side), panel.at[1]),
                (rows_hbm, rows),
                (owner_hbm, owner),
            )
        )
    ]
    for copy in copies[3:] + copies[:3]:
        copy.start()
    copies[3].wait()
    copies[4].wait()
    lane = lax.broadcasted_iota(jnp.int32, (8, LANES), 1)
    parts = [jnp.zeros((8, LANES), jnp.int32)] * 8
    for i in range(CAP):
        parts[i % 8] = jnp.where(lane == i, rows[i], parts[i % 8])
        parts[i % 8] = jnp.where(lane == CAP + i, owner[i], parts[i % 8])
    slots = parts[0]
    for part in parts[1:]:
        slots = slots + part
    for i in range(8):
        slots_vmem[pl.ds(i * 8, 8), :] = slots
    slots_copy = pltpu.make_async_copy(slots_vmem, slots_hbm, sems.at[5])
    slots_copy.start()
    copies[0].wait()
    for at, out_ref in enumerate((send_ref, own_ref)):
        copies[1 + at].wait()
        for block in range(ROWS_DEV // LANES):
            lanes = pl.ds(block * LANES, LANES)
            factor = (1 - 2 * sign[pl.ds(block, 1), :]).astype(jnp.float32)
            out_ref[:, lanes] = panel[at, :, lanes] * factor
    slots_copy.wait()


def prepare(side, hidden_panel, sign_bits, pick_rows, pick_owner):
    half = jax.ShapeDtypeStruct((PART, ROWS_DEV), jnp.float32)
    return pl.pallas_call(
        prepare_kernel,
        out_shape=(half, half, pltpu.HBM((64, LANES), jnp.int32)),
        in_specs=[SMEM, HBM, HBM, HBM, HBM],
        out_specs=(VMEM, VMEM, HBM),
        scratch_shapes=[
            pltpu.VMEM((2, PART, ROWS_DEV), jnp.float32),
            pltpu.VMEM((ROWS_DEV // LANES, LANES), jnp.int32),
            pltpu.SMEM((CAP,), jnp.int32),
            pltpu.SMEM((CAP,), jnp.int32),
            pltpu.VMEM((64, LANES), jnp.int32),
            pltpu.SemaphoreType.DMA((6,)),
        ],
        compiler_params=pltpu.CompilerParams(vmem_limit_bytes=8 * 2**20),
        cost_estimate=pl.CostEstimate(flops=10**6, bytes_accessed=2**21, transcendentals=0),
        name="prepare",
    )(
        side,
        pltpu.with_memory_space_constraint(hidden_panel, pltpu.HBM),
        pltpu.with_memory_space_constraint(sign_bits.reshape(ROWS_DEV // LANES, LANES), pltpu.HBM),
        pltpu.with_memory_space_constraint(pick_rows, pltpu.HBM),
        pltpu.with_memory_space_constraint(pick_owner, pltpu.HBM),
    )


def local(hidden_panel, sign_bits, pick_rows, pick_owner):
    me = ((lax.axis_index("gx") * 8 + lax.axis_index("gy")) * 4 + lax.axis_index("x")) * 2 + lax.axis_index("core")
    side = (lax.axis_index("x") % 2).reshape(1).astype(jnp.int32)
    send, own, slots = prepare(side, hidden_panel, sign_bits, pick_rows, pick_owner)
    near = lax.ppermute(send, "x", [(i, i ^ 1) for i in range(4)])
    first_slots = lax.all_to_all(
        slots.reshape(64, 1, LANES), ("gx", "gy"), split_axis=0, concat_axis=0, tiled=True
    )
    sources = invert((me % 8).reshape(1).astype(jnp.int32), first_slots.reshape(64, LANES))
    own = join(own, near, sources)
    sources = lax.all_to_all(sources, ("x", "core"), split_axis=0, concat_axis=0, tiled=True)
    table = make_table(own, lax.ppermute(own, "core", [(0, 1), (1, 0)]))
    columns = pick_columns(me.reshape(1).astype(jnp.int32), sources, table)
    columns = lax.all_to_all(
        columns.reshape(CHIPS, 4, LANES), ("gx", "gy", "x"), split_axis=0, concat_axis=0, tiled=True
    )
    return finish(columns.reshape(OUT_ROWS, LANES))


def solution(mesh):
    inner = Mesh(mesh.devices.reshape(8, 8, 4, 2), ("gx", "gy", "x", "core"))
    rows = ("gx", "gy", "x", "core")
    return jax.shard_map(
        local,
        mesh=inner,
        in_specs=(P(None, rows), P(rows), P(rows), P(rows)),
        out_specs=P(None, rows),
        check_vma=False,
    )
```

```python
import jax
import jax.numpy as jnp
import numpy as np
from jax import lax
from jax.experimental import pallas as pl
from jax.experimental.pallas import tpu as pltpu
from jax.sharding import Mesh, PartitionSpec as P

PANEL = 32
ROWS_DEV = 8192
CAP = 64
DEVS = 512
PART = PANEL // 2
SOURCES = 4
BASE = 256
FOLDS = ROWS_DEV // BASE
PAD = 8
HALF = ROWS_DEV // 2
TABLE = HALF + 2 * PAD
LANES = 128
CHIPS = 256
OUT_ROWS = 4 * CHIPS
GROUPED = 8
PIECES = FOLDS // 4
SCALE = 2.0**-11
NT = (((1,), (1,)), ((), ()))
VMEM, SMEM, HBM = (pl.BlockSpec(memory_space=m) for m in (pltpu.VMEM, pltpu.SMEM, pltpu.HBM))


def hadamard_np(order):
    matrix = np.ones((1, 1), np.float32)
    while matrix.shape[0] < order:
        matrix = np.block([[matrix, matrix], [matrix, -matrix]])
    return matrix


def butterflies(parts):
    half = 1
    while half < len(parts):
        for start in range(0, len(parts), 2 * half):
            for i in range(start, start + half):
                low, high = parts[i], parts[i + half]
                parts[i], parts[i + half] = low + high, low - high
        half *= 2
    return parts


def join_kernel(own_ref, near_ref, sources_ref, out_ref):
    out_ref[0] = own_ref[...]
    out_ref[1] = near_ref[...]


def join(own, near, sources):
    return pl.pallas_call(
        join_kernel,
        out_shape=jax.ShapeDtypeStruct((2, PART, ROWS_DEV), jnp.float32),
        in_specs=[VMEM, VMEM, HBM],
        out_specs=VMEM,
        compiler_params=pltpu.CompilerParams(vmem_limit_bytes=8 * 2**20),
        cost_estimate=pl.CostEstimate(flops=0, bytes_accessed=2**21, transcendentals=0),
        name="join_halves",
    )(own, near, sources)


def table_kernel(own_ref, other_hbm, had_hbm, table, mixed, other_ref, had_ref, sems):
    other_copy = pltpu.make_async_copy(other_hbm, other_ref, sems.at[0])
    other_copy.start()
    had_copy = pltpu.make_async_copy(had_hbm, had_ref, sems.at[1])
    had_copy.start()
    for source, (ref, chip) in enumerate((ref, chip) for ref in (own_ref, other_ref) for chip in range(2)):
        if source == 2:
            other_copy.wait()

        def fold_rows(step, _, ref=ref, chip=chip, source=source):
            group, half = step // 2, step % 2
            rows = pl.ds(pl.multiple_of(group * 8, 8), 8)
            column = half * LANES
            parts = [ref[chip, rows, pl.ds(pl.multiple_of(fold * BASE + column, LANES), LANES)] for fold in range(FOLDS)]
            out_rows = pl.ds(pl.multiple_of(source * PART + group * 8, 8), 8)
            for fold, part in enumerate(butterflies(parts)):
                mixed[fold, out_rows, pl.ds(pl.multiple_of(column, LANES), LANES)] = part
            return 0

        lax.fori_loop(0, PART // 8 * 2, fold_rows, 0)

    had_copy.wait()
    edge = jnp.zeros((PAD, LANES), jnp.float32)
    table[pl.ds(0, PAD), :] = edge
    table[pl.ds(TABLE - PAD, PAD), :] = edge

    def transform(piece):
        highs, middles, lows = [], [], []
        for fold in (2 * piece, 2 * piece + FOLDS // 2, 2 * piece + 1, 2 * piece + 1 + FOLDS // 2):
            block = jnp.concatenate(
                butterflies([mixed[fold, pl.ds(source * PART, PART), :] for source in range(SOURCES)]), axis=0
            )
            highs.append(block.astype(jnp.bfloat16))
            rest = block - highs[-1].astype(jnp.float32)
            middles.append(rest.astype(jnp.bfloat16))
            lows.append((rest - middles[-1].astype(jnp.float32)).astype(jnp.bfloat16))
        out = jnp.zeros((BASE, 2 * LANES), jnp.float32)
        for pieces in (lows, middles, highs):
            out += lax.dot_general(
                had_ref[...], jnp.concatenate(pieces, axis=0), NT, preferred_element_type=jnp.float32
            )
        for i in range(2):
            table[pl.ds((2 * piece + i) * BASE + PAD, BASE), :] = out[:, i * LANES : (i + 1) * LANES]

    for piece in range(PIECES):
        transform(piece)


def make_table(own, other):
    had = jnp.asarray(hadamard_np(BASE), jnp.bfloat16)
    return pl.pallas_call(
        table_kernel,
        out_shape=jax.ShapeDtypeStruct((TABLE, LANES), jnp.float32),
        in_specs=[VMEM, HBM, HBM],
        out_specs=VMEM,
        scratch_shapes=[
            pltpu.VMEM((FOLDS, SOURCES * PART, BASE), jnp.float32),
            pltpu.VMEM((2, PART, ROWS_DEV), jnp.float32),
            pltpu.VMEM((BASE, BASE), jnp.bfloat16),
            pltpu.SemaphoreType.DMA((2,)),
        ],
        compiler_params=pltpu.CompilerParams(vmem_limit_bytes=24 * 2**20),
        cost_estimate=pl.CostEstimate(flops=10**9, bytes_accessed=10 * 2**20, transcendentals=0),
        name="local_transform",
    )(own, *(pltpu.with_memory_space_constraint(v, pltpu.HBM) for v in (other, had)))


def invert_kernel(group_ref, slots_ref, out_ref):
    lane = lax.broadcasted_iota(jnp.int32, (32, LANES), 1)
    even, odd = slots_ref[pl.ds(0, 32, stride=2), :], slots_ref[pl.ds(1, 32, stride=2), :]
    first = lane < CAP
    picks = jnp.where(first, even, pltpu.roll(odd, CAP, 1))
    owner = jnp.where(first, pltpu.roll(even, CAP, 1), odd)
    place = 2 * lax.broadcasted_iota(jnp.int32, (32, LANES), 0) + jnp.where(first, 0, 1)
    bf16 = lambda v: v.astype(jnp.float32).astype(jnp.bfloat16)
    high = bf16(jnp.where(owner >= 0, ((owner >> 5) & 1) * 128 + (owner >> 7), -1))
    low = bf16((owner & 7) * 8 + ((owner >> 6) & 1) * 4 + ((owner >> 3) & 3))
    values = bf16(picks & (BASE - 1)), bf16(picks >> 8), bf16(place + 1)
    high_at = bf16(lax.broadcasted_iota(jnp.int32, (256, LANES), 0))
    low_at = bf16(lax.broadcasted_iota(jnp.int32, (64, LANES), 0))
    one, zero = jnp.ones((), jnp.bfloat16), jnp.zeros((), jnp.bfloat16)
    total = jnp.zeros((192, 256), jnp.float32)
    for start in range(0, 32, 16):
        lhs, rhs = [], []
        for i in range(start, start + 16):
            at = lambda v: v[i : i + 1, :]
            rhs.append(jnp.where(at(high) == high_at, one, zero))
            hit = at(low) == low_at
            lhs.append(jnp.concatenate([jnp.where(hit, at(v), zero) for v in values], axis=0))
        total += lax.dot_general(
            jnp.concatenate(lhs, axis=1), jnp.concatenate(rhs, axis=1), NT, preferred_element_type=jnp.float32
        )
    base, fold, place = (total[i * 64 : (i + 1) * 64].astype(jnp.int32) for i in range(3))
    row = ((place - 1) * 8 + group_ref[0]) * ROWS_DEV + fold * BASE + base
    found = jnp.where(place > 0, row + 1, 0)
    for i in range(8):
        out_ref[i] = found[:, i % 2 * LANES : (i % 2 + 1) * LANES]


def invert(group, slots):
    return pl.pallas_call(
        invert_kernel,
        out_shape=jax.ShapeDtypeStruct((8, 64, LANES), jnp.int32),
        in_specs=[SMEM, VMEM],
        out_specs=VMEM,
        compiler_params=pltpu.CompilerParams(vmem_limit_bytes=8 * 2**20),
        cost_estimate=pl.CostEstimate(flops=4 * 10**8, bytes_accessed=2**19, transcendentals=0),
        name="invert_slots",
    )(group, slots)


def pick_kernel(
    me_ref, sources_ref, spread_ref, table, out_ref, where_vmem, signed, wide, where_smem, sems
):
    bf16 = lambda v: v.astype(jnp.float32).astype(jnp.bfloat16)
    source = sources_ref[0]
    for i in range(1, 8):
        source += sources_ref[i]
    source = source - 1
    device = source >> 13
    odd_bits = device & me_ref[0]
    for shift in (8, 4, 2, 1):
        odd_bits = odd_bits ^ (odd_bits >> shift)
    combo = ((source >> 12) & 1) * 4 + (device & 1) * 2 + ((device >> 1) & 1) + 1
    sub = lax.broadcasted_iota(jnp.int32, (64, 128), 0) % 8
    where = ((source & (HALF - 1)) + PAD - sub).T
    where_vmem[...] = jnp.concatenate([where[:64], where[64:]], axis=1)
    where_copies = []
    for i, rows in enumerate((pl.ds(0, 16), pl.ds(16, 48))):
        where_copies.append(pltpu.make_async_copy(where_vmem.at[rows, :], where_smem.at[rows, :], sems.at[i]))
        where_copies[-1].start()
    combo = bf16(jnp.where(odd_bits & 1 == 1, -combo, combo).T)
    for i in range(8):
        signed[pl.ds(i, 128, stride=8), :] = jnp.dot(
            combo, spread_ref[:, i * LANES : (i + 1) * LANES], preferred_element_type=jnp.float32
        )
    lane = lax.broadcasted_iota(jnp.int32, (8, LANES), 1)
    sub = lax.broadcasted_iota(jnp.int32, (8, LANES), 0)
    row_of = lane // PART
    lane_of = lane % PART - PART
    turn = lambda v, index: jnp.take_along_axis(v, index, axis=1, mode="promise_in_bounds")

    first_of = lambda group: (group & 1) * 64 + (group >> 1) * GROUPED

    def gather(group, place):
        block = first_of(group) + place
        rows = pl.ds(pl.multiple_of(block * 8, 8), 8)
        for g in range(8):
            at = lambda i: where_smem.at[pl.ds(place, 57), pl.ds(8 * g + i, 65)][(group >> 1) * GROUPED, (group & 1) * 64]
            value = table[pl.ds(at(0), 8), :]
            for i in range(1, 8):
                value = jnp.where(sub == i, table[pl.ds(at(i), 8), :], value)
            wide[rows, pl.ds(g * LANES, LANES)] = value

    def choose(block):
        rows = pl.ds(pl.multiple_of(block * 8, 8), 8)
        combo = signed[rows, :]
        index = lane_of + PART * jnp.abs(combo).astype(jnp.int32)
        out = turn(wide[rows, pl.ds(0, LANES)], index)
        for g in range(1, 8):
            out = jnp.where(row_of == g, turn(wide[rows, pl.ds(g * LANES, LANES)], index), out)
        out_ref[rows, :] = out * jnp.where(combo < 0, -SCALE, SCALE)

    def both(group, _):
        for i in range(GROUPED):
            choose(first_of(group - 1) + i)
        for i in range(GROUPED):
            gather(group, i)
        return 0

    groups = OUT_ROWS // 8 // GROUPED
    where_copies[0].wait()
    for i in range(GROUPED):
        gather(0, i)
    lax.fori_loop(1, 4, both, 0)
    where_copies[1].wait()
    lax.fori_loop(4, groups, both, 0)
    for i in range(GROUPED):
        choose(first_of(groups - 1) + i)


def spread_np():
    column = np.arange(8 * LANES)
    return (np.arange(64)[:, None] == (column % LANES // PART * 8 + column // LANES)[None, :]).astype(np.float32)


def pick_columns(me, sources, table):
    return pl.pallas_call(
        pick_kernel,
        out_shape=jax.ShapeDtypeStruct((OUT_ROWS, LANES), jnp.float32),
        in_specs=[SMEM, VMEM, VMEM, VMEM],
        out_specs=VMEM,
        scratch_shapes=[
            pltpu.VMEM((64, 128), jnp.int32),
            pltpu.VMEM((OUT_ROWS, LANES), jnp.float32),
            pltpu.VMEM((OUT_ROWS, 8 * LANES), jnp.float32),
            pltpu.SMEM((64, 128), jnp.int32),
            pltpu.SemaphoreType.DMA((2,)),
        ],
        compiler_params=pltpu.CompilerParams(vmem_limit_bytes=24 * 2**20),
        cost_estimate=pl.CostEstimate(flops=10**8, bytes_accessed=10 * 2**20, transcendentals=0),
        name="pick_columns",
    )(
        me,
        sources,
        jnp.asarray(spread_np(), jnp.bfloat16),
        table,
    )


def finish_kernel(parts_ref, chosen_ref, out_ref):
    totals = [parts_ref[pl.ds(i * 8, 8), :] for i in range(8)]
    for block in range(8, OUT_ROWS // 8):
        totals[block % 8] += parts_ref[pl.ds(block * 8, 8), :]
    while len(totals) > 1:
        totals = [low + high for low, high in zip(totals[::2], totals[1::2])]
    total = totals[0]
    group = lax.broadcasted_iota(jnp.int32, (8, LANES), 1) // PART == lax.broadcasted_iota(jnp.int32, (8, LANES), 0)
    spread = [jnp.where(group, jnp.broadcast_to(total[i : i + 1], (8, LANES)), 0.0) for i in range(8)]
    out = lax.dot_general(
        chosen_ref[...],
        jnp.concatenate(spread, axis=0),
        NT,
        precision=lax.Precision.HIGHEST,
        preferred_element_type=jnp.float32,
    )
    out_ref[pl.ds(0, PART), :] = out[:, :PANEL]
    out_ref[pl.ds(PART, PART), :] = out[:, PANEL:]


def finish(parts):
    chosen = (np.arange(PART)[:, None] == np.arange(LANES)[None, :] % PART).astype(np.float32)
    return pl.pallas_call(
        finish_kernel,
        out_shape=jax.ShapeDtypeStruct((PANEL, PANEL), jnp.float32),
        in_specs=[VMEM, VMEM],
        out_specs=VMEM,
        compiler_params=pltpu.CompilerParams(vmem_limit_bytes=4 * 2**20),
        cost_estimate=pl.CostEstimate(flops=10**6, bytes_accessed=2**19, transcendentals=0),
        name="finish",
    )(parts, jnp.asarray(chosen))


def prepare_kernel(
    side_ref, panel_hbm, sign_hbm, rows_hbm, owner_hbm, send_ref, own_ref, slots_hbm, panel, sign, rows, owner, slots_vmem, sems
):
    side = side_ref[0]
    half = lambda at: panel_hbm.at[pl.ds(pl.multiple_of(at * PART, PART), PART), :]
    copies = [
        pltpu.make_async_copy(source, target, sems.at[i])
        for i, (source, target) in enumerate(
            (
                (sign_hbm, sign),
                (half(1 - side), panel.at[0]),
                (half(side), panel.at[1]),
                (rows_hbm, rows),
                (owner_hbm, owner),
            )
        )
    ]
    for copy in copies[3:] + copies[:3]:
        copy.start()
    copies[3].wait()
    copies[4].wait()
    lane = lax.broadcasted_iota(jnp.int32, (8, LANES), 1)
    parts = [jnp.zeros((8, LANES), jnp.int32)] * 8
    for i in range(CAP):
        parts[i % 8] = jnp.where(lane == i, rows[i], parts[i % 8])
        parts[i % 8] = jnp.where(lane == CAP + i, owner[i], parts[i % 8])
    slots = parts[0]
    for part in parts[1:]:
        slots = slots + part
    for i in range(8):
        slots_vmem[pl.ds(i * 8, 8), :] = slots
    slots_copy = pltpu.make_async_copy(slots_vmem, slots_hbm, sems.at[5])
    slots_copy.start()
    copies[0].wait()
    for at, out_ref in enumerate((send_ref, own_ref)):
        copies[1 + at].wait()
        for block in range(ROWS_DEV // LANES):
            lanes = pl.ds(block * LANES, LANES)
            factor = (1 - 2 * sign[pl.ds(block, 1), :]).astype(jnp.float32)
            out_ref[:, lanes] = panel[at, :, lanes] * factor
    slots_copy.wait()


def prepare(side, hidden_panel, sign_bits, pick_rows, pick_owner):
    half = jax.ShapeDtypeStruct((PART, ROWS_DEV), jnp.float32)
    return pl.pallas_call(
        prepare_kernel,
        out_shape=(half, half, pltpu.HBM((64, LANES), jnp.int32)),
        in_specs=[SMEM, HBM, HBM, HBM, HBM],
        out_specs=(VMEM, VMEM, HBM),
        scratch_shapes=[
            pltpu.VMEM((2, PART, ROWS_DEV), jnp.float32),
            pltpu.VMEM((ROWS_DEV // LANES, LANES), jnp.int32),
            pltpu.SMEM((CAP,), jnp.int32),
            pltpu.SMEM((CAP,), jnp.int32),
            pltpu.VMEM((64, LANES), jnp.int32),
            pltpu.SemaphoreType.DMA((6,)),
        ],
        compiler_params=pltpu.CompilerParams(vmem_limit_bytes=8 * 2**20),
        cost_estimate=pl.CostEstimate(flops=10**6, bytes_accessed=2**21, transcendentals=0),
        name="prepare",
    )(
        side,
        pltpu.with_memory_space_constraint(hidden_panel, pltpu.HBM),
        pltpu.with_memory_space_constraint(sign_bits.reshape(ROWS_DEV // LANES, LANES), pltpu.HBM),
        pltpu.with_memory_space_constraint(pick_rows, pltpu.HBM),
        pltpu.with_memory_space_constraint(pick_owner, pltpu.HBM),
    )


def local(hidden_panel, sign_bits, pick_rows, pick_owner):
    me = ((lax.axis_index("gx") * 8 + lax.axis_index("gy")) * 4 + lax.axis_index("x")) * 2 + lax.axis_index("core")
    side = (lax.axis_index("x") % 2).reshape(1).astype(jnp.int32)
    send, own, slots = prepare(side, hidden_panel, sign_bits, pick_rows, pick_owner)
    near = lax.ppermute(send, "x", [(i, i ^ 1) for i in range(4)])
    first_slots = lax.all_to_all(
        slots.reshape(64, 1, LANES), ("gx", "gy"), split_axis=0, concat_axis=0, tiled=True
    )
    sources = invert((me % 8).reshape(1).astype(jnp.int32), first_slots.reshape(64, LANES))
    own = join(own, near, sources)
    sources = lax.all_to_all(sources, ("x", "core"), split_axis=0, concat_axis=0, tiled=True)
    table = make_table(own, lax.ppermute(own, "core", [(0, 1), (1, 0)]))
    columns = pick_columns(me.reshape(1).astype(jnp.int32), sources, table)
    columns = lax.all_to_all(
        columns.reshape(CHIPS, 4, LANES), ("gx", "gy", "x"), split_axis=0, concat_axis=0, tiled=True
    )
    return finish(columns.reshape(OUT_ROWS, LANES))


def solution(mesh):
    inner = Mesh(mesh.devices.reshape(8, 8, 4, 2), ("gx", "gy", "x", "core"))
    rows = ("gx", "gy", "x", "core")
    return jax.shard_map(
        local,
        mesh=inner,
        in_specs=(P(None, rows), P(rows), P(rows), P(rows)),
        out_specs=P(None, rows),
        check_vma=False,
    )
```

```python
import jax
import jax.numpy as jnp
import numpy as np
from jax import lax
from jax.experimental import pallas as pl
from jax.experimental.pallas import tpu as pltpu
from jax.sharding import Mesh, PartitionSpec as P

PANEL = 32
ROWS_DEV = 8192
CAP = 64
DEVS = 512
PART = PANEL // 2
SOURCES = 4
BASE = 256
FOLDS = ROWS_DEV // BASE
PAD = 8
HALF = ROWS_DEV // 2
TABLE = HALF + 2 * PAD
LANES = 128
CHIPS = 256
OUT_ROWS = 4 * CHIPS
GROUPED = 8
PIECES = FOLDS // 4
SCALE = 2.0**-11
NT = (((1,), (1,)), ((), ()))
VMEM, SMEM, HBM = (pl.BlockSpec(memory_space=m) for m in (pltpu.VMEM, pltpu.SMEM, pltpu.HBM))


def hadamard_np(order):
    matrix = np.ones((1, 1), np.float32)
    while matrix.shape[0] < order:
        matrix = np.block([[matrix, matrix], [matrix, -matrix]])
    return matrix


def butterflies(parts):
    half = 1
    while half < len(parts):
        for start in range(0, len(parts), 2 * half):
            for i in range(start, start + half):
                low, high = parts[i], parts[i + half]
                parts[i], parts[i + half] = low + high, low - high
        half *= 2
    return parts


def join_kernel(own_ref, near_ref, sources_ref, out_ref):
    out_ref[0] = own_ref[...]
    out_ref[1] = near_ref[...]


def join(own, near, sources):
    return pl.pallas_call(
        join_kernel,
        out_shape=jax.ShapeDtypeStruct((2, PART, ROWS_DEV), jnp.float32),
        in_specs=[VMEM, VMEM, HBM],
        out_specs=VMEM,
        compiler_params=pltpu.CompilerParams(vmem_limit_bytes=8 * 2**20),
        cost_estimate=pl.CostEstimate(flops=0, bytes_accessed=2**21, transcendentals=0),
        name="join_halves",
    )(own, near, sources)


def table_kernel(own_ref, other_hbm, had_hbm, table, mixed, other_ref, had_ref, sems):
    other_copy = pltpu.make_async_copy(other_hbm, other_ref, sems.at[0])
    other_copy.start()
    had_copy = pltpu.make_async_copy(had_hbm, had_ref, sems.at[1])
    had_copy.start()
    for source, (ref, chip) in enumerate((ref, chip) for ref in (own_ref, other_ref) for chip in range(2)):
        if source == 2:
            other_copy.wait()

        def fold_rows(step, _, ref=ref, chip=chip, source=source):
            group, half = step // 2, step % 2
            rows = pl.ds(pl.multiple_of(group * 8, 8), 8)
            column = half * LANES
            parts = [ref[chip, rows, pl.ds(pl.multiple_of(fold * BASE + column, LANES), LANES)] for fold in range(FOLDS)]
            out_rows = pl.ds(pl.multiple_of(source * PART + group * 8, 8), 8)
            for fold, part in enumerate(butterflies(parts)):
                mixed[fold, out_rows, pl.ds(pl.multiple_of(column, LANES), LANES)] = part
            return 0

        lax.fori_loop(0, PART // 8 * 2, fold_rows, 0)

    had_copy.wait()
    edge = jnp.zeros((PAD, LANES), jnp.float32)
    table[pl.ds(0, PAD), :] = edge
    table[pl.ds(TABLE - PAD, PAD), :] = edge

    def transform(piece):
        highs, middles, lows = [], [], []
        for fold in (2 * piece, 2 * piece + FOLDS // 2, 2 * piece + 1, 2 * piece + 1 + FOLDS // 2):
            block = jnp.concatenate(
                butterflies([mixed[fold, pl.ds(source * PART, PART), :] for source in range(SOURCES)]), axis=0
            )
            highs.append(block.astype(jnp.bfloat16))
            rest = block - highs[-1].astype(jnp.float32)
            middles.append(rest.astype(jnp.bfloat16))
            lows.append((rest - middles[-1].astype(jnp.float32)).astype(jnp.bfloat16))
        out = jnp.zeros((BASE, 2 * LANES), jnp.float32)
        for pieces in (lows, middles, highs):
            out += lax.dot_general(
                had_ref[...], jnp.concatenate(pieces, axis=0), NT, preferred_element_type=jnp.float32
            )
        for i in range(2):
            table[pl.ds((2 * piece + i) * BASE + PAD, BASE), :] = out[:, i * LANES : (i + 1) * LANES]

    for piece in range(PIECES):
        transform(piece)


def make_table(own, other):
    had = jnp.asarray(hadamard_np(BASE), jnp.bfloat16)
    return pl.pallas_call(
        table_kernel,
        out_shape=jax.ShapeDtypeStruct((TABLE, LANES), jnp.float32),
        in_specs=[VMEM, HBM, HBM],
        out_specs=VMEM,
        scratch_shapes=[
            pltpu.VMEM((FOLDS, SOURCES * PART, BASE), jnp.float32),
            pltpu.VMEM((2, PART, ROWS_DEV), jnp.float32),
            pltpu.VMEM((BASE, BASE), jnp.bfloat16),
            pltpu.SemaphoreType.DMA((2,)),
        ],
        compiler_params=pltpu.CompilerParams(vmem_limit_bytes=24 * 2**20),
        cost_estimate=pl.CostEstimate(flops=10**9, bytes_accessed=10 * 2**20, transcendentals=0),
        name="local_transform",
    )(own, *(pltpu.with_memory_space_constraint(v, pltpu.HBM) for v in (other, had)))


def invert_kernel(group_ref, slots_ref, out_ref):
    lane = lax.broadcasted_iota(jnp.int32, (32, LANES), 1)
    even, odd = slots_ref[pl.ds(0, 32, stride=2), :], slots_ref[pl.ds(1, 32, stride=2), :]
    first = lane < CAP
    picks = jnp.where(first, even, pltpu.roll(odd, CAP, 1))
    owner = jnp.where(first, pltpu.roll(even, CAP, 1), odd)
    place = 2 * lax.broadcasted_iota(jnp.int32, (32, LANES), 0) + jnp.where(first, 0, 1)
    bf16 = lambda v: v.astype(jnp.float32).astype(jnp.bfloat16)
    high = bf16(jnp.where(owner >= 0, ((owner >> 5) & 1) * 128 + (owner >> 7), -1))
    low = bf16((owner & 7) * 8 + ((owner >> 6) & 1) * 4 + ((owner >> 3) & 3))
    values = bf16(picks & (BASE - 1)), bf16(picks >> 8), bf16(place + 1)
    high_at = bf16(lax.broadcasted_iota(jnp.int32, (256, LANES), 0))
    low_at = bf16(lax.broadcasted_iota(jnp.int32, (64, LANES), 0))
    one, zero = jnp.ones((), jnp.bfloat16), jnp.zeros((), jnp.bfloat16)
    total = jnp.zeros((192, 256), jnp.float32)
    for start in range(0, 32, 16):
        lhs, rhs = [], []
        for i in range(start, start + 16):
            at = lambda v: v[i : i + 1, :]
            rhs.append(jnp.where(at(high) == high_at, one, zero))
            hit = at(low) == low_at
            lhs.append(jnp.concatenate([jnp.where(hit, at(v), zero) for v in values], axis=0))
        total += lax.dot_general(
            jnp.concatenate(lhs, axis=1), jnp.concatenate(rhs, axis=1), NT, preferred_element_type=jnp.float32
        )
    base, fold, place = (total[i * 64 : (i + 1) * 64].astype(jnp.int32) for i in range(3))
    row = ((place - 1) * 8 + group_ref[0]) * ROWS_DEV + fold * BASE + base
    found = jnp.where(place > 0, row + 1, 0)
    for i in range(8):
        out_ref[i] = found[:, i % 2 * LANES : (i % 2 + 1) * LANES]


def invert(group, slots):
    return pl.pallas_call(
        invert_kernel,
        out_shape=jax.ShapeDtypeStruct((8, 64, LANES), jnp.int32),
        in_specs=[SMEM, VMEM],
        out_specs=VMEM,
        compiler_params=pltpu.CompilerParams(vmem_limit_bytes=8 * 2**20),
        cost_estimate=pl.CostEstimate(flops=4 * 10**8, bytes_accessed=2**19, transcendentals=0),
        name="invert_slots",
    )(group, slots)


def pick_kernel(
    me_ref, sources_ref, spread_ref, table, out_ref, where_vmem, signed, wide, where_smem, sems
):
    bf16 = lambda v: v.astype(jnp.float32).astype(jnp.bfloat16)
    source = sources_ref[0]
    for i in range(1, 8):
        source += sources_ref[i]
    source = source - 1
    device = source >> 13
    odd_bits = device & me_ref[0]
    for shift in (8, 4, 2, 1):
        odd_bits = odd_bits ^ (odd_bits >> shift)
    combo = ((source >> 12) & 1) * 4 + (device & 1) * 2 + ((device >> 1) & 1) + 1
    sub = lax.broadcasted_iota(jnp.int32, (64, 128), 0) % 8
    where = ((source & (HALF - 1)) + PAD - sub).T
    where_vmem[...] = jnp.concatenate([where[:64], where[64:]], axis=1)
    where_copies = []
    for i, rows in enumerate((pl.ds(0, 8), pl.ds(8, 56))):
        where_copies.append(pltpu.make_async_copy(where_vmem.at[rows, :], where_smem.at[rows, :], sems.at[i]))
        where_copies[-1].start()
    combo = bf16(jnp.where(odd_bits & 1 == 1, -combo, combo).T)
    for i in range(8):
        signed[pl.ds(i, 128, stride=8), :] = jnp.dot(
            combo, spread_ref[:, i * LANES : (i + 1) * LANES], preferred_element_type=jnp.float32
        )
    lane = lax.broadcasted_iota(jnp.int32, (8, LANES), 1)
    sub = lax.broadcasted_iota(jnp.int32, (8, LANES), 0)
    row_of = lane // PART
    lane_of = lane % PART - PART
    turn = lambda v, index: jnp.take_along_axis(v, index, axis=1, mode="promise_in_bounds")

    first_of = lambda group: (group & 1) * 64 + (group >> 1) * GROUPED

    def gather(group, place):
        block = first_of(group) + place
        rows = pl.ds(pl.multiple_of(block * 8, 8), 8)
        for g in range(8):
            at = lambda i: where_smem.at[pl.ds(place, 57), pl.ds(8 * g + i, 65)][(group >> 1) * GROUPED, (group & 1) * 64]
            value = table[pl.ds(at(0), 8), :]
            for i in range(1, 8):
                value = jnp.where(sub == i, table[pl.ds(at(i), 8), :], value)
            wide[rows, pl.ds(g * LANES, LANES)] = value

    def choose(block):
        rows = pl.ds(pl.multiple_of(block * 8, 8), 8)
        combo = signed[rows, :]
        index = lane_of + PART * jnp.abs(combo).astype(jnp.int32)
        out = turn(wide[rows, pl.ds(0, LANES)], index)
        for g in range(1, 8):
            out = jnp.where(row_of == g, turn(wide[rows, pl.ds(g * LANES, LANES)], index), out)
        out_ref[rows, :] = out * jnp.where(combo < 0, -SCALE, SCALE)

    def both(group, _):
        for i in range(GROUPED):
            choose(first_of(group - 1) + i)
        for i in range(GROUPED):
            gather(group, i)
        return 0

    groups = OUT_ROWS // 8 // GROUPED
    where_copies[0].wait()
    for i in range(GROUPED):
        gather(0, i)
    lax.fori_loop(1, 2, both, 0)
    where_copies[1].wait()
    lax.fori_loop(2, groups, both, 0)
    for i in range(GROUPED):
        choose(first_of(groups - 1) + i)


def spread_np():
    column = np.arange(8 * LANES)
    return (np.arange(64)[:, None] == (column % LANES // PART * 8 + column // LANES)[None, :]).astype(np.float32)


def pick_columns(me, sources, table):
    return pl.pallas_call(
        pick_kernel,
        out_shape=jax.ShapeDtypeStruct((OUT_ROWS, LANES), jnp.float32),
        in_specs=[SMEM, VMEM, VMEM, VMEM],
        out_specs=VMEM,
        scratch_shapes=[
            pltpu.VMEM((64, 128), jnp.int32),
            pltpu.VMEM((OUT_ROWS, LANES), jnp.float32),
            pltpu.VMEM((OUT_ROWS, 8 * LANES), jnp.float32),
            pltpu.SMEM((64, 128), jnp.int32),
            pltpu.SemaphoreType.DMA((2,)),
        ],
        compiler_params=pltpu.CompilerParams(vmem_limit_bytes=24 * 2**20),
        cost_estimate=pl.CostEstimate(flops=10**8, bytes_accessed=10 * 2**20, transcendentals=0),
        name="pick_columns",
    )(
        me,
        sources,
        jnp.asarray(spread_np(), jnp.bfloat16),
        table,
    )


def finish_kernel(parts_ref, chosen_ref, out_ref):
    totals = [parts_ref[pl.ds(i * 8, 8), :] for i in range(8)]
    for block in range(8, OUT_ROWS // 8):
        totals[block % 8] += parts_ref[pl.ds(block * 8, 8), :]
    while len(totals) > 1:
        totals = [low + high for low, high in zip(totals[::2], totals[1::2])]
    total = totals[0]
    group = lax.broadcasted_iota(jnp.int32, (8, LANES), 1) // PART == lax.broadcasted_iota(jnp.int32, (8, LANES), 0)
    spread = [jnp.where(group, jnp.broadcast_to(total[i : i + 1], (8, LANES)), 0.0) for i in range(8)]
    out = lax.dot_general(
        chosen_ref[...],
        jnp.concatenate(spread, axis=0),
        NT,
        precision=lax.Precision.HIGHEST,
        preferred_element_type=jnp.float32,
    )
    out_ref[pl.ds(0, PART), :] = out[:, :PANEL]
    out_ref[pl.ds(PART, PART), :] = out[:, PANEL:]


def finish(parts):
    chosen = (np.arange(PART)[:, None] == np.arange(LANES)[None, :] % PART).astype(np.float32)
    return pl.pallas_call(
        finish_kernel,
        out_shape=jax.ShapeDtypeStruct((PANEL, PANEL), jnp.float32),
        in_specs=[VMEM, VMEM],
        out_specs=VMEM,
        compiler_params=pltpu.CompilerParams(vmem_limit_bytes=4 * 2**20),
        cost_estimate=pl.CostEstimate(flops=10**6, bytes_accessed=2**19, transcendentals=0),
        name="finish",
    )(parts, jnp.asarray(chosen))


def prepare_kernel(
    side_ref, panel_hbm, sign_hbm, rows_hbm, owner_hbm, send_ref, own_ref, slots_hbm, panel, sign, rows, owner, slots_vmem, sems
):
    side = side_ref[0]
    half = lambda at: panel_hbm.at[pl.ds(pl.multiple_of(at * PART, PART), PART), :]
    copies = [
        pltpu.make_async_copy(source, target, sems.at[i])
        for i, (source, target) in enumerate(
            (
                (sign_hbm, sign),
                (half(1 - side), panel.at[0]),
                (half(side), panel.at[1]),
                (rows_hbm, rows),
                (owner_hbm, owner),
            )
        )
    ]
    for copy in copies[3:] + copies[:3]:
        copy.start()
    copies[3].wait()
    copies[4].wait()
    lane = lax.broadcasted_iota(jnp.int32, (8, LANES), 1)
    parts = [jnp.zeros((8, LANES), jnp.int32)] * 8
    for i in range(CAP):
        parts[i % 8] = jnp.where(lane == i, rows[i], parts[i % 8])
        parts[i % 8] = jnp.where(lane == CAP + i, owner[i], parts[i % 8])
    slots = parts[0]
    for part in parts[1:]:
        slots = slots + part
    for i in range(8):
        slots_vmem[pl.ds(i * 8, 8), :] = slots
    slots_copy = pltpu.make_async_copy(slots_vmem, slots_hbm, sems.at[5])
    slots_copy.start()
    copies[0].wait()
    for at, out_ref in enumerate((send_ref, own_ref)):
        copies[1 + at].wait()
        for block in range(ROWS_DEV // LANES):
            lanes = pl.ds(block * LANES, LANES)
            factor = (1 - 2 * sign[pl.ds(block, 1), :]).astype(jnp.float32)
            out_ref[:, lanes] = panel[at, :, lanes] * factor
    slots_copy.wait()


def prepare(side, hidden_panel, sign_bits, pick_rows, pick_owner):
    half = jax.ShapeDtypeStruct((PART, ROWS_DEV), jnp.float32)
    return pl.pallas_call(
        prepare_kernel,
        out_shape=(half, half, pltpu.HBM((64, LANES), jnp.int32)),
        in_specs=[SMEM, HBM, HBM, HBM, HBM],
        out_specs=(VMEM, VMEM, HBM),
        scratch_shapes=[
            pltpu.VMEM((2, PART, ROWS_DEV), jnp.float32),
            pltpu.VMEM((ROWS_DEV // LANES, LANES), jnp.int32),
            pltpu.SMEM((CAP,), jnp.int32),
            pltpu.SMEM((CAP,), jnp.int32),
            pltpu.VMEM((64, LANES), jnp.int32),
            pltpu.SemaphoreType.DMA((6,)),
        ],
        compiler_params=pltpu.CompilerParams(vmem_limit_bytes=8 * 2**20),
        cost_estimate=pl.CostEstimate(flops=10**6, bytes_accessed=2**21, transcendentals=0),
        name="prepare",
    )(
        side,
        pltpu.with_memory_space_constraint(hidden_panel, pltpu.HBM),
        pltpu.with_memory_space_constraint(sign_bits.reshape(ROWS_DEV // LANES, LANES), pltpu.HBM),
        pltpu.with_memory_space_constraint(pick_rows, pltpu.HBM),
        pltpu.with_memory_space_constraint(pick_owner, pltpu.HBM),
    )


def local(hidden_panel, sign_bits, pick_rows, pick_owner):
    me = ((lax.axis_index("gx") * 8 + lax.axis_index("gy")) * 4 + lax.axis_index("x")) * 2 + lax.axis_index("core")
    side = (lax.axis_index("x") % 2).reshape(1).astype(jnp.int32)
    send, own, slots = prepare(side, hidden_panel, sign_bits, pick_rows, pick_owner)
    near = lax.ppermute(send, "x", [(i, i ^ 1) for i in range(4)])
    first_slots = lax.all_to_all(
        slots.reshape(64, 1, LANES), ("gx", "gy"), split_axis=0, concat_axis=0, tiled=True
    )
    sources = invert((me % 8).reshape(1).astype(jnp.int32), first_slots.reshape(64, LANES))
    own = join(own, near, sources)
    sources = lax.all_to_all(sources, ("x", "core"), split_axis=0, concat_axis=0, tiled=True)
    table = make_table(own, lax.ppermute(own, "core", [(0, 1), (1, 0)]))
    columns = pick_columns(me.reshape(1).astype(jnp.int32), sources, table)
    columns = lax.all_to_all(
        columns.reshape(CHIPS, 4, LANES), ("gx", "gy", "x"), split_axis=0, concat_axis=0, tiled=True
    )
    return finish(columns.reshape(OUT_ROWS, LANES))


def solution(mesh):
    inner = Mesh(mesh.devices.reshape(8, 8, 4, 2), ("gx", "gy", "x", "core"))
    rows = ("gx", "gy", "x", "core")
    return jax.shard_map(
        local,
        mesh=inner,
        in_specs=(P(None, rows), P(rows), P(rows), P(rows)),
        out_specs=P(None, rows),
        check_vma=False,
    )
```

```python
import jax
import jax.numpy as jnp
import numpy as np
from jax import lax
from jax.experimental import pallas as pl
from jax.experimental.pallas import tpu as pltpu
from jax.sharding import Mesh, PartitionSpec as P

PANEL = 32
ROWS_DEV = 8192
CAP = 64
DEVS = 512
PART = PANEL // 2
SOURCES = 4
BASE = 256
FOLDS = ROWS_DEV // BASE
PAD = 8
HALF = ROWS_DEV // 2
TABLE = HALF + 2 * PAD
LANES = 128
CHIPS = 256
OUT_ROWS = 4 * CHIPS
GROUPED = 8
PIECES = FOLDS // 4
SCALE = 2.0**-11
NT = (((1,), (1,)), ((), ()))
VMEM, SMEM, HBM = (pl.BlockSpec(memory_space=m) for m in (pltpu.VMEM, pltpu.SMEM, pltpu.HBM))


def hadamard_np(order):
    matrix = np.ones((1, 1), np.float32)
    while matrix.shape[0] < order:
        matrix = np.block([[matrix, matrix], [matrix, -matrix]])
    return matrix


def butterflies(parts):
    half = 1
    while half < len(parts):
        for start in range(0, len(parts), 2 * half):
            for i in range(start, start + half):
                low, high = parts[i], parts[i + half]
                parts[i], parts[i + half] = low + high, low - high
        half *= 2
    return parts


def join_kernel(own_ref, near_ref, sources_ref, out_ref):
    out_ref[0] = own_ref[...]
    out_ref[1] = near_ref[...]


def join(own, near, sources):
    return pl.pallas_call(
        join_kernel,
        out_shape=jax.ShapeDtypeStruct((2, PART, ROWS_DEV), jnp.float32),
        in_specs=[VMEM, VMEM, HBM],
        out_specs=VMEM,
        compiler_params=pltpu.CompilerParams(vmem_limit_bytes=8 * 2**20),
        cost_estimate=pl.CostEstimate(flops=0, bytes_accessed=2**21, transcendentals=0),
        name="join_halves",
    )(own, near, sources)


def table_kernel(own_ref, other_hbm, had_hbm, table, mixed, other_ref, had_ref, sems):
    other_copy = pltpu.make_async_copy(other_hbm, other_ref, sems.at[0])
    other_copy.start()
    had_copy = pltpu.make_async_copy(had_hbm, had_ref, sems.at[1])
    had_copy.start()
    for source, (ref, chip) in enumerate((ref, chip) for ref in (own_ref, other_ref) for chip in range(2)):
        if source == 2:
            other_copy.wait()

        def fold_rows(step, _, ref=ref, chip=chip, source=source):
            group, half = step // 2, step % 2
            rows = pl.ds(pl.multiple_of(group * 8, 8), 8)
            column = half * LANES
            parts = [ref[chip, rows, pl.ds(pl.multiple_of(fold * BASE + column, LANES), LANES)] for fold in range(FOLDS)]
            out_rows = pl.ds(pl.multiple_of(source * PART + group * 8, 8), 8)
            for fold, part in enumerate(butterflies(parts)):
                mixed[fold, out_rows, pl.ds(pl.multiple_of(column, LANES), LANES)] = part
            return 0

        lax.fori_loop(0, PART // 8 * 2, fold_rows, 0)

    had_copy.wait()
    edge = jnp.zeros((PAD, LANES), jnp.float32)
    table[pl.ds(0, PAD), :] = edge
    table[pl.ds(TABLE - PAD, PAD), :] = edge

    def transform(piece):
        highs, middles, lows = [], [], []
        for fold in (2 * piece, 2 * piece + FOLDS // 2, 2 * piece + 1, 2 * piece + 1 + FOLDS // 2):
            block = jnp.concatenate(
                butterflies([mixed[fold, pl.ds(source * PART, PART), :] for source in range(SOURCES)]), axis=0
            )
            highs.append(block.astype(jnp.bfloat16))
            rest = block - highs[-1].astype(jnp.float32)
            middles.append(rest.astype(jnp.bfloat16))
            lows.append((rest - middles[-1].astype(jnp.float32)).astype(jnp.bfloat16))
        out = jnp.zeros((BASE, 2 * LANES), jnp.float32)
        for pieces in (lows, middles, highs):
            out += lax.dot_general(
                had_ref[...], jnp.concatenate(pieces, axis=0), NT, preferred_element_type=jnp.float32
            )
        for i in range(2):
            table[pl.ds((2 * piece + i) * BASE + PAD, BASE), :] = out[:, i * LANES : (i + 1) * LANES]

    for piece in range(PIECES):
        transform(piece)


def make_table(own, other):
    had = jnp.asarray(hadamard_np(BASE), jnp.bfloat16)
    return pl.pallas_call(
        table_kernel,
        out_shape=jax.ShapeDtypeStruct((TABLE, LANES), jnp.float32),
        in_specs=[VMEM, HBM, HBM],
        out_specs=VMEM,
        scratch_shapes=[
            pltpu.VMEM((FOLDS, SOURCES * PART, BASE), jnp.float32),
            pltpu.VMEM((2, PART, ROWS_DEV), jnp.float32),
            pltpu.VMEM((BASE, BASE), jnp.bfloat16),
            pltpu.SemaphoreType.DMA((2,)),
        ],
        compiler_params=pltpu.CompilerParams(vmem_limit_bytes=24 * 2**20),
        cost_estimate=pl.CostEstimate(flops=10**9, bytes_accessed=10 * 2**20, transcendentals=0),
        name="local_transform",
    )(own, *(pltpu.with_memory_space_constraint(v, pltpu.HBM) for v in (other, had)))


def invert_kernel(group_ref, slots_ref, out_ref):
    lane = lax.broadcasted_iota(jnp.int32, (32, LANES), 1)
    even, odd = slots_ref[pl.ds(0, 32, stride=2), :], slots_ref[pl.ds(1, 32, stride=2), :]
    first = lane < CAP
    picks = jnp.where(first, even, pltpu.roll(odd, CAP, 1))
    owner = jnp.where(first, pltpu.roll(even, CAP, 1), odd)
    place = 2 * lax.broadcasted_iota(jnp.int32, (32, LANES), 0) + jnp.where(first, 0, 1)
    bf16 = lambda v: v.astype(jnp.float32).astype(jnp.bfloat16)
    high = bf16(jnp.where(owner >= 0, ((owner >> 5) & 1) * 128 + (owner >> 7), -1))
    low = bf16((owner & 7) * 8 + ((owner >> 6) & 1) * 4 + ((owner >> 3) & 3))
    values = bf16(picks & (BASE - 1)), bf16(picks >> 8), bf16(place + 1)
    high_at = bf16(lax.broadcasted_iota(jnp.int32, (256, LANES), 0))
    low_at = bf16(lax.broadcasted_iota(jnp.int32, (64, LANES), 0))
    one, zero = jnp.ones((), jnp.bfloat16), jnp.zeros((), jnp.bfloat16)
    total = jnp.zeros((192, 256), jnp.float32)
    for start in range(0, 32, 16):
        lhs, rhs = [], []
        for i in range(start, start + 16):
            at = lambda v: v[i : i + 1, :]
            rhs.append(jnp.where(at(high) == high_at, one, zero))
            hit = at(low) == low_at
            lhs.append(jnp.concatenate([jnp.where(hit, at(v), zero) for v in values], axis=0))
        total += lax.dot_general(
            jnp.concatenate(lhs, axis=1), jnp.concatenate(rhs, axis=1), NT, preferred_element_type=jnp.float32
        )
    base, fold, place = (total[i * 64 : (i + 1) * 64].astype(jnp.int32) for i in range(3))
    row = ((place - 1) * 8 + group_ref[0]) * ROWS_DEV + fold * BASE + base
    found = jnp.where(place > 0, row + 1, 0)
    for i in range(8):
        out_ref[i] = found[:, i % 2 * LANES : (i % 2 + 1) * LANES]


def invert(group, slots):
    return pl.pallas_call(
        invert_kernel,
        out_shape=jax.ShapeDtypeStruct((8, 64, LANES), jnp.int32),
        in_specs=[SMEM, VMEM],
        out_specs=VMEM,
        compiler_params=pltpu.CompilerParams(vmem_limit_bytes=8 * 2**20),
        cost_estimate=pl.CostEstimate(flops=4 * 10**8, bytes_accessed=2**19, transcendentals=0),
        name="invert_slots",
    )(group, slots)


def pick_kernel(
    me_ref, sources_ref, spread_ref, table, out_ref, where_vmem, signed, wide, where_smem, sems
):
    bf16 = lambda v: v.astype(jnp.float32).astype(jnp.bfloat16)
    source = sources_ref[0]
    for i in range(1, 8):
        source += sources_ref[i]
    source = source - 1
    device = source >> 13
    odd_bits = device & me_ref[0]
    for shift in (8, 4, 2, 1):
        odd_bits = odd_bits ^ (odd_bits >> shift)
    combo = ((source >> 12) & 1) * 4 + (device & 1) * 2 + ((device >> 1) & 1) + 1
    sub = lax.broadcasted_iota(jnp.int32, (64, 128), 0) % 8
    where = ((source & (HALF - 1)) + PAD - sub).T
    where_vmem[...] = jnp.concatenate([where[:64], where[64:]], axis=1)
    where_copies = []
    for i, rows in enumerate((pl.ds(0, 8), pl.ds(8, 16), pl.ds(24, 40))):
        where_copies.append(pltpu.make_async_copy(where_vmem.at[rows, :], where_smem.at[rows, :], sems.at[i]))
        where_copies[-1].start()
    combo = bf16(jnp.where(odd_bits & 1 == 1, -combo, combo).T)
    for i in range(8):
        signed[pl.ds(i, 128, stride=8), :] = jnp.dot(
            combo, spread_ref[:, i * LANES : (i + 1) * LANES], preferred_element_type=jnp.float32
        )
    lane = lax.broadcasted_iota(jnp.int32, (8, LANES), 1)
    sub = lax.broadcasted_iota(jnp.int32, (8, LANES), 0)
    row_of = lane // PART
    lane_of = lane % PART - PART
    turn = lambda v, index: jnp.take_along_axis(v, index, axis=1, mode="promise_in_bounds")

    first_of = lambda group: (group & 1) * 64 + (group >> 1) * GROUPED

    def gather(group, place):
        block = first_of(group) + place
        rows = pl.ds(pl.multiple_of(block * 8, 8), 8)
        for g in range(8):
            at = lambda i: where_smem.at[pl.ds(place, 57), pl.ds(8 * g + i, 65)][(group >> 1) * GROUPED, (group & 1) * 64]
            value = table[pl.ds(at(0), 8), :]
            for i in range(1, 8):
                value = jnp.where(sub == i, table[pl.ds(at(i), 8), :], value)
            wide[rows, pl.ds(g * LANES, LANES)] = value

    def choose(block):
        rows = pl.ds(pl.multiple_of(block * 8, 8), 8)
        combo = signed[rows, :]
        index = lane_of + PART * jnp.abs(combo).astype(jnp.int32)
        out = turn(wide[rows, pl.ds(0, LANES)], index)
        for g in range(1, 8):
            out = jnp.where(row_of == g, turn(wide[rows, pl.ds(g * LANES, LANES)], index), out)
        out_ref[rows, :] = out * jnp.where(combo < 0, -SCALE, SCALE)

    def both(group, _):
        for i in range(GROUPED):
            choose(first_of(group - 1) + i)
        for i in range(GROUPED):
            gather(group, i)
        return 0

    groups = OUT_ROWS // 8 // GROUPED
    where_copies[0].wait()
    for i in range(GROUPED):
        gather(0, i)
    lax.fori_loop(1, 2, both, 0)
    where_copies[1].wait()
    lax.fori_loop(2, 6, both, 0)
    where_copies[2].wait()
    lax.fori_loop(6, groups, both, 0)
    for i in range(GROUPED):
        choose(first_of(groups - 1) + i)


def spread_np():
    column = np.arange(8 * LANES)
    return (np.arange(64)[:, None] == (column % LANES // PART * 8 + column // LANES)[None, :]).astype(np.float32)


def pick_columns(me, sources, table):
    return pl.pallas_call(
        pick_kernel,
        out_shape=jax.ShapeDtypeStruct((OUT_ROWS, LANES), jnp.float32),
        in_specs=[SMEM, VMEM, VMEM, VMEM],
        out_specs=VMEM,
        scratch_shapes=[
            pltpu.VMEM((64, 128), jnp.int32),
            pltpu.VMEM((OUT_ROWS, LANES), jnp.float32),
            pltpu.VMEM((OUT_ROWS, 8 * LANES), jnp.float32),
            pltpu.SMEM((64, 128), jnp.int32),
            pltpu.SemaphoreType.DMA((3,)),
        ],
        compiler_params=pltpu.CompilerParams(vmem_limit_bytes=24 * 2**20),
        cost_estimate=pl.CostEstimate(flops=10**8, bytes_accessed=10 * 2**20, transcendentals=0),
        name="pick_columns",
    )(
        me,
        sources,
        jnp.asarray(spread_np(), jnp.bfloat16),
        table,
    )


def finish_kernel(parts_ref, chosen_ref, out_ref):
    totals = [parts_ref[pl.ds(i * 8, 8), :] for i in range(8)]
    for block in range(8, OUT_ROWS // 8):
        totals[block % 8] += parts_ref[pl.ds(block * 8, 8), :]
    while len(totals) > 1:
        totals = [low + high for low, high in zip(totals[::2], totals[1::2])]
    total = totals[0]
    group = lax.broadcasted_iota(jnp.int32, (8, LANES), 1) // PART == lax.broadcasted_iota(jnp.int32, (8, LANES), 0)
    spread = [jnp.where(group, jnp.broadcast_to(total[i : i + 1], (8, LANES)), 0.0) for i in range(8)]
    out = lax.dot_general(
        chosen_ref[...],
        jnp.concatenate(spread, axis=0),
        NT,
        precision=lax.Precision.HIGHEST,
        preferred_element_type=jnp.float32,
    )
    out_ref[pl.ds(0, PART), :] = out[:, :PANEL]
    out_ref[pl.ds(PART, PART), :] = out[:, PANEL:]


def finish(parts):
    chosen = (np.arange(PART)[:, None] == np.arange(LANES)[None, :] % PART).astype(np.float32)
    return pl.pallas_call(
        finish_kernel,
        out_shape=jax.ShapeDtypeStruct((PANEL, PANEL), jnp.float32),
        in_specs=[VMEM, VMEM],
        out_specs=VMEM,
        compiler_params=pltpu.CompilerParams(vmem_limit_bytes=4 * 2**20),
        cost_estimate=pl.CostEstimate(flops=10**6, bytes_accessed=2**19, transcendentals=0),
        name="finish",
    )(parts, jnp.asarray(chosen))


def prepare_kernel(
    side_ref, panel_hbm, sign_hbm, rows_hbm, owner_hbm, send_ref, own_ref, slots_hbm, panel, sign, rows, owner, slots_vmem, sems
):
    side = side_ref[0]
    half = lambda at: panel_hbm.at[pl.ds(pl.multiple_of(at * PART, PART), PART), :]
    copies = [
        pltpu.make_async_copy(source, target, sems.at[i])
        for i, (source, target) in enumerate(
            (
                (sign_hbm, sign),
                (half(1 - side), panel.at[0]),
                (half(side), panel.at[1]),
                (rows_hbm, rows),
                (owner_hbm, owner),
            )
        )
    ]
    for copy in copies[3:] + copies[:3]:
        copy.start()
    copies[3].wait()
    copies[4].wait()
    lane = lax.broadcasted_iota(jnp.int32, (8, LANES), 1)
    parts = [jnp.zeros((8, LANES), jnp.int32)] * 8
    for i in range(CAP):
        parts[i % 8] = jnp.where(lane == i, rows[i], parts[i % 8])
        parts[i % 8] = jnp.where(lane == CAP + i, owner[i], parts[i % 8])
    slots = parts[0]
    for part in parts[1:]:
        slots = slots + part
    for i in range(8):
        slots_vmem[pl.ds(i * 8, 8), :] = slots
    slots_copy = pltpu.make_async_copy(slots_vmem, slots_hbm, sems.at[5])
    slots_copy.start()
    copies[0].wait()
    for at, out_ref in enumerate((send_ref, own_ref)):
        copies[1 + at].wait()
        for block in range(ROWS_DEV // LANES):
            lanes = pl.ds(block * LANES, LANES)
            factor = (1 - 2 * sign[pl.ds(block, 1), :]).astype(jnp.float32)
            out_ref[:, lanes] = panel[at, :, lanes] * factor
    slots_copy.wait()


def prepare(side, hidden_panel, sign_bits, pick_rows, pick_owner):
    half = jax.ShapeDtypeStruct((PART, ROWS_DEV), jnp.float32)
    return pl.pallas_call(
        prepare_kernel,
        out_shape=(half, half, pltpu.HBM((64, LANES), jnp.int32)),
        in_specs=[SMEM, HBM, HBM, HBM, HBM],
        out_specs=(VMEM, VMEM, HBM),
        scratch_shapes=[
            pltpu.VMEM((2, PART, ROWS_DEV), jnp.float32),
            pltpu.VMEM((ROWS_DEV // LANES, LANES), jnp.int32),
            pltpu.SMEM((CAP,), jnp.int32),
            pltpu.SMEM((CAP,), jnp.int32),
            pltpu.VMEM((64, LANES), jnp.int32),
            pltpu.SemaphoreType.DMA((6,)),
        ],
        compiler_params=pltpu.CompilerParams(vmem_limit_bytes=8 * 2**20),
        cost_estimate=pl.CostEstimate(flops=10**6, bytes_accessed=2**21, transcendentals=0),
        name="prepare",
    )(
        side,
        pltpu.with_memory_space_constraint(hidden_panel, pltpu.HBM),
        pltpu.with_memory_space_constraint(sign_bits.reshape(ROWS_DEV // LANES, LANES), pltpu.HBM),
        pltpu.with_memory_space_constraint(pick_rows, pltpu.HBM),
        pltpu.with_memory_space_constraint(pick_owner, pltpu.HBM),
    )


def local(hidden_panel, sign_bits, pick_rows, pick_owner):
    me = ((lax.axis_index("gx") * 8 + lax.axis_index("gy")) * 4 + lax.axis_index("x")) * 2 + lax.axis_index("core")
    side = (lax.axis_index("x") % 2).reshape(1).astype(jnp.int32)
    send, own, slots = prepare(side, hidden_panel, sign_bits, pick_rows, pick_owner)
    near = lax.ppermute(send, "x", [(i, i ^ 1) for i in range(4)])
    first_slots = lax.all_to_all(
        slots.reshape(64, 1, LANES), ("gx", "gy"), split_axis=0, concat_axis=0, tiled=True
    )
    sources = invert((me % 8).reshape(1).astype(jnp.int32), first_slots.reshape(64, LANES))
    own = join(own, near, sources)
    sources = lax.all_to_all(sources, ("x", "core"), split_axis=0, concat_axis=0, tiled=True)
    table = make_table(own, lax.ppermute(own, "core", [(0, 1), (1, 0)]))
    columns = pick_columns(me.reshape(1).astype(jnp.int32), sources, table)
    columns = lax.all_to_all(
        columns.reshape(CHIPS, 4, LANES), ("gx", "gy", "x"), split_axis=0, concat_axis=0, tiled=True
    )
    return finish(columns.reshape(OUT_ROWS, LANES))


def solution(mesh):
    inner = Mesh(mesh.devices.reshape(8, 8, 4, 2), ("gx", "gy", "x", "core"))
    rows = ("gx", "gy", "x", "core")
    return jax.shard_map(
        local,
        mesh=inner,
        in_specs=(P(None, rows), P(rows), P(rows), P(rows)),
        out_specs=P(None, rows),
        check_vma=False,
    )
```
